128 devices in a mesh: gx: 8 (over y, core), gy: 16 (over z, x).
Axes of the slice: x: 4, y: 4, z: 4, core: 2. Of those that a mesh axis runs over, the one named last changes fastest.
Arguments:
- pressure: float32 [256, 512, 128], P('gx', 'gy'), may hold values from 0.5 to 1.5
- water_sat: float32 [256, 512, 128], P('gx', 'gy'), may hold values from 0.1 to 0.5
- gas_sat: float32 [256, 512, 128], P('gx', 'gy'), may hold values from 0.05 to 0.4
- old_content: float32 [3, 256, 512, 128], P(None, 'gx', 'gy'), may hold values from 0.05 to 0.6
- pore_volume: float32 [256, 512, 128], P('gx', 'gy'), may hold values from 0.2 to 2
- trans_x: float32 [256, 512, 128], P('gx', 'gy'), may hold values from 0.05 to 2
- trans_y: float32 [256, 512, 128], P('gx', 'gy'), may hold values from 0.05 to 2
- trans_z: float32 [256, 512, 128], P('gx', 'gy'), may hold values from 0.05 to 2
- active: int32 [256, 512, 128], P('gx', 'gy'), may hold values 0 or 1
- aggregate: int32 [256, 512, 128], P('gx', 'gy'), may hold values from 0 to 7, as said below
- well_cells: int32 [512, 16], P(('gx', 'gy')), may hold values from -1 to 16777215, as said below
- well_index: float32 [512, 16], P(('gx', 'gy')), may hold values from 0.5 to 5
- bottom_hole: float32 [512], P(('gx', 'gy')), may hold values from 0.3 to 1.8
- well_target: float32 [512], P(('gx', 'gy')), may hold values from -24 to 24
Outputs:
- residual: float32 [3, 256, 512, 128], P(None, 'gx', 'gy')
- pressure_update: float32 [256, 512, 128], P('gx', 'gy')
- well_residual: float32 [512], P(('gx', 'gy'))
The draws below stay inside these ranges and needn't reach their ends.
Inputs may be any that keep to these rules, and one draw needn't show every extreme that they name: `well_cells`: each row lists distinct cells of one well on consecutive layers, one a layer, then -1 in the remaining slots; every well has at least one cell and some well fills all 16 slots. `aggregate`: within every vertical column the value never falls with depth and every value appears.
All inputs are finite; a program needn't handle non-finite values. No bound on the sum of `active` on one device may be relied on, other than what follows from the above.
Results may differ from the reference program's by a relative error of at most 0.0003.
Values sent between devices are 32-bit elements; how exact they have to be, the bound alone decides.
A program may use at most 128 MiB of HBM per device.

```python
import math
import jax
import jax.numpy as jnp
from jax import lax

CX = 32
CY = 32
NZ = 128
PERF = 16
AGG_DEV = 8
CITERS = 24
NX = 256
NY = 512
NWELLS = 512
NAGG = 1024
N_GY = 16


def draw_well_cells(key, part):
    streams = jax.random.split(key, 6)
    head_x = jax.random.randint(streams[0], (NWELLS, 1), 0, NX)
    head_y = jax.random.randint(streams[1], (NWELLS, 1), 0, NY)
    first_layer = jax.random.randint(streams[2], (NWELLS, 1), 0, NZ - PERF + 1)
    step_x = jax.random.randint(streams[3], (NWELLS, 1), -1, 2)
    step_y = jax.random.randint(streams[4], (NWELLS, 1), -1, 2)
    perf_count = jax.random.randint(streams[5], (NWELLS, 1), 1, PERF + 1)
    perf_count = perf_count.at[0, 0].set(PERF)
    position = jnp.arange(PERF, dtype=jnp.int32)[None, :]
    along_x = jnp.clip(head_x + step_x * position, 0, NX - 1)
    along_y = jnp.clip(head_y + step_y * position, 0, NY - 1)
    layer_index = first_layer + position
    flat_index = along_x * (NY * NZ) + along_y * NZ + layer_index
    return jnp.where(position < perf_count, flat_index, -1).astype(jnp.int32)


def draw_aggregate(key, part):
    spacing = NZ // AGG_DEV
    reach_span = spacing // 4
    jitter = jax.random.randint(key, (AGG_DEV - 1, NX, NY, 1), -reach_span, reach_span + 1)
    bounds = (jnp.arange(1, AGG_DEV, dtype=jnp.int32) * spacing)[:, None, None, None] + jitter
    layer_index = jnp.arange(NZ, dtype=jnp.int32)[None, None, None, :]
    return jnp.sum((layer_index >= bounds).astype(jnp.int32), axis=0).astype(jnp.int32)


def place_ends(array, stream_key, smallest, high):
    longest = array.shape.index(max(array.shape))
    spots = []
    for shift in (0, 1):
        where = [jax.random.randint(jax.random.fold_in(stream_key, axis), (), 0, length) for axis, length in enumerate(array.shape)]
        where[longest] = (where[longest] + shift) % array.shape[longest]
        spots.append(tuple(where))
    return array.at[spots[0]].set(smallest).at[spots[1]].set(high)


def steps_of(rng, shape, pieces, smallest, top_value):
    factor_of = 1.0
    for axis_at, shards_of in pieces:
        heights = jax.random.uniform(jax.random.fold_in(jax.random.fold_in(rng, 6), axis_at), (shards_of,), jnp.float32, smallest / len(pieces), top_value / len(pieces))
        factor_of = factor_of * jnp.repeat(jnp.exp(heights), shape[axis_at] // shards_of).reshape((-1,) + (1,) * (len(shape) - 1 - axis_at))
    return factor_of


def scatter_about(own_key, dims, deviation, reach, shards=(), kind=jnp.bfloat16):
    result = deviation * jax.random.normal(own_key, dims, jnp.float32)
    if shards:
        result = result * steps_of(own_key, dims, shards, -0.22, 0.18)
    return jnp.clip(result, -reach, reach).astype(kind)


def setup_inputs(seed: int = 0) -> dict:
    splits = jax.random.split(jax.random.key(seed), 15)
    pressure = jnp.clip(0.5 + 1.0 * jax.random.uniform(splits[0], (NX, NY, NZ), jnp.float32) ** steps_of(splits[0], (NX, NY, NZ), ((0, 8), (1, 16)), -0.2, 0.2), 0.5, 1.5)
    water_sat = jnp.clip(0.1 + 0.4 * jax.random.uniform(splits[1], (NX, NY, NZ), jnp.float32) ** steps_of(splits[1], (NX, NY, NZ), ((0, 8), (1, 16)), -0.2, 0.2), 0.1, 0.5)
    gas_sat = jnp.clip(0.05 + 0.35 * jax.random.uniform(splits[2], (NX, NY, NZ), jnp.float32) ** steps_of(splits[2], (NX, NY, NZ), ((0, 8), (1, 16)), -0.2, 0.2), 0.05, 0.4)
    old_content = jnp.clip(0.05 + 0.55 * jax.random.uniform(splits[3], (3, NX, NY, NZ), jnp.float32) ** steps_of(splits[3], (3, NX, NY, NZ), ((1, 8), (2, 16)), -0.2, 0.2), 0.05, 0.6)
    pore_volume = jnp.clip(jnp.exp(math.log(2.0) - 2.3025851 * jax.random.uniform(splits[4], (NX, NY, NZ), jnp.float32) ** steps_of(splits[4], (NX, NY, NZ), ((0, 8), (1, 16)), -0.2, 0.2)), 0.2, 2.0)
    trans_x = jnp.clip(jnp.exp(math.log(2.0) - 3.6888794 * jax.random.uniform(splits[5], (NX, NY, NZ), jnp.float32) ** steps_of(splits[5], (NX, NY, NZ), ((0, 8), (1, 16)), -0.2, 0.2)), 0.05, 2.0)
    trans_y = jnp.clip(jnp.exp(math.log(2.0) - 3.6888794 * jax.random.uniform(splits[6], (NX, NY, NZ), jnp.float32) ** steps_of(splits[6], (NX, NY, NZ), ((0, 8), (1, 16)), -0.2, 0.2)), 0.05, 2.0)
    trans_z = jnp.clip(jnp.exp(math.log(2.0) - 3.6888794 * jax.random.uniform(splits[7], (NX, NY, NZ), jnp.float32) ** steps_of(splits[7], (NX, NY, NZ), ((0, 8), (1, 16)), -0.2, 0.2)), 0.05, 2.0)
    active = place_ends((jax.random.randint(splits[8], (NX, NY, NZ), 0, 16) < 15).astype(jnp.int32), jax.random.fold_in(splits[8], 1), 0, 1)
    aggregate = draw_aggregate(jax.random.fold_in(splits[14], 71), 0)
    well_cells = draw_well_cells(jax.random.fold_in(splits[14], 71), 0)
    well_index = jnp.clip(jnp.exp(math.log(5.0) - 2.3025851 * jax.random.uniform(splits[11], (NWELLS, PERF), jnp.float32) ** steps_of(splits[11], (NWELLS, PERF), ((0, 128),), -0.2, 0.2)), 0.5, 5.0)
    bottom_hole = jnp.clip(0.3 + 1.5 * jax.random.uniform(splits[12], (NWELLS,), jnp.float32) ** steps_of(splits[12], (NWELLS,), ((0, 128),), -0.2, 0.2), 0.3, 1.8)
    well_target = scatter_about(splits[13], (NWELLS,), 4.0, 24.0, ((0, 128),), jnp.float32)
    return dict(pressure=pressure, water_sat=water_sat, gas_sat=gas_sat, old_content=old_content, pore_volume=pore_volume, trans_x=trans_x, trans_y=trans_y, trans_z=trans_z, active=active, aggregate=aggregate, well_cells=well_cells, well_index=well_index, bottom_hole=bottom_hole, well_target=well_target)


precise = lax.Precision.HIGHEST
compress = (0.001, 0.001, 0.005)
viscosity = (0.5, 1.5, 0.2)
density = (1.0, 0.8, 0.2)
gravity_step = 0.05
relax = 0.6
dead_leak = 0.001


def phase_mobility(pressure, water_sat, gas_sat):
    oil_sat = 1.0 - water_sat - gas_sat
    saturation = (water_sat, oil_sat, gas_sat)
    factors = tuple(1.0 + compress[k] * (pressure - 1.0) for k in range(3))
    mobility = tuple(factors[k] * saturation[k] * saturation[k] / viscosity[k] for k in range(3))
    return saturation, factors, mobility


def mean_flux(face_trans, mob_low, mob_high, potential):
    return face_trans * (0.5 * (mob_low + mob_high)) * potential


def spread(values, direction):
    width_high = [(0, 0), (0, 0), (0, 0)]
    width_low = [(0, 0), (0, 0), (0, 0)]
    width_high[direction] = (0, 1)
    width_low[direction] = (1, 0)
    return jnp.pad(values, width_high), jnp.pad(values, width_low)


def pairs(values):
    return ((values[:-1], values[1:]), (values[:, :-1], values[:, 1:]), (values[:, :, :-1], values[:, :, 1:]))


def apply_operator(values, coefs, diagonal):
    value_pairs = pairs(values)
    sides = []
    for direction in range(3):
        from_high = spread(coefs[direction] * value_pairs[direction][1], direction)[0]
        from_low = spread(coefs[direction] * value_pairs[direction][0], direction)[1]
        sides.append(from_high + from_low)
    return diagonal * values - ((sides[0] + sides[1]) + sides[2])


def coarse_solve(matrix, rhs_all):
    def one_step(step, carry):
        solution, rest, search, norm_now = carry
        image = jnp.dot(matrix, search, precision=precise)
        alpha = norm_now / jnp.sum(search * image)
        solution = solution + alpha * search
        rest = rest - alpha * image
        norm_next = jnp.sum(rest * rest)
        search = rest + (norm_next / norm_now) * search
        return solution, rest, search, norm_next

    start = (jnp.zeros_like(rhs_all), rhs_all, rhs_all, jnp.sum(rhs_all * rhs_all))
    return lax.fori_loop(0, CITERS, one_step, start)[0]


def reference(pressure, water_sat, gas_sat, old_content, pore_volume, trans_x, trans_y, trans_z, active, aggregate, well_cells, well_index, bottom_hole, well_target):
    live_mask = active.astype(jnp.float32)
    saturation, factors, mobility = phase_mobility(pressure, water_sat, gas_sat)
    total_mob = mobility[0] + mobility[1] + mobility[2]
    mask_pairs = pairs(live_mask)
    trans_all = (trans_x, trans_y, trans_z)
    faces = []
    for direction in range(3):
        own_trans = pairs(trans_all[direction])[direction][0]
        faces.append(own_trans * mask_pairs[direction][0] * mask_pairs[direction][1])
    press_pairs = pairs(pressure)
    flat_cells = well_cells.reshape(-1)
    valid_perf = flat_cells >= 0
    safe_index = jnp.where(valid_perf, flat_cells, 0).astype(jnp.int32)
    perf_press = pressure.reshape(-1)[safe_index]
    strength = jnp.where(valid_perf, well_index.reshape(-1) * live_mask.reshape(-1)[safe_index], 0.0)
    hole_press = jnp.broadcast_to(bottom_hole[:, None], well_cells.shape).reshape(-1)
    drawdown = hole_press - perf_press
    phase_rates = [strength * mobility[k].reshape(-1)[safe_index] * drawdown for k in range(3)]
    perf_total = phase_rates[0] + phase_rates[1] + phase_rates[2]
    well_residual = jnp.sum(perf_total.reshape(well_cells.shape), axis=1) - well_target
    cell_count = pressure.size
    residuals = []
    for k in range(3):
        mob_pairs = pairs(mobility[k])
        net_parts = []
        for direction in range(3):
            potential = press_pairs[direction][0] - press_pairs[direction][1]
            if direction == 2:
                potential = potential + density[k] * gravity_step
            phase_flux = mean_flux(faces[direction], mob_pairs[direction][0], mob_pairs[direction][1], potential)
            high_side, low_side = spread(phase_flux, direction)
            net_parts.append(high_side - low_side)
        source = jnp.zeros((cell_count,), jnp.float32).at[safe_index].add(phase_rates[k]).reshape(pressure.shape)
        stored = pore_volume * (factors[k] * saturation[k] - old_content[k])
        residuals.append(live_mask * (stored + ((net_parts[0] + net_parts[1]) + net_parts[2])) - source)
    total_pairs = pairs(total_mob)
    coefs = [faces[d] * (0.5 * (total_pairs[d][0] + total_pairs[d][1])) for d in range(3)]
    well_diag = jnp.zeros((cell_count,), jnp.float32).at[safe_index].add(strength * total_mob.reshape(-1)[safe_index]).reshape(pressure.shape)
    storage = pore_volume * (compress[0] * saturation[0] + compress[1] * saturation[1] + compress[2] * saturation[2])
    leak = live_mask * (storage + well_diag) + dead_leak * (1.0 - live_mask)
    sides = []
    for d in range(3):
        high_side, low_side = spread(coefs[d], d)
        sides.append(high_side + low_side)
    diagonal = (sides[0] + sides[1]) + sides[2] + leak
    pressure_rhs = -(residuals[0] + residuals[1] + residuals[2])
    smoothed = relax * pressure_rhs / diagonal
    remainder = pressure_rhs - apply_operator(smoothed, coefs, diagonal)
    block_x = (jnp.arange(NX, dtype=jnp.int32) // CX)[:, None, None]
    block_y = (jnp.arange(NY, dtype=jnp.int32) // CY)[None, :, None]
    global_agg = ((block_x * N_GY + block_y) * AGG_DEV + aggregate).astype(jnp.int32)
    flat_agg = global_agg.reshape(-1)
    coarse_rhs = jax.ops.segment_sum(remainder.reshape(-1), flat_agg, num_segments=NAGG)
    matrix = jnp.diag(jax.ops.segment_sum(leak.reshape(-1), flat_agg, num_segments=NAGG))
    agg_pairs = pairs(global_agg)
    for d in range(3):
        low_agg = agg_pairs[d][0].reshape(-1)
        high_agg = agg_pairs[d][1].reshape(-1)
        crossing = jnp.where(low_agg != high_agg, coefs[d].reshape(-1), 0.0)
        row_ids = jnp.concatenate([low_agg, high_agg, low_agg, high_agg])
        col_ids = jnp.concatenate([low_agg, high_agg, high_agg, low_agg])
        entries = jnp.concatenate([crossing, crossing, -crossing, -crossing])
        flat_pos = (row_ids * NAGG + col_ids).astype(jnp.int32)
        matrix = matrix + jax.ops.segment_sum(entries, flat_pos, num_segments=NAGG * NAGG).reshape(NAGG, NAGG)
    coarse = coarse_solve(matrix, coarse_rhs)
    corrected = smoothed + coarse[global_agg]
    pressure_update = corrected + relax * (pressure_rhs - apply_operator(corrected, coefs, diagonal)) / diagonal
    return jnp.stack(residuals), pressure_update, well_residual
```

```python
import jax
import jax.numpy as jnp
from jax import lax
from jax.experimental import pallas as pl
from jax.experimental.pallas import tpu as pltpu
from jax.sharding import PartitionSpec as P

CX, CY, NZ = 32, 32, 128
PERF = 16
GROUPS = 8
CITERS = 24
NGX, NGY = 8, 16
NDEV = NGX * NGY
ROWS = 384
RHS_AT, OUT_AT = 320, 328

precise = lax.Precision.HIGHEST
compress = (0.001, 0.001, 0.005)
viscosity = (0.5, 1.5, 0.2)
density = (1.0, 0.8, 0.2)
gravity_step = 0.05
relax = 0.6
dead_leak = 0.001

BIG = 60 * 1024 * 1024
f32, i32 = jnp.float32, jnp.int32
MESH = pl.DeviceIdType.MESH
ANY = pl.BlockSpec(memory_space=pl.ANY)
VMEM = pl.BlockSpec(memory_space=pltpu.VMEM)
SMEM = pl.BlockSpec(memory_space=pltpu.SMEM)


def iota(shape, dim):
    return lax.broadcasted_iota(i32, shape, dim)


def greet(barrier):
    place_x, place_y = lax.axis_index("gx"), lax.axis_index("gy")
    for k in range(1, NGX):
        pl.semaphore_signal(barrier, inc=1, device_id=(lax.rem(place_x + k, NGX), place_y), device_id_type=MESH)
    for k in range(1, NGY):
        pl.semaphore_signal(barrier, inc=1, device_id=(place_x, lax.rem(place_y + k, NGY)), device_id_type=MESH)


def remote(src, dst, send, recv, x, y):
    return pltpu.make_async_remote_copy(
        src_ref=src, dst_ref=dst, send_sem=send, recv_sem=recv, device_id=(x, y), device_id_type=MESH
    )


def exchange_kernel(
    p, ws, gs, act, tx, ty, agg, cells, windex, hole,
    xlo_f, xlo_i, xhi_f, xhi_i, ylo_f, ylo_i, yhi_f, yhi_i, wells,
    face_send, face_recv, send_x, recv_x, send_y, recv_y,
):
    place_x, place_y = lax.axis_index("gx"), lax.axis_index("gy")
    me = place_y * NGX + place_x
    barrier = pltpu.get_barrier_semaphore()
    greet(barrier)
    lane = iota((1, NZ), 1)
    pad = lambda v: jnp.concatenate([v, jnp.zeros((4, NZ - PERF), f32)], axis=1)
    both = pad(cells[...].astype(f32)) + pltpu.roll(pad(windex[...]), PERF, 1)
    row, hole_row = jnp.zeros((1, NZ), f32), jnp.zeros((1, NZ), f32)
    for j in range(4):
        piece = both[j : j + 1]
        if j:
            piece = pltpu.roll(piece, 32 * j, 1)
        row = row + piece
        hole_row = jnp.where(lane // 32 == j, hole[j], hole_row)
    wells[0, pl.ds(me, 1), :] = row
    wells[1, pl.ds(me, 1), :] = hole_row
    pl.semaphore_wait(barrier, NGX - 1 + NGY - 1)

    own = wells.at[:, pl.ds(me, 1), :]
    sends = []
    for k in range(1, NGX):
        sends.append(remote(own, own, send_x.at[k], recv_x.at[k], lax.rem(place_x + k, NGX), place_y))
    up_x, down_x = lax.rem(place_x + 1, NGX), lax.rem(place_x + NGX - 1, NGX)
    up_y, down_y = lax.rem(place_y + 1, NGY), lax.rem(place_y + NGY - 1, NGY)
    faces = []

    def face(src, dst, x, y):
        n = len(faces)
        faces.append(remote(src, dst, face_send.at[n], face_recv.at[n], x, y))

    for n, ref in enumerate((p, ws, gs, tx)):
        face(ref.at[CX - 1], xlo_f.at[n], up_x, place_y)
    for n, ref in enumerate((act, agg)):
        face(ref.at[CX - 1], xlo_i.at[n], up_x, place_y)
    for n, ref in enumerate((p, ws, gs)):
        face(ref.at[0], xhi_f.at[n], down_x, place_y)
    for n, ref in enumerate((act, agg)):
        face(ref.at[0], xhi_i.at[n], down_x, place_y)
    for n, ref in enumerate((p, ws, gs, ty)):
        face(ref.at[:, CY - 1, :], ylo_f.at[n], place_x, up_y)
    for n, ref in enumerate((act, agg)):
        face(ref.at[:, CY - 1, :], ylo_i.at[n], place_x, up_y)
    for n, ref in enumerate((p, ws, gs)):
        face(ref.at[:, 0, :], yhi_f.at[n], place_x, down_y)
    for n, ref in enumerate((act, agg)):
        face(ref.at[:, 0, :], yhi_i.at[n], place_x, down_y)
    for copy in sends + faces:
        copy.start()
    for k in range(1, NGX):
        source = place_y * NGX + lax.rem(place_x + NGX - k, NGX)
        there = wells.at[:, pl.ds(source, 1), :]
        remote(there, there, send_x.at[k], recv_x.at[k], place_x, place_y).wait_recv()
    block = wells.at[:, pl.ds(place_y * NGX, NGX), :]
    for k in range(1, NGY):
        copy = remote(block, block, send_y.at[k], recv_y.at[k], place_x, lax.rem(place_y + k, NGY))
        copy.start()
        sends.append(copy)
    for k in range(1, NGY):
        source = lax.rem(place_y + NGY - k, NGY)
        there = wells.at[:, pl.ds(source * NGX, NGX), :]
        remote(there, there, send_y.at[k], recv_y.at[k], place_x, place_y).wait_recv()
    for copy in faces:
        copy.wait_recv()
    for copy in sends + faces:
        copy.wait_send()


def exchange(p, ws, gs, act, tx, ty, agg, cells, windex, hole):
    shape = lambda n, t: jax.ShapeDtypeStruct((n, 32, NZ), t)
    dma = pltpu.SemaphoreType.DMA
    return pl.pallas_call(
        exchange_kernel,
        out_shape=[
            shape(4, f32), shape(2, i32), shape(3, f32), shape(2, i32),
            shape(4, f32), shape(2, i32), shape(3, f32), shape(2, i32),
            jax.ShapeDtypeStruct((2, NDEV, NZ), f32),
        ],
        in_specs=[ANY] * 7 + [VMEM, VMEM, SMEM],
        out_specs=[ANY] * 8 + [VMEM],
        scratch_shapes=[dma((22,)), dma((22,)), dma((NGX,)), dma((NGX,)), dma((NGY,)), dma((NGY,))],
        compiler_params=pltpu.CompilerParams(collective_id=0, has_side_effects=True, vmem_limit_bytes=BIG),
        name="exchange",
    )(p, ws, gs, act, tx, ty, agg, cells, windex, hole)


def mobility_of(p, ws, gs):
    so = 1.0 - ws - gs
    out = []
    for k, s in enumerate((ws, so, gs)):
        out.append((1.0 + compress[k] * (p - 1.0)) * s * s * (1.0 / viscosity[k]))
    return out


def lane_next(v):
    return pltpu.roll(v, NZ - 1, 1)


def lane_prev(v):
    return pltpu.roll(v, 1, 1)


PAIRS = [(a, b) for a in range(GROUPS) for b in range(a + 1, GROUPS)]


def local_kernel(
    p_h, ws_h, gs_h, old_h, pv_h, tx_h, ty_h, tz_h, act_h, agg_h,
    xlo_fh, xlo_ih, xhi_fh, xhi_ih, ylo_fh, ylo_ih, yhi_fh, yhi_ih, wells,
    res_o, t_o, dinv_o, cx_o, cy_o, cz_o, sums_o, faces_o, parts_o,
    p, ws, gs, act, agg, old, pv, tx, ty, tz,
    xlo_f, xlo_i, xhi_i, ylo_f, ylo_i, yhi_f, yhi_i,
    lam, live, mob, w0, w1, trows, loc, loc_s,
    fy, cx, cy, cz, s, rem, leak, dinv, res, t, yh, acc, e4, own4, nb4, s4,
    sem, out_sem, one_sem,
):
    place_x, place_y = lax.axis_index("gx"), lax.axis_index("gy")
    copies = []

    def fetch(src, dst):
        copy = pltpu.make_async_copy(src, dst, sem.at[len(copies)])
        copy.start()
        copies.append(copy)

    body = (pl.ds(0, CX), pl.ds(0, CY), slice(None))
    for src, dst in ((p_h, p), (ws_h, ws), (gs_h, gs), (act_h, act)):
        fetch(src, dst.at[body])
    for n, dst in enumerate((p, ws, gs)):
        fetch(xhi_fh.at[n], dst.at[CX, pl.ds(0, CY), :])
    fetch(xhi_ih.at[0], act.at[CX, pl.ds(0, CY), :])
    early = len(copies)
    for src, dst in ((xlo_fh, xlo_f), (xlo_ih, xlo_i), (xhi_ih, xhi_i), (ylo_fh, ylo_f), (ylo_ih, ylo_i), (yhi_fh, yhi_f), (yhi_ih, yhi_i)):
        fetch(src, dst)
    for src, dst in ((tx_h, tx), (ty_h, ty), (tz_h, tz), (pv_h, pv), (old_h, old)):
        fetch(src, dst)
    fetch(agg_h, agg.at[body])
    fetch(xhi_ih.at[1], agg.at[CX, pl.ds(0, CY), :])

    lane = iota((NDEV, NZ), 1)
    table = wells[0]
    cell = table.astype(i32)
    cell_x, cell_y, layer = cell >> 16, (cell >> 7) & 511, cell & 127
    slot = lane & 31
    here = (slot < PERF) & (cell >= 0) & ((cell_x >> 5) == place_x) & ((cell_y >> 5) == place_y)
    local = ((((cell_x & 31) << 5) + (cell_y & 31)) << 7) + layer
    local = jnp.where(here, local, -1)
    flag = jnp.where(here, 1.0, 0.0).astype(jnp.bfloat16)
    at_in, at_out = iota((NZ, NZ), 0), iota((NZ, NZ), 1)
    pick = ((at_in // 32 == at_out // 32) & (at_out % 32 == 16)) | (at_out == 17)
    counts = jnp.dot(flag, jnp.where(pick, 1.0, 0.0).astype(jnp.bfloat16), preferred_element_type=f32).astype(i32)
    first_layer = pltpu.roll(layer, 18, 1)
    loc[...] = jnp.where(slot < PERF, local, jnp.where(slot == 18, first_layer, counts))
    to_scalar = pltpu.make_async_copy(loc, loc_s, one_sem)
    to_scalar.start()

    w0[...] = jnp.zeros_like(w0)
    w1[...] = jnp.zeros_like(w1)
    trows[...] = jnp.zeros_like(trows)
    for copy in copies[:early]:
        copy.wait()

    end_x = jnp.where(place_x == NGX - 1, 0.0, 1.0)
    end_y = jnp.where(place_y == NGY - 1, 0.0, 1.0)

    def mobilities(x, _):
        pp = p[x, pl.ds(0, CY), :]
        parts = mobility_of(pp, ws[x, pl.ds(0, CY), :], gs[x, pl.ds(0, CY), :])
        for k in range(3):
            lam[k, x, pl.ds(0, CY), :] = parts[k]
        m = act[x, pl.ds(0, CY), :].astype(f32) * jnp.where(x == CX, end_x, 1.0)
        live[x, pl.ds(0, CY), :] = m
        mob[x] = m * (parts[0] + parts[1] + parts[2])
        return 0

    lax.fori_loop(0, CX + 1, mobilities, 0)
    to_scalar.wait()

    row_lane = iota((1, NZ), 1)

    def one_row(r, _):
        @pl.when(loc_s[r, 17] > 0)
        def _():
            for j in range(4):

                @pl.when(loc_s[r, 32 * j + 16] > 0)
                def _():
                    shift = loc_s[r, 32 * j + 18] - (32 * j + PERF) + 2 * NZ
                    shift = lax.rem(shift, NZ)
                    index_z = pltpu.roll(wells[0, pl.ds(r, 1), :], shift, 1)
                    hole_z = pltpu.roll(wells[1, pl.ds(r, 1), :], shift, 1)
                    drive_z = index_z * hole_z
                    mob_z = jnp.zeros((1, NZ), f32)
                    press_z = jnp.zeros((1, NZ), f32)
                    for k in range(PERF):
                        at = loc_s[r, 32 * j + k]
                        z = (at & 127) | (at >> 31)
                        q = jnp.maximum(at, 0) >> 7
                        qx, qy = q >> 5, q & 31
                        hit = row_lane == z
                        w0[qx, pl.ds(qy, 1), :] += jnp.where(hit, index_z, 0.0)
                        w1[qx, pl.ds(qy, 1), :] += jnp.where(hit, drive_z, 0.0)
                        mob_z = jnp.where(hit, mob[qx, pl.ds(qy, 1), :], mob_z)
                        press_z = jnp.where(hit, p[qx, pl.ds(qy, 1), :], press_z)
                    well = ((r & (NGX - 1)) * NGY + (r >> 3)) * 4 + j
                    trows[pl.ds(well, 1), :] = index_z * mob_z * (hole_z - press_z)

        return 0

    lax.fori_loop(0, NDEV, one_row, 0)
    total = lax.dot_general(
        jnp.ones((8, NZ), f32), trows[...], (((1,), (1,)), ((), ())), precision=precise, preferred_element_type=f32
    )
    sub = iota((8, NZ), 0)
    parts = jnp.zeros((8, NZ), f32)
    for k in range(NGX):
        piece = total[:, NZ * (k // 2) : NZ * (k // 2) + NZ]
        if k % 2:
            piece = pltpu.roll(piece, 64, 1)
        parts = jnp.where(sub == k, piece, parts)
    parts_o[...] = parts

    for copy in copies[early:]:
        copy.wait()

    dead_x = jnp.where(place_x == 0, 0.0, 1.0)
    dead_y = jnp.where(place_y == 0, 0.0, 1.0)
    low = mobility_of(xlo_f[0], xlo_f[1], xlo_f[2])
    face = xlo_f[3] * (xlo_i[0].astype(f32) * dead_x) * live[0, pl.ds(0, CY), :]
    drop = xlo_f[0] - p[0, pl.ds(0, CY), :]
    high = [lam[k, 0, pl.ds(0, CY), :] for k in range(3)]
    below = [face * (0.5 * (low[k] + high[k])) * drop for k in range(3)]
    below.append(face * (0.5 * ((low[0] + low[1] + low[2]) + (high[0] + high[1] + high[2]))))
    cx[0] = below[3]
    low = mobility_of(ylo_f[0], ylo_f[1], ylo_f[2])
    for k in range(3):
        yh[k] = low[k]
    yh[3] = ylo_f[0]
    yh[4] = ylo_f[3] * (ylo_i[0].astype(f32) * dead_y)
    high = mobility_of(yhi_f[0], yhi_f[1], yhi_f[2])
    for k in range(3):
        yh[5 + k] = high[k]
    yh[8] = yhi_f[0]
    yh[9] = yhi_i[0].astype(f32) * end_y

    layer_8 = iota((8, NZ), 1)
    row_8 = iota((8, NZ), 0)

    def residuals(x, carry):
        below = [list(v) for v in carry]
        one = pl.ds(x, 1)
        for k in range(3):
            lam[k, x, pl.ds(CY, 1), :] = yh[5 + k, one, :]
        p[x, pl.ds(CY, 1), :] = yh[8, one, :]
        live[x, pl.ds(CY, 1), :] = yh[9, one, :]
        agg[x, pl.ds(CY, 1), :] = yhi_i[1, one, :]
        own4[2, one, :] = agg[x, pl.ds(0, 1), :]
        own4[3, one, :] = agg[x, pl.ds(CY - 1, 1), :]
        face0 = yh[4, one, :] * live[x, pl.ds(0, 1), :]
        drop0 = yh[3, one, :] - p[x, pl.ds(0, 1), :]
        up0 = [lam[k, x, pl.ds(0, 1), :] for k in range(3)]
        dn0 = [yh[k, one, :] for k in range(3)]
        for k in range(3):
            fy[k, x, pl.ds(0, 1), :] = face0 * (0.5 * (dn0[k] + up0[k])) * drop0
        cy0 = face0 * (0.5 * ((dn0[0] + dn0[1] + dn0[2]) + (up0[0] + up0[1] + up0[2])))
        cy[x, pl.ds(0, 1), :] = cy0
        e4[2, one, :] = cy0
        for c in range(4):
            at = pl.ds(8 * c, 8)
            up = pl.ds(8 * c + 1, 8)
            pp, m = p[x, at, :], live[x, at, :]
            la = [lam[k, x, at, :] for k in range(3)]
            lt = la[0] + la[1] + la[2]
            net = []
            ln = [lam[k, x + 1, at, :] for k in range(3)]
            f = tx[x, at, :] * m * live[x + 1, at, :]
            d = pp - p[x + 1, at, :]
            for k in range(3):
                flux = f * (0.5 * (la[k] + ln[k])) * d
                net.append(flux - below[k][c])
                below[k][c] = flux
            e = f * (0.5 * (lt + (ln[0] + ln[1] + ln[2])))
            cx[x + 1, at, :] = e
            diag = e + below[3][c]
            below[3][c] = e
            ln = [lam[k, x, up, :] for k in range(3)]
            f = ty[x, at, :] * m * live[x, up, :]
            d = pp - p[x, up, :]
            for k in range(3):
                flux = f * (0.5 * (la[k] + ln[k])) * d
                fy[k, x, up, :] = flux
                net[k] = net[k] + (flux - fy[k, x, at, :])
            e = f * (0.5 * (lt + (ln[0] + ln[1] + ln[2])))
            cy[x, up, :] = e
            diag = diag + (e + cy[x, at, :])
            ln = [lane_next(v) for v in la]
            f = jnp.where(layer_8 == NZ - 1, 0.0, tz[x, at, :] * m * lane_next(m))
            d = pp - lane_next(pp)
            for k in range(3):
                flux = f * (0.5 * (la[k] + ln[k])) * (d + density[k] * gravity_step)
                net[k] = net[k] + (flux - lane_prev(flux))
            e = f * (0.5 * (lt + (ln[0] + ln[1] + ln[2])))
            cz[x, at, :] = e
            diag = diag + (e + lane_prev(e))
            sw, sg = ws[x, at, :], gs[x, at, :]
            so = 1.0 - sw - sg
            vol = pv[x, at, :]
            wa, wb = w0[x, at, :], w1[x, at, :]
            pull = m * (wb - pp * wa)
            rhs = None
            for k, sat in enumerate((sw, so, sg)):
                held = (1.0 + compress[k] * (pp - 1.0)) * sat
                r = m * (vol * (held - old[k, x, at, :]) + net[k]) - pull * la[k]
                res[k, x, at, :] = r
                rhs = r if rhs is None else rhs + r
            rhs = -rhs
            store = vol * (compress[0] * sw + compress[1] * so + compress[2] * sg)
            lk = m * (store + m * wa * lt) + dead_leak * (1.0 - m)
            leak[x, at, :] = lk
            diag = diag + lk
            di = relax / diag
            dinv[x, at, :] = di
            sm = rhs * di
            s[x + 1, pl.ds(8 * c + 1, 8), :] = sm
            rem[x, at, :] = rhs - diag * sm
        e4[3, one, :] = cy[x, pl.ds(CY, 1), :]
        s4[2, one, :] = s[x + 1, pl.ds(1, 1), :]
        s4[3, one, :] = s[x + 1, pl.ds(CY, 1), :]
        s[x + 1, pl.ds(0, 1), :] = jnp.zeros((1, NZ), f32)
        s[x + 1, pl.ds(CY + 1, 1), :] = jnp.zeros((1, NZ), f32)
        return tuple(tuple(v) for v in below)

    lax.fori_loop(0, CX, residuals, tuple(tuple(v[8 * c : 8 * c + 8] for c in range(4)) for v in below))
    s4[0] = s[1, pl.ds(1, CY), :]
    s4[1] = s[CX, pl.ds(1, CY), :]
    s[0] = jnp.zeros_like(s[0])
    s[CX + 1] = jnp.zeros_like(s[0])
    outs = []

    def give(src, dst):
        copy = pltpu.make_async_copy(src, dst, out_sem.at[len(outs)])
        copy.start()
        outs.append(copy)

    give(res, res_o)
    give(dinv, dinv_o)
    give(cx, cx_o)
    give(cy, cy_o)
    give(cz, cz_o)
    give(s4, faces_o)

    zero = jnp.zeros((8, NZ), f32)

    def remainders(x, carry):
        lk_sum, re_sum, z_sum = [list(v) for v in carry]
        for c in range(4):
            at = pl.ds(8 * c, 8)
            up = pl.ds(8 * c + 1, 8)
            here = s[x + 1, up, :]
            z = cz[x, at, :]
            near = cx[x + 1, at, :] * s[x + 2, up, :] + cx[x, at, :] * s[x, up, :]
            near = near + (cy[x, up, :] * s[x + 1, pl.ds(8 * c + 2, 8), :] + cy[x, at, :] * s[x + 1, at, :])
            near = near + (z * lane_next(here) + lane_prev(z * here))
            re = rem[x, at, :] + near
            t[x, at, :] = here + dinv[x, at, :] * re
            lk = leak[x, at, :]
            a = agg[x, at, :]
            cross = jnp.where(a != lane_next(a), z, 0.0)
            for g in range(GROUPS):
                hit = a == g
                re_sum[g] = re_sum[g] + jnp.where(hit, re, 0.0)
                lk_sum[g] = lk_sum[g] + jnp.where(hit, lk, 0.0)
                if g < GROUPS - 1:
                    z_sum[g] = z_sum[g] + jnp.where(hit, cross, 0.0)
        return tuple(lk_sum), tuple(re_sum), tuple(z_sum)

    lk_sum, re_sum, z_sum = lax.fori_loop(
        0, CX, remainders, ((zero,) * GROUPS, (zero,) * GROUPS, (zero,) * (GROUPS - 1))
    )
    give(t, t_o)

    def line(v):
        return jnp.sum(v, axis=0, keepdims=True)

    acc[...] = jnp.zeros_like(acc)
    for g in range(GROUPS):
        acc[g * GROUPS + g, :] = line(lk_sum[g])[0]
        acc[RHS_AT + g, :] = line(re_sum[g])[0]

    def crossings(x, sums):
        sums = list(sums)
        for c in range(4):
            at = pl.ds(8 * c, 8)
            up = pl.ds(8 * c + 1, 8)
            a = agg[x, at, :]
            for b, e, ok in (
                (agg[x + 1, at, :], cx[x + 1, at, :], x < CX - 1),
                (agg[x, up, :], cy[x, up, :], (row_8 < 7) if c == 3 else None),
            ):
                code = jnp.minimum(a, b) * GROUPS + jnp.maximum(a, b)
                if ok is not None:
                    code = jnp.where(ok, code, -1)
                for n, (g, h) in enumerate(PAIRS):
                    sums[n] = sums[n] + jnp.where(code == g * GROUPS + h, e, 0.0)
        return tuple(sums)

    sums = lax.fori_loop(0, CX, crossings, (zero,) * len(PAIRS))
    for n, (g, h) in enumerate(PAIRS):
        v = sums[n]
        if h == g + 1:
            v = v + z_sum[g]
        v = line(v)[0]
        acc[h * GROUPS + g, :] = v
        acc[g * GROUPS + h, :] = v

    e4[0] = cx[0]
    e4[1] = cx[CX]
    own4[0] = agg[0, pl.ds(0, CY), :]
    own4[1] = agg[CX - 1, pl.ds(0, CY), :]
    nb4[0] = xlo_i[1]
    nb4[1] = xhi_i[1]
    nb4[2] = ylo_i[1]
    nb4[3] = yhi_i[1]

    def side(d, _):
        e, a, b = e4[d], own4[d], nb4[d]
        es = e * s4[d]
        goes = []
        for g in range(GROUPS):
            goes.append(line(jnp.where(b == g, es, 0.0)))
        acc[pl.ds(pl.multiple_of(OUT_AT + d * GROUPS, 8), GROUPS), :] = jnp.concatenate(goes, axis=0)
        for h in range(GROUPS):
            w = jnp.where(b == h, e, 0.0)
            rows = [line(jnp.where(a == g, w, 0.0)) for g in range(GROUPS)]
            start = pl.multiple_of(((d + 1) * GROUPS + h) * GROUPS, 8)
            acc[pl.ds(start, GROUPS), :] = jnp.concatenate(rows, axis=0)
        return 0

    lax.fori_loop(0, 4, side, 0)
    for n in range(3):
        flat = jnp.sum(acc[pl.ds(NZ * n, NZ), :].T, axis=0, keepdims=True)
        sums_o[n] = flat
    for copy in outs:
        copy.wait()


def local(args, halos, wells):
    v = pltpu.VMEM
    blk = (CX, CY, NZ)
    sds = jax.ShapeDtypeStruct
    dma = pltpu.SemaphoreType.DMA
    return pl.pallas_call(
        local_kernel,
        out_shape=[
            sds((3,) + blk, f32), sds(blk, f32), sds(blk, f32), sds((CX + 1, CY, NZ), f32),
            sds((CX, CY + 8, NZ), f32), sds(blk, f32), sds((3, 1, NZ), f32), sds((4, 32, NZ), f32), sds((8, NZ), f32),
        ],
        in_specs=[ANY] * 18 + [VMEM],
        out_specs=[ANY] * 6 + [VMEM, ANY, VMEM],
        scratch_shapes=[
            v((CX + 1, CY + 8, NZ), f32), v((CX + 1, CY, NZ), f32), v((CX + 1, CY, NZ), f32), v((CX + 1, CY, NZ), i32),
            v((CX + 1, CY + 8, NZ), i32), v((3,) + blk, f32), v(blk, f32), v(blk, f32), v(blk, f32), v(blk, f32),
            v((4, 32, NZ), f32), v((2, 32, NZ), i32), v((2, 32, NZ), i32), v((4, 32, NZ), f32), v((2, 32, NZ), i32),
            v((3, 32, NZ), f32), v((2, 32, NZ), i32),
            v((3, CX + 1, CY + 8, NZ), f32), v((CX + 1, CY + 8, NZ), f32), v((CX + 1, CY, NZ), f32),
            v(blk, f32), v(blk, f32), v((4 * NDEV, NZ), f32), v((NDEV, NZ), i32), pltpu.SMEM((NDEV, NZ), i32),
            v((3, CX, CY + 8, NZ), f32), v((CX + 1, CY, NZ), f32), v((CX, CY + 8, NZ), f32), v(blk, f32),
            v((CX + 2, CY + 8, NZ), f32), v(blk, f32), v(blk, f32), v(blk, f32), v((3,) + blk, f32), v(blk, f32),
            v((10, 32, NZ), f32), v((ROWS, NZ), f32), v((4, 32, NZ), f32), v((4, 32, NZ), i32), v((4, 32, NZ), i32), v((4, 32, NZ), f32),
            dma((32,)), dma((8,)), dma,
        ],
        compiler_params=pltpu.CompilerParams(vmem_limit_bytes=BIG),
        name="local",
    )(*args, *halos, wells)


def coarse_kernel(
    sums, parts, faces, t_h, dinv_h, cx_h, cy_h, cz_h, agg_h, xlo_i, xhi_i, ylo_i, yhi_i,
    update_o, well_o,
    gather, mat, slots, send_rows, rows_x, rows_y, tall, dinv, cx, cy, cz, agg, far, pc,
    sem, send_x, recv_x, send_y, recv_y, psend_x, precv_x, psend_y, precv_y, fsend, frecv,
):
    place_x, place_y = lax.axis_index("gx"), lax.axis_index("gy")
    me = place_y * NGX + place_x
    barrier = pltpu.get_barrier_semaphore()
    greet(barrier)
    loads = []
    body = (slice(None), pl.ds(0, CY), slice(None))
    for src, dst in ((t_h, tall), (dinv_h, dinv), (cx_h, cx), (cy_h, cy), (cz_h, cz), (agg_h, agg)):
        copy = pltpu.make_async_copy(src, dst, sem.at[len(loads)])
        copy.start()
        loads.append(copy)
    for n in range(3):
        gather[n, pl.ds(me, 1), :] = sums[n]
    rows_x[pl.ds(place_x, 1), :] = parts[pl.ds(place_x, 1), :]
    pl.semaphore_wait(barrier, NGX - 1 + NGY - 1)

    sends = []
    own = gather.at[:, pl.ds(me, 1), :]
    for k in range(1, NGX):
        peer = lax.rem(place_x + k, NGX)
        sends.append(remote(own, own, send_x.at[k], recv_x.at[k], peer, place_y))
    for k in range(1, NGX):
        peer = lax.rem(place_x + k, NGX)
        sends.append(
            remote(parts.at[pl.ds(peer, 1), :], rows_x.at[pl.ds(place_x, 1), :], psend_x.at[k], precv_x.at[k], peer, place_y)
        )
    halo = [
        remote(faces.at[1], far.at[0], fsend.at[0], frecv.at[0], lax.rem(place_x + 1, NGX), place_y),
        remote(faces.at[0], far.at[1], fsend.at[1], frecv.at[1], lax.rem(place_x + NGX - 1, NGX), place_y),
        remote(faces.at[3], far.at[2], fsend.at[2], frecv.at[2], place_x, lax.rem(place_y + 1, NGY)),
        remote(faces.at[2], far.at[3], fsend.at[3], frecv.at[3], place_x, lax.rem(place_y + NGY - 1, NGY)),
    ]
    for copy in sends + halo:
        copy.start()
    for k in range(1, NGX):
        source = place_y * NGX + lax.rem(place_x + NGX - k, NGX)
        there = gather.at[:, pl.ds(source, 1), :]
        remote(there, there, send_x.at[k], recv_x.at[k], place_x, place_y).wait_recv()
    block = gather.at[:, pl.ds(place_y * NGX, NGX), :]
    for k in range(1, NGY):
        copy = remote(block, block, send_y.at[k], recv_y.at[k], place_x, lax.rem(place_y + k, NGY))
        copy.start()
        sends.append(copy)
    for k in range(1, NGX):
        source = lax.rem(place_x + NGX - k, NGX)
        there = rows_x.at[pl.ds(source, 1), :]
        remote(there, there, psend_x.at[k], precv_x.at[k], place_x, place_y).wait_recv()
    line = jnp.sum(rows_x[...], axis=0, keepdims=True)
    for k in range(NGY):
        send_rows[k : k + 1, :] = line if k == 0 else pltpu.roll(line, NZ - 4 * k, 1)
    rows_y[pl.ds(place_y, 1), :] = send_rows[pl.ds(place_y, 1), :]
    for k in range(1, NGY):
        peer = lax.rem(place_y + k, NGY)
        copy = remote(
            send_rows.at[pl.ds(peer, 1), :], rows_y.at[pl.ds(place_y, 1), :], psend_y.at[k], precv_y.at[k], place_x, peer
        )
        copy.start()
        sends.append(copy)
    for k in range(1, NGY):
        source = lax.rem(place_y + NGY - k, NGY)
        there = gather.at[:, pl.ds(source * NGX, NGX), :]
        remote(there, there, send_y.at[k], recv_y.at[k], place_x, place_y).wait_recv()

    for n in range(3):
        mat[pl.ds(NZ * n, NZ), :] = gather[n].T
    sub = iota((8, NZ), 0)

    def rows(n):
        return mat[pl.ds(8 * n, 8), :]

    moves = (0, 1, NZ - 1, NGX, NZ - NGX)
    total = jnp.zeros((8, NZ), f32)
    for n in range(5 * GROUPS):
        total = total + rows(n)
    for h in range(GROUPS):
        block = rows(h)
        slots[pl.ds(8 * h, 8), :] = jnp.where(sub == h, total, -block)
    for d in range(1, 5):
        for h in range(GROUPS):
            v = -rows(d * GROUPS + h)
            slots[pl.ds((d * GROUPS + h) * 8, 8), :] = pltpu.roll(v, (NZ - moves[d]) % NZ, 1)
    rhs = rows(RHS_AT // 8)
    for d in range(1, 5):
        away = (0, 2, 1, 4, 3)[d]
        rhs = rhs + pltpu.roll(rows(OUT_AT // 8 + away - 1), moves[d], 1)

    def dot(a, b):
        return jnp.sum(jnp.sum(a * b, axis=0, keepdims=True), axis=1, keepdims=True)

    def one_step(_, carry):
        x, r, q, rr = carry
        sums5 = [None] * 5
        for h in range(GROUPS):
            spread = jnp.broadcast_to(q[h : h + 1, :], (8, NZ))
            for d in range(5):
                v = slots[pl.ds((d * GROUPS + h) * 8, 8), :] * spread
                sums5[d] = v if sums5[d] is None else sums5[d] + v
        image = sums5[0]
        for d in range(1, 5):
            image = image + pltpu.roll(sums5[d], moves[d], 1)
        alpha = rr / dot(q, image)
        x = x + alpha * q
        r = r - alpha * image
        new = dot(r, r)
        q = r + (new / rr) * q
        return x, r, q, new

    coarse = lax.fori_loop(0, CITERS, one_step, (jnp.zeros((8, NZ), f32), rhs, rhs, dot(rhs, rhs)))[0]
    mine = iota((8, NZ), 1) == me
    values = []
    for d in range(5):
        v = coarse if d == 0 else pltpu.roll(coarse, moves[d], 1)
        values.append(jnp.sum(jnp.where(mine, v, 0.0), axis=1, keepdims=True))

    def look_up(ids, d):
        v = jnp.broadcast_to(values[d][0:1, :], ids.shape)
        for g in range(1, GROUPS):
            v = jnp.where(ids == g, values[d][g : g + 1, :], v)
        return v

    for copy in halo:
        copy.wait_recv()
    for copy in loads:
        copy.wait()
    far[0] = cx[0] * (far[0] + look_up(xlo_i[1], 1))
    far[1] = far[1] + look_up(xhi_i[1], 2)
    far[2] = far[2] + look_up(ylo_i[1], 3)
    far[3] = far[3] + look_up(yhi_i[1], 4)

    def fill(x, _):
        pc[x, pl.ds(0, CY), :] = look_up(agg[x], 0)
        pc[x, pl.ds(CY, 1), :] = far[3, pl.ds(x, 1), :]
        return 0

    lax.fori_loop(0, CX, fill, 0)
    pc[CX, pl.ds(0, CY), :] = far[1]
    def finish(x, below):
        c_here = pc[x, pl.ds(0, CY), :]
        e = cx[x + 1]
        near = e * pc[x + 1, pl.ds(0, CY), :] + below
        above = e * c_here
        up = cy[x, pl.ds(1, CY), :]
        near = near + up * pc[x, pl.ds(1, CY), :]
        lowrow = cy[x, pl.ds(0, 1), :] * far[2, pl.ds(x, 1), :]
        down = pltpu.roll(up * c_here, 1, 0)
        near = near + jnp.where(iota((CY, NZ), 0) == 0, lowrow, down)
        z = cz[x]
        near = near + (z * lane_next(c_here) + lane_prev(z * c_here))
        update_o[x] = tall[x] + (1.0 - relax) * c_here + dinv[x] * near
        return above

    lax.fori_loop(0, CX, finish, far[0])
    for k in range(1, NGY):
        source = lax.rem(place_y + NGY - k, NGY)
        there = rows_y.at[pl.ds(source, 1), :]
        remote(there, there, psend_y.at[k], precv_y.at[k], place_x, place_y).wait_recv()
    well_o[...] = jnp.sum(rows_y[...], axis=0, keepdims=True)
    for copy in sends + halo:
        copy.wait_send()


def coarse_part(sums, parts, faces, t, dinv, cx, cy, cz, agg, xlo_i, xhi_i, ylo_i, yhi_i):
    v = pltpu.VMEM
    blk = (CX, CY, NZ)
    sds = jax.ShapeDtypeStruct
    dma = pltpu.SemaphoreType.DMA
    return pl.pallas_call(
        coarse_kernel,
        out_shape=[sds(blk, f32), sds((1, NZ), f32)],
        in_specs=[VMEM, VMEM, ANY] + [ANY] * 6 + [VMEM] * 4,
        out_specs=[VMEM, VMEM],
        scratch_shapes=[
            v((3, NDEV, NZ), f32), v((ROWS, NZ), f32), v((5 * 64, NZ), f32), v((NGY, NZ), f32), v((NGX, NZ), f32), v((NGY, NZ), f32),
            v(blk, f32), v(blk, f32), v((CX + 1, CY, NZ), f32), v((CX, CY + 8, NZ), f32), v(blk, f32), v(blk, i32),
            v((4, 32, NZ), f32), v((CX + 1, CY + 8, NZ), f32),
            dma((8,)), dma((NGX,)), dma((NGX,)), dma((NGY,)), dma((NGY,)),
            dma((NGX,)), dma((NGX,)), dma((NGY,)), dma((NGY,)), dma((4,)), dma((4,)),
        ],
        compiler_params=pltpu.CompilerParams(
            collective_id=1, has_side_effects=True, vmem_limit_bytes=BIG
        ),
        name="coarse",
    )(sums, parts, faces, t, dinv, cx, cy, cz, agg, xlo_i, xhi_i, ylo_i, yhi_i)


def per_device(
    pressure, water_sat, gas_sat, old_content, pore_volume, trans_x, trans_y, trans_z, active, aggregate,
    well_cells, well_index, bottom_hole, well_target,
):
    *halos, wells = exchange(
        pressure, water_sat, gas_sat, active, trans_x, trans_y, aggregate, well_cells, well_index, bottom_hole
    )
    xlo_f, xlo_i, xhi_f, xhi_i, ylo_f, ylo_i, yhi_f, yhi_i = halos
    args = (pressure, water_sat, gas_sat, old_content, pore_volume, trans_x, trans_y, trans_z, active, aggregate)
    residual, t, dinv, cx, cy, cz, sums, faces, parts = local(args, halos, wells)
    update, well = coarse_part(sums, parts, faces, t, dinv, cx, cy, cz, aggregate, xlo_i, xhi_i, ylo_i, yhi_i)
    return residual, update, well[0, :4] - well_target


def solution(mesh):
    cells = P("gx", "gy", None)
    three = P(None, "gx", "gy", None)
    well, one = P(("gx", "gy"), None), P(("gx", "gy"))
    return jax.shard_map(
        per_device,
        mesh=mesh,
        in_specs=(cells, cells, cells, three) + (cells,) * 6 + (well, well, one, one),
        out_specs=(three, cells, one),
        check_vma=False,
    )
```

```python
import jax
import jax.numpy as jnp
from jax import lax
from jax.experimental import pallas as pl
from jax.experimental.pallas import tpu as pltpu
from jax.sharding import PartitionSpec as P

CX, CY, NZ = 32, 32, 128
PERF = 16
GROUPS = 8
CITERS = 24
NGX, NGY = 8, 16
NDEV = NGX * NGY
ROWS = 384
RHS_AT, OUT_AT, LEAK_AT = 320, 328, 360

precise = lax.Precision.HIGHEST
compress = (0.001, 0.001, 0.005)
viscosity = (0.5, 1.5, 0.2)
density = (1.0, 0.8, 0.2)
gravity_step = 0.05
relax = 0.6
dead_leak = 0.001

BIG = 60 * 1024 * 1024
f32, i32 = jnp.float32, jnp.int32
MESH = pl.DeviceIdType.MESH
ANY = pl.BlockSpec(memory_space=pl.ANY)
VMEM = pl.BlockSpec(memory_space=pltpu.VMEM)
SMEM = pl.BlockSpec(memory_space=pltpu.SMEM)


def iota(shape, dim):
    return lax.broadcasted_iota(i32, shape, dim)


def greet(barrier):
    place_x, place_y = lax.axis_index("gx"), lax.axis_index("gy")
    for k in range(1, NGX):
        pl.semaphore_signal(barrier, inc=1, device_id=(lax.rem(place_x + k, NGX), place_y), device_id_type=MESH)
    for k in range(1, NGY):
        pl.semaphore_signal(barrier, inc=1, device_id=(place_x, lax.rem(place_y + k, NGY)), device_id_type=MESH)


def loop(first, last, body, carry, steps):
    def several(i, carry):
        for n in range(steps):
            carry = body(first + i * steps + n, carry)
        return carry

    return lax.fori_loop(0, (last - first) // steps, several, carry)


def remote(src, dst, send, recv, x, y):
    return pltpu.make_async_remote_copy(
        src_ref=src, dst_ref=dst, send_sem=send, recv_sem=recv, device_id=(x, y), device_id_type=MESH
    )


def mobility_of(p, ws, gs):
    so = 1.0 - ws - gs
    out = []
    for k, s in enumerate((ws, so, gs)):
        out.append((1.0 + compress[k] * (p - 1.0)) * s * s * (1.0 / viscosity[k]))
    return out


def lane_next(v):
    return pltpu.roll(v, NZ - 1, 1)


def lane_prev(v):
    return pltpu.roll(v, 1, 1)


def line(v):
    return jnp.sum(v, axis=0, keepdims=True)


PAIRS = [(a, b) for a in range(GROUPS) for b in range(a + 1, GROUPS)]
BODY = (pl.ds(0, CX), pl.ds(0, CY), slice(None))


def exchange_kernel(
    p_h, ws_h, gs_h, act_h, tx_h, ty_h, tz_h, agg_h, cells, windex, hole,
    net_o, cx_o, cy_o, cz_o, mob_o, sums_o, nb_o, wells,
    p, ws, gs, act, tx, ty, tz, agg, xlo_f, xlo_i, xhi_f, xhi_i, ylo_f, ylo_i, yhi_f, yhi_i,
    lam, live, mob, net, fy, cx, cy, cz, yh, acc, e4, own4, nb4,
    load_sem, out_sem, face_send, face_recv, send_x, recv_x, send_y, recv_y,
):
    place_x, place_y = lax.axis_index("gx"), lax.axis_index("gy")
    me = place_y * NGX + place_x
    barrier = pltpu.get_barrier_semaphore()
    greet(barrier)
    loads = []
    for src, dst in (
        (p_h, p.at[BODY]), (ws_h, ws), (gs_h, gs), (act_h, act), (tx_h, tx), (ty_h, ty), (tz_h, tz), (agg_h, agg.at[BODY])
    ):
        copy = pltpu.make_async_copy(src, dst, load_sem.at[len(loads)])
        copy.start()
        loads.append(copy)
    lane = iota((1, NZ), 1)
    pad = lambda v: jnp.concatenate([v, jnp.zeros((4, NZ - PERF), f32)], axis=1)
    both = pad(cells[...].astype(f32)) + pltpu.roll(pad(windex[...]), PERF, 1)
    row, hole_row = jnp.zeros((1, NZ), f32), jnp.zeros((1, NZ), f32)
    for j in range(4):
        piece = both[j : j + 1]
        if j:
            piece = pltpu.roll(piece, 32 * j, 1)
        row = row + piece
        hole_row = jnp.where(lane // 32 == j, hole[j], hole_row)
    wells[0, pl.ds(me, 1), :] = row
    wells[1, pl.ds(me, 1), :] = hole_row
    pl.semaphore_wait(barrier, NGX - 1 + NGY - 1)

    own = wells.at[:, pl.ds(me, 1), :]
    sends = []
    for k in range(1, NGX):
        sends.append(remote(own, own, send_x.at[k], recv_x.at[k], lax.rem(place_x + k, NGX), place_y))
    up_x, down_x = lax.rem(place_x + 1, NGX), lax.rem(place_x + NGX - 1, NGX)
    up_y, down_y = lax.rem(place_y + 1, NGY), lax.rem(place_y + NGY - 1, NGY)
    faces = []

    def face(src, dst, x, y):
        n = len(faces)
        faces.append(remote(src, dst, face_send.at[n], face_recv.at[n], x, y))

    for n, ref in enumerate((p_h, ws_h, gs_h, tx_h)):
        face(ref.at[CX - 1], xlo_f.at[n], up_x, place_y)
    for n, ref in enumerate((act_h, agg_h)):
        face(ref.at[CX - 1], xlo_i.at[n], up_x, place_y)
    for n, ref in enumerate((p_h, ws_h, gs_h)):
        face(ref.at[0], xhi_f.at[n], down_x, place_y)
    for n, ref in enumerate((act_h, agg_h)):
        face(ref.at[0], xhi_i.at[n], down_x, place_y)
    for n, ref in enumerate((p_h, ws_h, gs_h, ty_h)):
        face(ref.at[:, CY - 1, :], ylo_f.at[n], place_x, up_y)
    for n, ref in enumerate((act_h, agg_h)):
        face(ref.at[:, CY - 1, :], ylo_i.at[n], place_x, up_y)
    for n, ref in enumerate((p_h, ws_h, gs_h)):
        face(ref.at[:, 0, :], yhi_f.at[n], place_x, down_y)
    for n, ref in enumerate((act_h, agg_h)):
        face(ref.at[:, 0, :], yhi_i.at[n], place_x, down_y)
    for copy in sends + faces:
        copy.start()

    for copy in loads[:4]:
        copy.wait()

    def mobilities(x, _):
        parts = mobility_of(p[x, pl.ds(0, CY), :], ws[x], gs[x])
        for k in range(3):
            lam[k, x, pl.ds(0, CY), :] = parts[k]
        m = act[x].astype(f32)
        live[x, pl.ds(0, CY), :] = m
        mob[x] = m * (parts[0] + parts[1] + parts[2])
        return 0

    loop(0, CX, mobilities, 0, 8)
    outs = []

    def give(src, dst):
        copy = pltpu.make_async_copy(src, dst, out_sem.at[len(outs)])
        copy.start()
        outs.append(copy)

    give(mob, mob_o)
    for copy in loads[4:]:
        copy.wait()
    for copy in faces:
        copy.wait_recv()

    end_x = jnp.where(place_x == NGX - 1, 0.0, 1.0)
    end_y = jnp.where(place_y == NGY - 1, 0.0, 1.0)
    dead_x = jnp.where(place_x == 0, 0.0, 1.0)
    dead_y = jnp.where(place_y == 0, 0.0, 1.0)
    high = mobility_of(xhi_f[0], xhi_f[1], xhi_f[2])
    for k in range(3):
        lam[k, CX, pl.ds(0, CY), :] = high[k]
    p[CX, pl.ds(0, CY), :] = xhi_f[0]
    live[CX, pl.ds(0, CY), :] = xhi_i[0].astype(f32) * end_x
    agg[CX, pl.ds(0, CY), :] = xhi_i[1]
    low = mobility_of(xlo_f[0], xlo_f[1], xlo_f[2])
    face_trans = xlo_f[3] * (xlo_i[0].astype(f32) * dead_x) * live[0, pl.ds(0, CY), :]
    drop = xlo_f[0] - p[0, pl.ds(0, CY), :]
    high = [lam[k, 0, pl.ds(0, CY), :] for k in range(3)]
    below = [face_trans * (0.5 * (low[k] + high[k])) * drop for k in range(3)]
    below.append(face_trans * (0.5 * ((low[0] + low[1] + low[2]) + (high[0] + high[1] + high[2]))))
    cx[0] = below[3]
    low = mobility_of(ylo_f[0], ylo_f[1], ylo_f[2])
    for k in range(3):
        yh[k] = low[k]
    yh[3] = ylo_f[0]
    yh[4] = ylo_f[3] * (ylo_i[0].astype(f32) * dead_y)
    high = mobility_of(yhi_f[0], yhi_f[1], yhi_f[2])
    for k in range(3):
        yh[5 + k] = high[k]
    yh[8] = yhi_f[0]
    yh[9] = yhi_i[0].astype(f32) * end_y
    layer_8 = iota((8, NZ), 1)
    row_8 = iota((8, NZ), 0)

    def fluxes(x, carry):
        below = [list(v) for v in carry]
        one = pl.ds(x, 1)
        for k in range(3):
            lam[k, x, pl.ds(CY, 1), :] = yh[5 + k, one, :]
        p[x, pl.ds(CY, 1), :] = yh[8, one, :]
        live[x, pl.ds(CY, 1), :] = yh[9, one, :]
        agg[x, pl.ds(CY, 1), :] = yhi_i[1, one, :]
        own4[2, one, :] = agg[x, pl.ds(0, 1), :]
        own4[3, one, :] = agg[x, pl.ds(CY - 1, 1), :]
        face0 = yh[4, one, :] * live[x, pl.ds(0, 1), :]
        drop0 = yh[3, one, :] - p[x, pl.ds(0, 1), :]
        up0 = [lam[k, x, pl.ds(0, 1), :] for k in range(3)]
        dn0 = [yh[k, one, :] for k in range(3)]
        for k in range(3):
            fy[k, x, pl.ds(0, 1), :] = face0 * (0.5 * (dn0[k] + up0[k])) * drop0
        cy0 = face0 * (0.5 * ((dn0[0] + dn0[1] + dn0[2]) + (up0[0] + up0[1] + up0[2])))
        cy[x, pl.ds(0, 1), :] = cy0
        e4[2, one, :] = cy0
        for c in range(4):
            at = pl.ds(8 * c, 8)
            up = pl.ds(8 * c + 1, 8)
            pp, m = p[x, at, :], live[x, at, :]
            la = [lam[k, x, at, :] for k in range(3)]
            lt = la[0] + la[1] + la[2]
            sums = []
            ln = [lam[k, x + 1, at, :] for k in range(3)]
            f = tx[x, at, :] * m * live[x + 1, at, :]
            d = pp - p[x + 1, at, :]
            for k in range(3):
                flux = f * (0.5 * (la[k] + ln[k])) * d
                sums.append(flux - below[k][c])
                below[k][c] = flux
            e = f * (0.5 * (lt + (ln[0] + ln[1] + ln[2])))
            cx[x + 1, at, :] = e
            ln = [lam[k, x, up, :] for k in range(3)]
            f = ty[x, at, :] * m * live[x, up, :]
            d = pp - p[x, up, :]
            for k in range(3):
                flux = f * (0.5 * (la[k] + ln[k])) * d
                fy[k, x, up, :] = flux
                sums[k] = sums[k] + (flux - fy[k, x, at, :])
            e = f * (0.5 * (lt + (ln[0] + ln[1] + ln[2])))
            cy[x, up, :] = e
            ln = [lane_next(v) for v in la]
            f = jnp.where(layer_8 == NZ - 1, 0.0, tz[x, at, :] * m * lane_next(m))
            d = pp - lane_next(pp)
            for k in range(3):
                flux = f * (0.5 * (la[k] + ln[k])) * (d + density[k] * gravity_step)
                net[k, x, at, :] = sums[k] + (flux - lane_prev(flux))
            cz[x, at, :] = f * (0.5 * (lt + (ln[0] + ln[1] + ln[2])))
        e4[3, one, :] = cy[x, pl.ds(CY, 1), :]
        return tuple(tuple(v) for v in below[:3])

    first = tuple(tuple(v[8 * c : 8 * c + 8] for c in range(4)) for v in below[:3])
    half = loop(0, CX // 2, fluxes, first, 4)
    for k in range(1, NGX):
        source = place_y * NGX + lax.rem(place_x + NGX - k, NGX)
        there = wells.at[:, pl.ds(source, 1), :]
        remote(there, there, send_x.at[k], recv_x.at[k], lax.rem(place_x + k, NGX), place_y).wait_recv()
    block = wells.at[:, pl.ds(place_y * NGX, NGX), :]
    for k in range(1, NGY):
        copy = remote(block, block, send_y.at[k], recv_y.at[k], place_x, lax.rem(place_y + k, NGY))
        copy.start()
        sends.append(copy)
    loop(CX // 2, CX, fluxes, half, 4)
    for src, dst in ((net, net_o), (cx, cx_o), (cy, cy_o), (cz, cz_o)):
        give(src, dst)

    zero = jnp.zeros((8, NZ), f32)

    def crossings(x, sums):
        sums = list(sums)
        for c in range(4):
            at = pl.ds(8 * c, 8)
            up = pl.ds(8 * c + 1, 8)
            a = agg[x, at, :]
            for b, e, ok in (
                (agg[x + 1, at, :], cx[x + 1, at, :], x < CX - 1),
                (agg[x, up, :], cy[x, up, :], (row_8 < 7) if c == 3 else None),
            ):
                code = jnp.minimum(a, b) * GROUPS + jnp.maximum(a, b)
                if ok is not None:
                    code = jnp.where(ok, code, -1)
                for n, (g, h) in enumerate(PAIRS):
                    sums[n] = sums[n] + jnp.where(code == g * GROUPS + h, e, 0.0)
            cross = jnp.where(a != lane_next(a), cz[x, at, :], 0.0)
            for n, (g, h) in enumerate(PAIRS):
                if h == g + 1:
                    sums[n] = sums[n] + jnp.where(a == g, cross, 0.0)
        return tuple(sums)

    acc[...] = jnp.zeros_like(acc)
    sums = loop(0, CX, crossings, (zero,) * len(PAIRS), 2)
    for n, (g, h) in enumerate(PAIRS):
        v = line(sums[n])[0]
        acc[h * GROUPS + g, :] = v
        acc[g * GROUPS + h, :] = v

    e4[0] = cx[0]
    e4[1] = cx[CX]
    own4[0] = agg[0, pl.ds(0, CY), :]
    own4[1] = agg[CX - 1, pl.ds(0, CY), :]
    nb4[0] = xlo_i[1]
    nb4[1] = xhi_i[1]
    nb4[2] = ylo_i[1]
    nb4[3] = yhi_i[1]
    give(nb4, nb_o)

    def side(d, _):
        e, a, b = e4[d], own4[d], nb4[d]
        for h in range(GROUPS):
            w = jnp.where(b == h, e, 0.0)
            rows = [line(jnp.where(a == g, w, 0.0)) for g in range(GROUPS)]
            start = pl.multiple_of(((d + 1) * GROUPS + h) * GROUPS, 8)
            acc[pl.ds(start, GROUPS), :] = jnp.concatenate(rows, axis=0)
        return 0

    lax.fori_loop(0, 4, side, 0)
    for n in range(3):
        sums_o[n] = jnp.sum(acc[pl.ds(NZ * n, NZ), :].T, axis=0, keepdims=True)
    for k in range(1, NGY):
        source = lax.rem(place_y + NGY - k, NGY)
        there = wells.at[:, pl.ds(source * NGX, NGX), :]
        remote(there, there, send_y.at[k], recv_y.at[k], place_x, lax.rem(place_y + k, NGY)).wait_recv()
    for copy in sends + faces:
        copy.wait_send()
    for copy in outs:
        copy.wait()


BLK = (CX, CY, NZ)


def exchange(p, ws, gs, act, tx, ty, tz, agg, cells, windex, hole):
    sds = jax.ShapeDtypeStruct
    dma = pltpu.SemaphoreType.DMA
    v = pltpu.VMEM
    face = lambda n, t: v((n, 32, NZ), t)
    return pl.pallas_call(
        exchange_kernel,
        out_shape=[
            sds((3,) + BLK, f32), sds((CX + 1, CY, NZ), f32), sds((CX, CY + 8, NZ), f32), sds(BLK, f32), sds(BLK, f32),
            sds((3, 1, NZ), f32), sds((4, 32, NZ), i32), sds((2, NDEV, NZ), f32),
        ],
        in_specs=[ANY] * 8 + [VMEM, VMEM, SMEM],
        out_specs=[ANY] * 5 + [VMEM, ANY, VMEM],
        scratch_shapes=[
            v((CX + 1, CY + 8, NZ), f32), v(BLK, f32), v(BLK, f32), v(BLK, i32),
            v(BLK, f32), v(BLK, f32), v(BLK, f32), v((CX + 1, CY + 8, NZ), i32),
            face(4, f32), face(2, i32), face(3, f32), face(2, i32), face(4, f32), face(2, i32), face(3, f32), face(2, i32),
            v((3, CX + 1, CY + 8, NZ), f32), v((CX + 1, CY + 8, NZ), f32), v(BLK, f32), v((3,) + BLK, f32),
            v((3, CX, CY + 8, NZ), f32), v((CX + 1, CY, NZ), f32), v((CX, CY + 8, NZ), f32), v(BLK, f32),
            face(10, f32), v((ROWS, NZ), f32), face(4, f32), face(4, i32), face(4, i32),
            dma((8,)), dma((8,)), dma((22,)), dma((22,)), dma((NGX,)), dma((NGX,)), dma((NGY,)), dma((NGY,)),
        ],
        compiler_params=pltpu.CompilerParams(collective_id=0, has_side_effects=True, vmem_limit_bytes=BIG),
        name="exchange",
    )(p, ws, gs, act, tx, ty, tz, agg, cells, windex, hole)


def local_kernel(
    p_h, ws_h, gs_h, old_h, pv_h, act_h, agg_h, mob_h, net_h, cx_h, cy_h, cz_h, nb_h, wells, sums,
    res_o, t_o, dinv_o, sums_o, faces_o, parts_o,
    p, ws, gs, act, agg, old, pv, net, cx, cy, cz, nb4,
    mob, w0, w1, trows, loc, loc_s, s, rem, leak, dinv, res, t, acc, s4,
    sem, out_sem, one_sem,
):
    place_x, place_y = lax.axis_index("gx"), lax.axis_index("gy")
    copies = []

    def fetch(src, dst):
        copy = pltpu.make_async_copy(src, dst, sem.at[len(copies)])
        copy.start()
        copies.append(copy)

    fetch(mob_h, mob)
    fetch(p_h, p)
    early = len(copies)
    for src, dst in (
        (ws_h, ws), (gs_h, gs), (act_h, act), (pv_h, pv), (old_h, old), (net_h, net), (cx_h, cx), (cy_h, cy), (cz_h, cz),
        (agg_h, agg), (nb_h, nb4),
    ):
        fetch(src, dst)

    lane = iota((NDEV, NZ), 1)
    table = wells[0]
    cell = table.astype(i32)
    cell_x, cell_y, layer = cell >> 16, (cell >> 7) & 511, cell & 127
    slot = lane & 31
    here = (slot < PERF) & (cell >= 0) & ((cell_x >> 5) == place_x) & ((cell_y >> 5) == place_y)
    local = ((((cell_x & 31) << 5) + (cell_y & 31)) << 7) + layer
    local = jnp.where(here, local, -1)
    flag = jnp.where(here, 1.0, 0.0).astype(jnp.bfloat16)
    at_in, at_out = iota((NZ, NZ), 0), iota((NZ, NZ), 1)
    pick = ((at_in // 32 == at_out // 32) & (at_out % 32 == 16)) | (at_out == 17)
    counts = jnp.dot(flag, jnp.where(pick, 1.0, 0.0).astype(jnp.bfloat16), preferred_element_type=f32).astype(i32)
    first_layer = pltpu.roll(layer, 18, 1)
    loc[...] = jnp.where(slot < PERF, local, jnp.where(slot == 18, first_layer, counts))
    to_scalar = pltpu.make_async_copy(loc, loc_s, one_sem)
    to_scalar.start()

    w0[...] = jnp.zeros_like(w0)
    w1[...] = jnp.zeros_like(w1)
    trows[...] = jnp.zeros_like(trows)
    for copy in copies[:early]:
        copy.wait()
    to_scalar.wait()

    row_lane = iota((1, NZ), 1)

    def one_row(r, _):
        @pl.when(loc_s[r, 17] > 0)
        def _():
            for j in range(4):

                @pl.when(loc_s[r, 32 * j + 16] > 0)
                def _():
                    shift = loc_s[r, 32 * j + 18] - (32 * j + PERF) + 2 * NZ
                    shift = lax.rem(shift, NZ)
                    index_z = pltpu.roll(wells[0, pl.ds(r, 1), :], shift, 1)
                    hole_z = pltpu.roll(wells[1, pl.ds(r, 1), :], shift, 1)
                    drive_z = index_z * hole_z
                    mob_z = jnp.zeros((1, NZ), f32)
                    press_z = jnp.zeros((1, NZ), f32)
                    for k in range(PERF):
                        at = loc_s[r, 32 * j + k]
                        z = (at & 127) | (at >> 31)
                        q = jnp.maximum(at, 0) >> 7
                        qx, qy = q >> 5, q & 31
                        hit = row_lane == z
                        w0[qx, pl.ds(qy, 1), :] += jnp.where(hit, index_z, 0.0)
                        w1[qx, pl.ds(qy, 1), :] += jnp.where(hit, drive_z, 0.0)
                        mob_z = jnp.where(hit, mob[qx, pl.ds(qy, 1), :], mob_z)
                        press_z = jnp.where(hit, p[qx, pl.ds(qy, 1), :], press_z)
                    well = ((r & (NGX - 1)) * NGY + (r >> 3)) * 4 + j
                    trows[pl.ds(well, 1), :] = index_z * mob_z * (hole_z - press_z)

        return 0

    loop(0, NDEV, one_row, 0, 4)
    total = lax.dot_general(
        jnp.ones((8, NZ), f32), trows[...], (((1,), (1,)), ((), ())), precision=precise, preferred_element_type=f32
    )
    sub = iota((8, NZ), 0)
    parts = jnp.zeros((8, NZ), f32)
    for k in range(NGX):
        piece = total[:, NZ * (k // 2) : NZ * (k // 2) + NZ]
        if k % 2:
            piece = pltpu.roll(piece, 64, 1)
        parts = jnp.where(sub == k, piece, parts)
    parts_o[...] = parts

    for copy in copies[early:]:
        copy.wait()

    def residuals(x, _):
        for c in range(4):
            at = pl.ds(8 * c, 8)
            z = cz[x, at, :]
            diag = (cx[x + 1, at, :] + cx[x, at, :]) + (cy[x, pl.ds(8 * c + 1, 8), :] + cy[x, at, :]) + (z + lane_prev(z))
            pp, m = p[x, at, :], act[x, at, :].astype(f32)
            sw, sg = ws[x, at, :], gs[x, at, :]
            so = 1.0 - sw - sg
            vol = pv[x, at, :]
            wa, wb = w0[x, at, :], w1[x, at, :]
            pull = m * (wb - pp * wa)
            rhs = None
            for k, sat in enumerate((sw, so, sg)):
                held = (1.0 + compress[k] * (pp - 1.0)) * sat
                r = m * (vol * (held - old[k, x, at, :]) + net[k, x, at, :]) - pull * (held * sat * (1.0 / viscosity[k]))
                res[k, x, at, :] = r
                rhs = r if rhs is None else rhs + r
            rhs = -rhs
            store = vol * (compress[0] * sw + compress[1] * so + compress[2] * sg)
            lk = m * store + wa * mob[x, at, :] + dead_leak * (1.0 - m)
            leak[x, at, :] = lk
            diag = diag + lk
            di = relax / diag
            dinv[x, at, :] = di
            sm = rhs * di
            s[x + 1, pl.ds(8 * c + 1, 8), :] = sm
            rem[x, at, :] = rhs - diag * sm
        one = pl.ds(x, 1)
        s4[2, one, :] = s[x + 1, pl.ds(1, 1), :]
        s4[3, one, :] = s[x + 1, pl.ds(CY, 1), :]
        s[x + 1, pl.ds(0, 1), :] = jnp.zeros((1, NZ), f32)
        s[x + 1, pl.ds(CY + 1, 1), :] = jnp.zeros((1, NZ), f32)
        return 0

    loop(0, CX, residuals, 0, 4)
    s4[0] = s[1, pl.ds(1, CY), :]
    s4[1] = s[CX, pl.ds(1, CY), :]
    s[0] = jnp.zeros_like(s[0])
    s[CX + 1] = jnp.zeros_like(s[0])
    outs = []

    def give(src, dst):
        copy = pltpu.make_async_copy(src, dst, out_sem.at[len(outs)])
        copy.start()
        outs.append(copy)

    give(res, res_o)
    give(dinv, dinv_o)
    give(s4, faces_o)

    zero = jnp.zeros((8, NZ), f32)

    def remainders(x, carry):
        lk_sum, re_sum = [list(v) for v in carry]
        for c in range(4):
            at = pl.ds(8 * c, 8)
            up = pl.ds(8 * c + 1, 8)
            here = s[x + 1, up, :]
            z = cz[x, at, :]
            near = cx[x + 1, at, :] * s[x + 2, up, :] + cx[x, at, :] * s[x, up, :]
            near = near + (cy[x, up, :] * s[x + 1, pl.ds(8 * c + 2, 8), :] + cy[x, at, :] * s[x + 1, at, :])
            near = near + (z * lane_next(here) + lane_prev(z * here))
            re = rem[x, at, :] + near
            t[x, at, :] = here + dinv[x, at, :] * re
            lk = leak[x, at, :]
            a = agg[x, at, :]
            for g in range(GROUPS):
                hit = a == g
                re_sum[g] = re_sum[g] + jnp.where(hit, re, 0.0)
                lk_sum[g] = lk_sum[g] + jnp.where(hit, lk, 0.0)
        return tuple(lk_sum), tuple(re_sum)

    lk_sum, re_sum = loop(0, CX, remainders, ((zero,) * GROUPS, (zero,) * GROUPS), 4)
    give(t, t_o)
    rows = [line(v) for v in re_sum]
    acc[...] = jnp.zeros_like(acc)
    for n in range(2):
        coef = (cx[0], cx[CX])[n]
        es = coef * s4[n]
        rows += [line(jnp.where(nb4[n] == g, es, 0.0)) for g in range(GROUPS)]
    e4 = trows
    for x in range(CX):
        e4[pl.ds(x, 1), :] = cy[x, pl.ds(0, 1), :]
        e4[pl.ds(CX + x, 1), :] = cy[x, pl.ds(CY, 1), :]
    for n in range(2):
        es = e4[pl.ds(CX * n, CX), :] * s4[2 + n]
        rows += [line(jnp.where(nb4[2 + n] == g, es, 0.0)) for g in range(GROUPS)]
    rows += [line(v) for v in lk_sum]
    first = RHS_AT - 2 * NZ
    for n in range(6):
        acc[pl.ds(first + 8 * n, 8), :] = jnp.concatenate(rows[8 * n : 8 * n + 8], axis=0)
    sums_o[0] = sums[0]
    sums_o[1] = sums[1]
    sums_o[2] = sums[2] + jnp.sum(acc[...].T, axis=0, keepdims=True)
    for copy in outs:
        copy.wait()


def local(p, ws, gs, old, pv, act, agg, mob, net, cx, cy, cz, nb, wells, sums):
    v = pltpu.VMEM
    sds = jax.ShapeDtypeStruct
    dma = pltpu.SemaphoreType.DMA
    return pl.pallas_call(
        local_kernel,
        out_shape=[
            sds((3,) + BLK, f32), sds(BLK, f32), sds(BLK, f32), sds((3, 1, NZ), f32), sds((4, 32, NZ), f32), sds((8, NZ), f32)
        ],
        in_specs=[ANY] * 13 + [VMEM, VMEM],
        out_specs=[ANY] * 3 + [VMEM, ANY, VMEM],
        scratch_shapes=[
            v(BLK, f32), v(BLK, f32), v(BLK, f32), v(BLK, i32), v(BLK, i32), v((3,) + BLK, f32), v(BLK, f32),
            v((3,) + BLK, f32), v((CX + 1, CY, NZ), f32), v((CX, CY + 8, NZ), f32), v(BLK, f32), v((4, 32, NZ), i32),
            v(BLK, f32), v(BLK, f32), v(BLK, f32), v((4 * NDEV, NZ), f32), v((NDEV, NZ), i32), pltpu.SMEM((NDEV, NZ), i32),
            v((CX + 2, CY + 8, NZ), f32), v(BLK, f32), v(BLK, f32), v(BLK, f32), v((3,) + BLK, f32), v(BLK, f32),
            v((NZ, NZ), f32), v((4, 32, NZ), f32),
            dma((16,)), dma((8,)), dma,
        ],
        compiler_params=pltpu.CompilerParams(vmem_limit_bytes=BIG),
        name="local",
    )(p, ws, gs, old, pv, act, agg, mob, net, cx, cy, cz, nb, wells, sums)


def coarse_kernel(
    sums, parts, faces, t_h, dinv_h, cx_h, cy_h, cz_h, agg_h, nb4,
    update_o, well_o,
    gather, mat, slots, send_rows, rows_x, rows_y, tall, dinv, cx, cy, cz, agg, far, pc,
    sem, send_x, recv_x, send_y, recv_y, psend_x, precv_x, psend_y, precv_y, fsend, frecv,
):
    place_x, place_y = lax.axis_index("gx"), lax.axis_index("gy")
    me = place_y * NGX + place_x
    barrier = pltpu.get_barrier_semaphore()
    greet(barrier)
    loads = []
    body = (slice(None), pl.ds(0, CY), slice(None))
    for src, dst in ((t_h, tall), (dinv_h, dinv), (cx_h, cx), (cy_h, cy), (cz_h, cz), (agg_h, agg)):
        copy = pltpu.make_async_copy(src, dst, sem.at[len(loads)])
        copy.start()
        loads.append(copy)
    for n in range(3):
        gather[n, pl.ds(me, 1), :] = sums[n]
    rows_x[pl.ds(place_x, 1), :] = parts[pl.ds(place_x, 1), :]
    pl.semaphore_wait(barrier, NGX - 1 + NGY - 1)

    sends = []
    own = gather.at[:, pl.ds(me, 1), :]
    for k in range(1, NGX):
        peer = lax.rem(place_x + k, NGX)
        sends.append(remote(own, own, send_x.at[k], recv_x.at[k], peer, place_y))
    for k in range(1, NGX):
        peer = lax.rem(place_x + k, NGX)
        sends.append(
            remote(parts.at[pl.ds(peer, 1), :], rows_x.at[pl.ds(place_x, 1), :], psend_x.at[k], precv_x.at[k], peer, place_y)
        )
    halo = [
        remote(faces.at[1], far.at[0], fsend.at[0], frecv.at[0], lax.rem(place_x + 1, NGX), place_y),
        remote(faces.at[0], far.at[1], fsend.at[1], frecv.at[1], lax.rem(place_x + NGX - 1, NGX), place_y),
        remote(faces.at[3], far.at[2], fsend.at[2], frecv.at[2], place_x, lax.rem(place_y + 1, NGY)),
        remote(faces.at[2], far.at[3], fsend.at[3], frecv.at[3], place_x, lax.rem(place_y + NGY - 1, NGY)),
    ]
    for copy in sends + halo:
        copy.start()
    for k in range(1, NGX):
        source = place_y * NGX + lax.rem(place_x + NGX - k, NGX)
        there = gather.at[:, pl.ds(source, 1), :]
        remote(there, there, send_x.at[k], recv_x.at[k], place_x, place_y).wait_recv()
    block = gather.at[:, pl.ds(place_y * NGX, NGX), :]
    for k in range(1, NGY):
        copy = remote(block, block, send_y.at[k], recv_y.at[k], place_x, lax.rem(place_y + k, NGY))
        copy.start()
        sends.append(copy)
    for k in range(1, NGX):
        source = lax.rem(place_x + NGX - k, NGX)
        there = rows_x.at[pl.ds(source, 1), :]
        remote(there, there, psend_x.at[k], precv_x.at[k], place_x, place_y).wait_recv()
    line = jnp.sum(rows_x[...], axis=0, keepdims=True)
    for k in range(NGY):
        send_rows[k : k + 1, :] = line if k == 0 else pltpu.roll(line, NZ - 4 * k, 1)
    rows_y[pl.ds(place_y, 1), :] = send_rows[pl.ds(place_y, 1), :]
    for k in range(1, NGY):
        peer = lax.rem(place_y + k, NGY)
        copy = remote(
            send_rows.at[pl.ds(peer, 1), :], rows_y.at[pl.ds(place_y, 1), :], psend_y.at[k], precv_y.at[k], place_x, peer
        )
        copy.start()
        sends.append(copy)
    for k in range(1, NGY):
        source = lax.rem(place_y + NGY - k, NGY)
        there = gather.at[:, pl.ds(source * NGX, NGX), :]
        remote(there, there, send_y.at[k], recv_y.at[k], place_x, place_y).wait_recv()

    for n in range(3):
        mat[pl.ds(NZ * n, NZ), :] = gather[n].T
    sub = iota((8, NZ), 0)

    def rows(n):
        return mat[pl.ds(8 * n, 8), :]

    moves = (0, 1, NZ - 1, NGX, NZ - NGX)
    total = jnp.zeros((8, NZ), f32)
    for n in range(5 * GROUPS):
        total = total + rows(n)
    total = total + rows(LEAK_AT // 8)
    for h in range(GROUPS):
        block = rows(h)
        slots[pl.ds(8 * h, 8), :] = jnp.where(sub == h, total, -block)
    for d in range(1, 5):
        for h in range(GROUPS):
            v = -rows(d * GROUPS + h)
            slots[pl.ds((d * GROUPS + h) * 8, 8), :] = pltpu.roll(v, (NZ - moves[d]) % NZ, 1)
    rhs = rows(RHS_AT // 8)
    for d in range(1, 5):
        away = (0, 2, 1, 4, 3)[d]
        rhs = rhs + pltpu.roll(rows(OUT_AT // 8 + away - 1), moves[d], 1)

    def dot(a, b):
        return jnp.sum(jnp.sum(a * b, axis=0, keepdims=True), axis=1, keepdims=True)

    def one_step(_, carry):
        x, r, q, rr = carry
        sums5 = [None] * 5
        for h in range(GROUPS):
            spread = jnp.broadcast_to(q[h : h + 1, :], (8, NZ))
            for d in range(5):
                v = slots[pl.ds((d * GROUPS + h) * 8, 8), :] * spread
                sums5[d] = v if sums5[d] is None else sums5[d] + v
        image = sums5[0]
        for d in range(1, 5):
            image = image + pltpu.roll(sums5[d], moves[d], 1)
        alpha = rr / dot(q, image)
        x = x + alpha * q
        r = r - alpha * image
        new = dot(r, r)
        q = r + (new / rr) * q
        return x, r, q, new

    coarse = loop(0, CITERS, one_step, (jnp.zeros((8, NZ), f32), rhs, rhs, dot(rhs, rhs)), 4)[0]
    mine = iota((8, NZ), 1) == me
    values = []
    for d in range(5):
        v = coarse if d == 0 else pltpu.roll(coarse, moves[d], 1)
        values.append(jnp.sum(jnp.where(mine, v, 0.0), axis=1, keepdims=True))

    def look_up(ids, d):
        v = jnp.broadcast_to(values[d][0:1, :], ids.shape)
        for g in range(1, GROUPS):
            v = jnp.where(ids == g, values[d][g : g + 1, :], v)
        return v

    for copy in halo:
        copy.wait_recv()
    for copy in loads:
        copy.wait()
    pc[0, pl.ds(8, CY), :] = far[0] + look_up(nb4[0], 1)
    pc[CX + 1, pl.ds(8, CY), :] = far[1] + look_up(nb4[1], 2)
    far[2] = far[2] + look_up(nb4[2], 3)
    far[3] = far[3] + look_up(nb4[3], 4)

    def fill(x, _):
        pc[x + 1, pl.ds(8, CY), :] = look_up(agg[x], 0)
        pc[x + 1, pl.ds(7, 1), :] = far[2, pl.ds(x, 1), :]
        pc[x + 1, pl.ds(CY + 8, 1), :] = far[3, pl.ds(x, 1), :]
        return 0

    loop(0, CX, fill, 0, 8)

    def finish(x, _):
        for c in range(4):
            at = pl.ds(8 * c, 8)
            mid = pl.ds(8 * c + 8, 8)
            here = pc[x + 1, mid, :]
            z = cz[x, at, :]
            near = cx[x + 1, at, :] * pc[x + 2, mid, :] + cx[x, at, :] * pc[x, mid, :]
            near = near + (
                cy[x, pl.ds(8 * c + 1, 8), :] * pc[x + 1, pl.ds(8 * c + 9, 8), :]
                + cy[x, at, :] * pc[x + 1, pl.ds(8 * c + 7, 8), :]
            )
            near = near + (z * lane_next(here) + lane_prev(z * here))
            update_o[x, at, :] = tall[x, at, :] + (1.0 - relax) * here + dinv[x, at, :] * near
        return 0

    loop(0, CX, finish, 0, 8)
    for k in range(1, NGY):
        source = lax.rem(place_y + NGY - k, NGY)
        there = rows_y.at[pl.ds(source, 1), :]
        remote(there, there, psend_y.at[k], precv_y.at[k], place_x, place_y).wait_recv()
    well_o[...] = jnp.sum(rows_y[...], axis=0, keepdims=True)
    for copy in sends + halo:
        copy.wait_send()


def coarse_part(sums, parts, faces, t, dinv, cx, cy, cz, agg, nb4):
    v = pltpu.VMEM
    sds = jax.ShapeDtypeStruct
    dma = pltpu.SemaphoreType.DMA
    return pl.pallas_call(
        coarse_kernel,
        out_shape=[sds(BLK, f32), sds((1, NZ), f32)],
        in_specs=[VMEM, VMEM, ANY] + [ANY] * 6 + [VMEM],
        out_specs=[VMEM, VMEM],
        scratch_shapes=[
            v((3, NDEV, NZ), f32), v((ROWS, NZ), f32), v((5 * 64, NZ), f32), v((NGY, NZ), f32), v((NGX, NZ), f32), v((NGY, NZ), f32),
            v(BLK, f32), v(BLK, f32), v((CX + 1, CY, NZ), f32), v((CX, CY + 8, NZ), f32), v(BLK, f32), v(BLK, i32),
            v((4, 32, NZ), f32), v((CX + 2, CY + 16, NZ), f32),
            dma((8,)), dma((NGX,)), dma((NGX,)), dma((NGY,)), dma((NGY,)),
            dma((NGX,)), dma((NGX,)), dma((NGY,)), dma((NGY,)), dma((4,)), dma((4,)),
        ],
        compiler_params=pltpu.CompilerParams(
            collective_id=1, has_side_effects=True, vmem_limit_bytes=BIG
        ),
        name="coarse",
    )(sums, parts, faces, t, dinv, cx, cy, cz, agg, nb4)


def per_device(
    pressure, water_sat, gas_sat, old_content, pore_volume, trans_x, trans_y, trans_z, active, aggregate,
    well_cells, well_index, bottom_hole, well_target,
):
    net, cx, cy, cz, mob, sums, nb, wells = exchange(
        pressure, water_sat, gas_sat, active, trans_x, trans_y, trans_z, aggregate, well_cells, well_index, bottom_hole
    )
    residual, t, dinv, sums, faces, parts = local(
        pressure, water_sat, gas_sat, old_content, pore_volume, active, aggregate, mob, net, cx, cy, cz, nb, wells, sums
    )
    update, well = coarse_part(sums, parts, faces, t, dinv, cx, cy, cz, aggregate, nb)
    return residual, update, well[0, :4] - well_target


def solution(mesh):
    cells = P("gx", "gy", None)
    three = P(None, "gx", "gy", None)
    well, one = P(("gx", "gy"), None), P(("gx", "gy"))
    return jax.shard_map(
        per_device,
        mesh=mesh,
        in_specs=(cells, cells, cells, three) + (cells,) * 6 + (well, well, one, one),
        out_specs=(three, cells, one),
        check_vma=False,
    )
```

```python
import jax
import jax.numpy as jnp
from jax import lax
from jax.experimental import pallas as pl
from jax.experimental.pallas import tpu as pltpu
from jax.sharding import PartitionSpec as P

CX, CY, NZ = 32, 32, 128
PERF = 16
GROUPS = 8
CITERS = 24
NGX, NGY = 8, 16
NDEV = NGX * NGY
ROWS = 384
RHS_AT, OUT_AT, LEAK_AT = 320, 328, 360

precise = lax.Precision.HIGHEST
compress = (0.001, 0.001, 0.005)
viscosity = (0.5, 1.5, 0.2)
density = (1.0, 0.8, 0.2)
gravity_step = 0.05
relax = 0.6
dead_leak = 0.001

BIG = 60 * 1024 * 1024
f32, i32 = jnp.float32, jnp.int32
MESH = pl.DeviceIdType.MESH
ANY = pl.BlockSpec(memory_space=pl.ANY)
VMEM = pl.BlockSpec(memory_space=pltpu.VMEM)
SMEM = pl.BlockSpec(memory_space=pltpu.SMEM)


def iota(shape, dim):
    return lax.broadcasted_iota(i32, shape, dim)


def greet(barrier):
    place_x, place_y = lax.axis_index("gx"), lax.axis_index("gy")
    for k in range(1, NGX):
        pl.semaphore_signal(barrier, inc=1, device_id=(lax.rem(place_x + k, NGX), place_y), device_id_type=MESH)
    for k in range(1, NGY):
        pl.semaphore_signal(barrier, inc=1, device_id=(place_x, lax.rem(place_y + k, NGY)), device_id_type=MESH)


def loop(first, last, body, carry, steps):
    def several(i, carry):
        for n in range(steps):
            carry = body(first + i * steps + n, carry)
        return carry

    return lax.fori_loop(0, (last - first) // steps, several, carry)


def remote(src, dst, send, recv, x, y):
    return pltpu.make_async_remote_copy(
        src_ref=src, dst_ref=dst, send_sem=send, recv_sem=recv, device_id=(x, y), device_id_type=MESH
    )


def mobility_of(p, ws, gs):
    so = 1.0 - ws - gs
    out = []
    for k, s in enumerate((ws, so, gs)):
        out.append((1.0 + compress[k] * (p - 1.0)) * s * s * (1.0 / viscosity[k]))
    return out


def lane_next(v):
    return pltpu.roll(v, NZ - 1, 1)


def lane_prev(v):
    return pltpu.roll(v, 1, 1)


def line(v):
    return jnp.sum(v, axis=0, keepdims=True)


PAIRS = [(a, b) for a in range(GROUPS) for b in range(a + 1, GROUPS)]
BODY = (pl.ds(0, CX), pl.ds(0, CY), slice(None))


def exchange_kernel(
    p_h, ws_h, gs_h, act_h, tx_h, ty_h, tz_h, agg_h, cells, windex, hole,
    net_o, cx_o, cy_o, cz_o, mob_o, sums_o, nb_o, wells,
    p, ws, gs, act, tx, ty, tz, agg, xlo_f, xlo_i, xhi_f, xhi_i, ylo_f, ylo_i, yhi_f, yhi_i,
    lam, live, mob, net, fy, cx, cy, cz, rim, acc, e4, own4, nb4,
    load_sem, out_sem, face_send, face_recv, send_x, recv_x, send_y, recv_y,
):
    place_x, place_y = lax.axis_index("gx"), lax.axis_index("gy")
    me = place_y * NGX + place_x
    barrier = pltpu.get_barrier_semaphore()
    greet(barrier)
    loads = []
    for src, dst in (
        (p_h, p.at[BODY]), (ws_h, ws), (gs_h, gs), (act_h, act), (tx_h, tx), (ty_h, ty), (tz_h, tz), (agg_h, agg.at[BODY])
    ):
        copy = pltpu.make_async_copy(src, dst, load_sem.at[len(loads)])
        copy.start()
        loads.append(copy)
    lane = iota((1, NZ), 1)
    pad = lambda v: jnp.concatenate([v, jnp.zeros((4, NZ - PERF), f32)], axis=1)
    both = pad(cells[...].astype(f32)) + pltpu.roll(pad(windex[...]), PERF, 1)
    row, hole_row = jnp.zeros((1, NZ), f32), jnp.zeros((1, NZ), f32)
    for j in range(4):
        piece = both[j : j + 1]
        if j:
            piece = pltpu.roll(piece, 32 * j, 1)
        row = row + piece
        hole_row = jnp.where(lane // 32 == j, hole[j], hole_row)
    wells[0, pl.ds(me, 1), :] = row
    wells[1, pl.ds(me, 1), :] = hole_row
    pl.semaphore_wait(barrier, NGX - 1 + NGY - 1)

    own = wells.at[:, pl.ds(me, 1), :]
    sends = []
    for k in range(1, NGX):
        sends.append(remote(own, own, send_x.at[k], recv_x.at[k], lax.rem(place_x + k, NGX), place_y))
    up_x, down_x = lax.rem(place_x + 1, NGX), lax.rem(place_x + NGX - 1, NGX)
    up_y, down_y = lax.rem(place_y + 1, NGY), lax.rem(place_y + NGY - 1, NGY)
    faces = []

    def face(src, dst, x, y):
        n = len(faces)
        faces.append(remote(src, dst, face_send.at[n], face_recv.at[n], x, y))

    for n, ref in enumerate((p_h, ws_h, gs_h, tx_h)):
        face(ref.at[CX - 1], xlo_f.at[n], up_x, place_y)
    for n, ref in enumerate((act_h, agg_h)):
        face(ref.at[CX - 1], xlo_i.at[n], up_x, place_y)
    for n, ref in enumerate((p_h, ws_h, gs_h)):
        face(ref.at[0], xhi_f.at[n], down_x, place_y)
    for n, ref in enumerate((act_h, agg_h)):
        face(ref.at[0], xhi_i.at[n], down_x, place_y)
    for n, ref in enumerate((p_h, ws_h, gs_h, ty_h)):
        face(ref.at[:, CY - 1, :], ylo_f.at[n], place_x, up_y)
    for n, ref in enumerate((act_h, agg_h)):
        face(ref.at[:, CY - 1, :], ylo_i.at[n], place_x, up_y)
    for n, ref in enumerate((p_h, ws_h, gs_h)):
        face(ref.at[:, 0, :], yhi_f.at[n], place_x, down_y)
    for n, ref in enumerate((act_h, agg_h)):
        face(ref.at[:, 0, :], yhi_i.at[n], place_x, down_y)
    for copy in sends + faces:
        copy.start()

    for copy in loads[:4]:
        copy.wait()

    def mobilities(x, _):
        parts = mobility_of(p[x, pl.ds(0, CY), :], ws[x], gs[x])
        for k in range(3):
            lam[k, x, pl.ds(0, CY), :] = parts[k]
        m = act[x].astype(f32)
        live[x, pl.ds(0, CY), :] = m
        mob[x] = m * (parts[0] + parts[1] + parts[2])
        none = jnp.zeros((1, NZ), f32)
        for k in range(3):
            lam[k, x, pl.ds(CY, 1), :] = none
            fy[k, x, pl.ds(0, 1), :] = none
        p[x, pl.ds(CY, 1), :] = none
        live[x, pl.ds(CY, 1), :] = none
        agg[x, pl.ds(CY, 1), :] = jnp.zeros((1, NZ), i32)
        cy[x, pl.ds(0, 1), :] = none
        one = pl.ds(x, 1)
        for side, y in ((0, 0), (1, CY - 1)):
            for k in range(3):
                rim[side, k, one, :] = parts[k][y : y + 1]
            rim[side, 3, one, :] = p[x, pl.ds(y, 1), :]
            rim[side, 4, one, :] = m[y : y + 1]
        return 0

    for k in range(3):
        lam[k, CX] = jnp.zeros((CY + 8, NZ), f32)
    p[CX] = jnp.zeros((CY + 8, NZ), f32)
    live[CX] = jnp.zeros((CY + 8, NZ), f32)
    agg[CX] = jnp.zeros((CY + 8, NZ), i32)
    loop(0, CX, mobilities, 0, 8)
    outs = []

    def give(src, dst):
        copy = pltpu.make_async_copy(src, dst, out_sem.at[len(outs)])
        copy.start()
        outs.append(copy)

    give(mob, mob_o)
    for copy in loads[4:]:
        copy.wait()
    layer_8 = iota((8, NZ), 1)
    row_8 = iota((8, NZ), 0)

    def fluxes(x, carry):
        below = [list(v) for v in carry]
        for c in range(4):
            at = pl.ds(8 * c, 8)
            up = pl.ds(8 * c + 1, 8)
            pp, m = p[x, at, :], live[x, at, :]
            la = [lam[k, x, at, :] for k in range(3)]
            lt = la[0] + la[1] + la[2]
            sums = []
            ln = [lam[k, x + 1, at, :] for k in range(3)]
            f = tx[x, at, :] * m * live[x + 1, at, :]
            d = pp - p[x + 1, at, :]
            for k in range(3):
                flux = f * (0.5 * (la[k] + ln[k])) * d
                sums.append(flux - below[k][c])
                below[k][c] = flux
            e = f * (0.5 * (lt + (ln[0] + ln[1] + ln[2])))
            cx[x + 1, at, :] = e
            ln = [lam[k, x, up, :] for k in range(3)]
            f = ty[x, at, :] * m * live[x, up, :]
            d = pp - p[x, up, :]
            for k in range(3):
                flux = f * (0.5 * (la[k] + ln[k])) * d
                fy[k, x, up, :] = flux
                sums[k] = sums[k] + (flux - fy[k, x, at, :])
            e = f * (0.5 * (lt + (ln[0] + ln[1] + ln[2])))
            cy[x, up, :] = e
            ln = [lane_next(v) for v in la]
            f = jnp.where(layer_8 == NZ - 1, 0.0, tz[x, at, :] * m * lane_next(m))
            d = pp - lane_next(pp)
            for k in range(3):
                flux = f * (0.5 * (la[k] + ln[k])) * (d + density[k] * gravity_step)
                net[k, x, at, :] = sums[k] + (flux - lane_prev(flux))
            cz[x, at, :] = f * (0.5 * (lt + (ln[0] + ln[1] + ln[2])))
        return tuple(tuple(v) for v in below[:3])

    zero = jnp.zeros((8, NZ), f32)
    first = ((zero,) * 4,) * 3
    half = loop(0, CX // 2, fluxes, first, 4)
    for k in range(1, NGX):
        source = place_y * NGX + lax.rem(place_x + NGX - k, NGX)
        there = wells.at[:, pl.ds(source, 1), :]
        remote(there, there, send_x.at[k], recv_x.at[k], lax.rem(place_x + k, NGX), place_y).wait_recv()
    block = wells.at[:, pl.ds(place_y * NGX, NGX), :]
    for k in range(1, NGY):
        copy = remote(block, block, send_y.at[k], recv_y.at[k], place_x, lax.rem(place_y + k, NGY))
        copy.start()
        sends.append(copy)
    loop(CX // 2, CX, fluxes, half, 4)
    give(cz, cz_o)
    for copy in faces:
        copy.wait_recv()

    def face_flux(f, low, high):
        e = f * (0.5 * ((low[0] + low[1] + low[2]) + (high[0] + high[1] + high[2])))
        return [f * (0.5 * (low[k] + high[k])) * (low[3] - high[3]) for k in range(3)], e

    live_at = lambda ids, flag: ids.astype(f32) * jnp.where(flag, 0.0, 1.0)
    body = pl.ds(0, CY)
    low = mobility_of(xlo_f[0], xlo_f[1], xlo_f[2]) + [xlo_f[0]]
    high = [lam[k, 0, body, :] for k in range(3)] + [p[0, body, :]]
    flux, e = face_flux(xlo_f[3] * live_at(xlo_i[0], place_x == 0) * live[0, body, :], low, high)
    for k in range(3):
        net[k, 0] = net[k, 0] - flux[k]
    cx[0] = e
    e4[0] = e
    low = [lam[k, CX - 1, body, :] for k in range(3)] + [p[CX - 1, body, :]]
    high = mobility_of(xhi_f[0], xhi_f[1], xhi_f[2]) + [xhi_f[0]]
    flux, e = face_flux(tx[CX - 1] * live[CX - 1, body, :] * live_at(xhi_i[0], place_x == NGX - 1), low, high)
    for k in range(3):
        net[k, CX - 1] = net[k, CX - 1] + flux[k]
    cx[CX] = e
    e4[1] = e
    low = mobility_of(ylo_f[0], ylo_f[1], ylo_f[2]) + [ylo_f[0]]
    high = [rim[0, k] for k in range(4)]
    flux_low, e = face_flux(ylo_f[3] * live_at(ylo_i[0], place_y == 0) * rim[0, 4], low, high)
    e4[2] = e
    low = [rim[1, k] for k in range(4)]
    high = mobility_of(yhi_f[0], yhi_f[1], yhi_f[2]) + [yhi_f[0]]
    for x in range(CX):
        rim[0, 0, pl.ds(x, 1), :] = ty[x, pl.ds(CY - 1, 1), :]
    flux_high, e = face_flux(rim[0, 0] * rim[1, 4] * live_at(yhi_i[0], place_y == NGY - 1), low, high)
    e4[3] = e
    for x in range(CX):
        one = slice(x, x + 1)
        first_row, last_row = pl.ds(0, 1), pl.ds(CY - 1, 1)
        for k in range(3):
            net[k, x, first_row, :] = net[k, x, first_row, :] - flux_low[k][one]
            net[k, x, last_row, :] = net[k, x, last_row, :] + flux_high[k][one]
        cy[x, first_row, :] = e4[2, pl.ds(x, 1), :]
        cy[x, pl.ds(CY, 1), :] = e[one]
        own4[2, pl.ds(x, 1), :] = agg[x, first_row, :]
        own4[3, pl.ds(x, 1), :] = agg[x, last_row, :]
    for src, dst in ((net, net_o), (cx, cx_o), (cy, cy_o)):
        give(src, dst)

    def crossings(x, sums):
        sums = list(sums)
        for c in range(4):
            at = pl.ds(8 * c, 8)
            up = pl.ds(8 * c + 1, 8)
            a = agg[x, at, :]
            for b, e, ok in (
                (agg[x + 1, at, :], cx[x + 1, at, :], x < CX - 1),
                (agg[x, up, :], cy[x, up, :], (row_8 < 7) if c == 3 else None),
            ):
                code = jnp.minimum(a, b) * GROUPS + jnp.maximum(a, b)
                if ok is not None:
                    code = jnp.where(ok, code, -1)
                for n, (g, h) in enumerate(PAIRS):
                    sums[n] = sums[n] + jnp.where(code == g * GROUPS + h, e, 0.0)
            cross = jnp.where(a != lane_next(a), cz[x, at, :], 0.0)
            for n, (g, h) in enumerate(PAIRS):
                if h == g + 1:
                    sums[n] = sums[n] + jnp.where(a == g, cross, 0.0)
        return tuple(sums)

    acc[...] = jnp.zeros_like(acc)
    sums = loop(0, CX, crossings, (zero,) * len(PAIRS), 2)
    for n, (g, h) in enumerate(PAIRS):
        v = line(sums[n])[0]
        acc[h * GROUPS + g, :] = v
        acc[g * GROUPS + h, :] = v

    own4[0] = agg[0, pl.ds(0, CY), :]
    own4[1] = agg[CX - 1, pl.ds(0, CY), :]
    nb4[0] = xlo_i[1]
    nb4[1] = xhi_i[1]
    nb4[2] = ylo_i[1]
    nb4[3] = yhi_i[1]
    give(nb4, nb_o)

    def side(d, _):
        e, a, b = e4[d], own4[d], nb4[d]
        for h in range(GROUPS):
            w = jnp.where(b == h, e, 0.0)
            rows = [line(jnp.where(a == g, w, 0.0)) for g in range(GROUPS)]
            start = pl.multiple_of(((d + 1) * GROUPS + h) * GROUPS, 8)
            acc[pl.ds(start, GROUPS), :] = jnp.concatenate(rows, axis=0)
        return 0

    lax.fori_loop(0, 4, side, 0)
    for n in range(3):
        sums_o[n] = jnp.sum(acc[pl.ds(NZ * n, NZ), :].T, axis=0, keepdims=True)
    for k in range(1, NGY):
        source = lax.rem(place_y + NGY - k, NGY)
        there = wells.at[:, pl.ds(source * NGX, NGX), :]
        remote(there, there, send_y.at[k], recv_y.at[k], place_x, lax.rem(place_y + k, NGY)).wait_recv()
    for copy in sends + faces:
        copy.wait_send()
    for copy in outs:
        copy.wait()


BLK = (CX, CY, NZ)


def exchange(p, ws, gs, act, tx, ty, tz, agg, cells, windex, hole):
    sds = jax.ShapeDtypeStruct
    dma = pltpu.SemaphoreType.DMA
    v = pltpu.VMEM
    face = lambda n, t: v((n, 32, NZ), t)
    return pl.pallas_call(
        exchange_kernel,
        out_shape=[
            sds((3,) + BLK, f32), sds((CX + 1, CY, NZ), f32), sds((CX, CY + 8, NZ), f32), sds(BLK, f32), sds(BLK, f32),
            sds((3, 1, NZ), f32), sds((4, 32, NZ), i32), sds((2, NDEV, NZ), f32),
        ],
        in_specs=[ANY] * 8 + [VMEM, VMEM, SMEM],
        out_specs=[ANY] * 5 + [VMEM, ANY, VMEM],
        scratch_shapes=[
            v((CX + 1, CY + 8, NZ), f32), v(BLK, f32), v(BLK, f32), v(BLK, i32),
            v(BLK, f32), v(BLK, f32), v(BLK, f32), v((CX + 1, CY + 8, NZ), i32),
            face(4, f32), face(2, i32), face(3, f32), face(2, i32), face(4, f32), face(2, i32), face(3, f32), face(2, i32),
            v((3, CX + 1, CY + 8, NZ), f32), v((CX + 1, CY + 8, NZ), f32), v(BLK, f32), v((3,) + BLK, f32),
            v((3, CX, CY + 8, NZ), f32), v((CX + 1, CY, NZ), f32), v((CX, CY + 8, NZ), f32), v(BLK, f32),
            v((2, 5, 32, NZ), f32), v((ROWS, NZ), f32), face(4, f32), face(4, i32), face(4, i32),
            dma((8,)), dma((8,)), dma((22,)), dma((22,)), dma((NGX,)), dma((NGX,)), dma((NGY,)), dma((NGY,)),
        ],
        compiler_params=pltpu.CompilerParams(collective_id=0, has_side_effects=True, vmem_limit_bytes=BIG),
        name="exchange",
    )(p, ws, gs, act, tx, ty, tz, agg, cells, windex, hole)


def local_kernel(
    p_h, ws_h, gs_h, old_h, pv_h, act_h, agg_h, mob_h, net_h, cx_h, cy_h, cz_h, nb_h, wells, sums,
    res_o, t_o, dinv_o, sums_o, faces_o, parts_o,
    p, ws, gs, act, agg, old, pv, net, cx, cy, cz, nb4,
    mob, w0, w1, trows, loc, cols, loc_s, s, rem, leak, dinv, res, t, acc, s4,
    sem, out_sem, one_sem,
):
    place_x, place_y = lax.axis_index("gx"), lax.axis_index("gy")
    copies = []

    def fetch(src, dst):
        copy = pltpu.make_async_copy(src, dst, sem.at[len(copies)])
        copy.start()
        copies.append(copy)

    fetch(mob_h, mob)
    fetch(p_h, p)
    early = len(copies)
    for src, dst in (
        (ws_h, ws), (gs_h, gs), (act_h, act), (pv_h, pv), (old_h, old), (net_h, net), (cx_h, cx), (cy_h, cy), (cz_h, cz),
        (agg_h, agg), (nb_h, nb4),
    ):
        fetch(src, dst)

    lane = iota((NDEV, NZ), 1)
    table = wells[0]
    cell = table.astype(i32)
    cell_x, cell_y, layer = cell >> 16, (cell >> 7) & 511, cell & 127
    slot = lane & 31
    here = (slot < PERF) & (cell >= 0) & ((cell_x >> 5) == place_x) & ((cell_y >> 5) == place_y)
    local = ((((cell_x & 31) << 5) + (cell_y & 31)) << 7) + layer
    local = jnp.where(here, local, -1)
    flag = jnp.where(here, 1.0, 0.0).astype(jnp.bfloat16)
    at_in, at_out = iota((NZ, NZ), 0), iota((NZ, NZ), 1)
    pick = ((at_in // 32 == at_out // 32) & (at_out % 32 == 16)) | (at_out == 17)
    counts = jnp.dot(flag, jnp.where(pick, 1.0, 0.0).astype(jnp.bfloat16), preferred_element_type=f32).astype(i32)
    first_layer = pltpu.roll(layer, 18, 1)
    cols[...] = jnp.where(here, local >> 7, -1)
    loc[...] = jnp.where(slot < PERF, local, jnp.where(slot == 18, first_layer, counts))
    to_scalar = pltpu.make_async_copy(loc, loc_s, one_sem)
    to_scalar.start()

    w0[...] = jnp.zeros_like(w0)
    w1[...] = jnp.zeros_like(w1)
    trows[...] = jnp.zeros_like(trows)
    for copy in copies[:early]:
        copy.wait()
    to_scalar.wait()

    row_lane = iota((1, NZ), 1)

    def one_row(r, _):
        @pl.when(loc_s[r, 17] > 0)
        def _():
            for j in range(4):

                @pl.when(loc_s[r, 32 * j + 16] > 0)
                def _():
                    top = loc_s[r, 32 * j + 18]
                    shift = lax.rem(top - (32 * j + PERF) + 2 * NZ, NZ)
                    index_z = pltpu.roll(wells[0, pl.ds(r, 1), :], shift, 1)
                    hole_z = pltpu.roll(wells[1, pl.ds(r, 1), :], shift, 1)
                    column_z = pltpu.roll(cols[pl.ds(r, 1), :], lax.rem(top - 32 * j + NZ, NZ), 1)
                    column_z = jnp.where((row_lane >= top) & (row_lane < top + PERF), column_z, -1)
                    drive_z = index_z * hole_z
                    mob_z = jnp.zeros((1, NZ), f32)
                    press_z = jnp.zeros((1, NZ), f32)
                    stores = []
                    for k in range(PERF):
                        q = jnp.maximum(loc_s[r, 32 * j + k], 0) >> 7
                        qx, qy = q >> 5, pl.ds(q & 31, 1)
                        hit = column_z == q
                        stores.append((
                            qx, qy, w0[qx, qy, :] + jnp.where(hit, index_z, 0.0), w1[qx, qy, :] + jnp.where(hit, drive_z, 0.0)
                        ))
                        mob_z = jnp.where(hit, mob[qx, qy, :], mob_z)
                        press_z = jnp.where(hit, p[qx, qy, :], press_z)
                    for qx, qy, sum0, sum1 in stores:
                        w0[qx, qy, :] = sum0
                        w1[qx, qy, :] = sum1
                    well = ((r & (NGX - 1)) * NGY + (r >> 3)) * 4 + j
                    trows[pl.ds(well, 1), :] = index_z * mob_z * (hole_z - press_z)

        return 0

    loop(0, NDEV, one_row, 0, 4)
    total = lax.dot_general(
        jnp.ones((8, NZ), f32), trows[...], (((1,), (1,)), ((), ())), precision=precise, preferred_element_type=f32
    )
    sub = iota((8, NZ), 0)
    parts = jnp.zeros((8, NZ), f32)
    for k in range(NGX):
        piece = total[:, NZ * (k // 2) : NZ * (k // 2) + NZ]
        if k % 2:
            piece = pltpu.roll(piece, 64, 1)
        parts = jnp.where(sub == k, piece, parts)
    parts_o[...] = parts

    for copy in copies[early:]:
        copy.wait()

    def residuals(x, _):
        for c in range(4):
            at = pl.ds(8 * c, 8)
            z = cz[x, at, :]
            diag = (cx[x + 1, at, :] + cx[x, at, :]) + (cy[x, pl.ds(8 * c + 1, 8), :] + cy[x, at, :]) + (z + lane_prev(z))
            pp, m = p[x, at, :], act[x, at, :].astype(f32)
            sw, sg = ws[x, at, :], gs[x, at, :]
            so = 1.0 - sw - sg
            vol = pv[x, at, :]
            wa, wb = w0[x, at, :], w1[x, at, :]
            pull = m * (wb - pp * wa)
            rhs = None
            for k, sat in enumerate((sw, so, sg)):
                held = (1.0 + compress[k] * (pp - 1.0)) * sat
                r = m * (vol * (held - old[k, x, at, :]) + net[k, x, at, :]) - pull * (held * sat * (1.0 / viscosity[k]))
                res[k, x, at, :] = r
                rhs = r if rhs is None else rhs + r
            rhs = -rhs
            store = vol * (compress[0] * sw + compress[1] * so + compress[2] * sg)
            lk = m * store + wa * mob[x, at, :] + dead_leak * (1.0 - m)
            leak[x, at, :] = lk
            diag = diag + lk
            di = relax / diag
            dinv[x, at, :] = di
            sm = rhs * di
            s[x + 1, pl.ds(8 * c + 1, 8), :] = sm
            rem[x, at, :] = rhs - diag * sm
        one = pl.ds(x, 1)
        s4[2, one, :] = s[x + 1, pl.ds(1, 1), :]
        s4[3, one, :] = s[x + 1, pl.ds(CY, 1), :]
        s[x + 1, pl.ds(0, 1), :] = jnp.zeros((1, NZ), f32)
        s[x + 1, pl.ds(CY + 1, 1), :] = jnp.zeros((1, NZ), f32)
        return 0

    loop(0, CX, residuals, 0, 4)
    s4[0] = s[1, pl.ds(1, CY), :]
    s4[1] = s[CX, pl.ds(1, CY), :]
    s[0] = jnp.zeros_like(s[0])
    s[CX + 1] = jnp.zeros_like(s[0])
    outs = []

    def give(src, dst):
        copy = pltpu.make_async_copy(src, dst, out_sem.at[len(outs)])
        copy.start()
        outs.append(copy)

    give(res, res_o)
    give(dinv, dinv_o)
    give(s4, faces_o)

    zero = jnp.zeros((8, NZ), f32)

    def remainders(x, carry):
        lk_sum, re_sum = [list(v) for v in carry]
        for c in range(4):
            at = pl.ds(8 * c, 8)
            up = pl.ds(8 * c + 1, 8)
            here = s[x + 1, up, :]
            z = cz[x, at, :]
            near = cx[x + 1, at, :] * s[x + 2, up, :] + cx[x, at, :] * s[x, up, :]
            near = near + (cy[x, up, :] * s[x + 1, pl.ds(8 * c + 2, 8), :] + cy[x, at, :] * s[x + 1, at, :])
            near = near + (z * lane_next(here) + lane_prev(z * here))
            re = rem[x, at, :] + near
            t[x, at, :] = here + dinv[x, at, :] * re
            lk = leak[x, at, :]
            a = agg[x, at, :]
            for g in range(GROUPS):
                hit = a == g
                re_sum[g] = re_sum[g] + jnp.where(hit, re, 0.0)
                lk_sum[g] = lk_sum[g] + jnp.where(hit, lk, 0.0)
        return tuple(lk_sum), tuple(re_sum)

    lk_sum, re_sum = loop(0, CX, remainders, ((zero,) * GROUPS, (zero,) * GROUPS), 4)
    give(t, t_o)
    rows = [line(v) for v in re_sum]
    acc[...] = jnp.zeros_like(acc)
    for n in range(2):
        coef = (cx[0], cx[CX])[n]
        es = coef * s4[n]
        rows += [line(jnp.where(nb4[n] == g, es, 0.0)) for g in range(GROUPS)]
    e4 = trows
    for x in range(CX):
        e4[pl.ds(x, 1), :] = cy[x, pl.ds(0, 1), :]
        e4[pl.ds(CX + x, 1), :] = cy[x, pl.ds(CY, 1), :]
    for n in range(2):
        es = e4[pl.ds(CX * n, CX), :] * s4[2 + n]
        rows += [line(jnp.where(nb4[2 + n] == g, es, 0.0)) for g in range(GROUPS)]
    rows += [line(v) for v in lk_sum]
    first = RHS_AT - 2 * NZ
    for n in range(6):
        acc[pl.ds(first + 8 * n, 8), :] = jnp.concatenate(rows[8 * n : 8 * n + 8], axis=0)
    sums_o[0] = sums[0]
    sums_o[1] = sums[1]
    sums_o[2] = sums[2] + jnp.sum(acc[...].T, axis=0, keepdims=True)
    for copy in outs:
        copy.wait()


def local(p, ws, gs, old, pv, act, agg, mob, net, cx, cy, cz, nb, wells, sums):
    v = pltpu.VMEM
    sds = jax.ShapeDtypeStruct
    dma = pltpu.SemaphoreType.DMA
    return pl.pallas_call(
        local_kernel,
        out_shape=[
            sds((3,) + BLK, f32), sds(BLK, f32), sds(BLK, f32), sds((3, 1, NZ), f32), sds((4, 32, NZ), f32), sds((8, NZ), f32)
        ],
        in_specs=[ANY] * 13 + [VMEM, VMEM],
        out_specs=[ANY] * 3 + [VMEM, ANY, VMEM],
        scratch_shapes=[
            v(BLK, f32), v(BLK, f32), v(BLK, f32), v(BLK, i32), v(BLK, i32), v((3,) + BLK, f32), v(BLK, f32),
            v((3,) + BLK, f32), v((CX + 1, CY, NZ), f32), v((CX, CY + 8, NZ), f32), v(BLK, f32), v((4, 32, NZ), i32),
            v(BLK, f32), v(BLK, f32), v(BLK, f32), v((4 * NDEV, NZ), f32), v((NDEV, NZ), i32), v((NDEV, NZ), i32), pltpu.SMEM((NDEV, NZ), i32),
            v((CX + 2, CY + 8, NZ), f32), v(BLK, f32), v(BLK, f32), v(BLK, f32), v((3,) + BLK, f32), v(BLK, f32),
            v((NZ, NZ), f32), v((4, 32, NZ), f32),
            dma((16,)), dma((8,)), dma,
        ],
        compiler_params=pltpu.CompilerParams(vmem_limit_bytes=BIG),
        name="local",
    )(p, ws, gs, old, pv, act, agg, mob, net, cx, cy, cz, nb, wells, sums)


def coarse_kernel(
    sums, parts, faces, t_h, dinv_h, cx_h, cy_h, cz_h, agg_h, nb4,
    update_o, well_o,
    gather, mat, slots, send_rows, rows_x, rows_y, tall, dinv, cx, cy, cz, agg, far, pc,
    sem, send_x, recv_x, send_y, recv_y, psend_x, precv_x, psend_y, precv_y, fsend, frecv,
):
    place_x, place_y = lax.axis_index("gx"), lax.axis_index("gy")
    me = place_y * NGX + place_x
    barrier = pltpu.get_barrier_semaphore()
    greet(barrier)
    loads = []
    body = (slice(None), pl.ds(0, CY), slice(None))
    for src, dst in ((t_h, tall), (dinv_h, dinv), (cx_h, cx), (cy_h, cy), (cz_h, cz), (agg_h, agg)):
        copy = pltpu.make_async_copy(src, dst, sem.at[len(loads)])
        copy.start()
        loads.append(copy)
    for n in range(3):
        gather[n, pl.ds(me, 1), :] = sums[n]
    rows_x[pl.ds(place_x, 1), :] = parts[pl.ds(place_x, 1), :]
    pl.semaphore_wait(barrier, NGX - 1 + NGY - 1)

    sends = []
    own = gather.at[:, pl.ds(me, 1), :]
    for k in range(1, NGX):
        peer = lax.rem(place_x + k, NGX)
        sends.append(remote(own, own, send_x.at[k], recv_x.at[k], peer, place_y))
    for k in range(1, NGX):
        peer = lax.rem(place_x + k, NGX)
        sends.append(
            remote(parts.at[pl.ds(peer, 1), :], rows_x.at[pl.ds(place_x, 1), :], psend_x.at[k], precv_x.at[k], peer, place_y)
        )
    halo = [
        remote(faces.at[1], far.at[0], fsend.at[0], frecv.at[0], lax.rem(place_x + 1, NGX), place_y),
        remote(faces.at[0], far.at[1], fsend.at[1], frecv.at[1], lax.rem(place_x + NGX - 1, NGX), place_y),
        remote(faces.at[3], far.at[2], fsend.at[2], frecv.at[2], place_x, lax.rem(place_y + 1, NGY)),
        remote(faces.at[2], far.at[3], fsend.at[3], frecv.at[3], place_x, lax.rem(place_y + NGY - 1, NGY)),
    ]
    for copy in sends + halo:
        copy.start()
    for k in range(1, NGX):
        source = place_y * NGX + lax.rem(place_x + NGX - k, NGX)
        there = gather.at[:, pl.ds(source, 1), :]
        remote(there, there, send_x.at[k], recv_x.at[k], place_x, place_y).wait_recv()
    block = gather.at[:, pl.ds(place_y * NGX, NGX), :]
    for k in range(1, NGY):
        copy = remote(block, block, send_y.at[k], recv_y.at[k], place_x, lax.rem(place_y + k, NGY))
        copy.start()
        sends.append(copy)
    for k in range(1, NGX):
        source = lax.rem(place_x + NGX - k, NGX)
        there = rows_x.at[pl.ds(source, 1), :]
        remote(there, there, psend_x.at[k], precv_x.at[k], place_x, place_y).wait_recv()
    line = jnp.sum(rows_x[...], axis=0, keepdims=True)
    for k in range(NGY):
        send_rows[k : k + 1, :] = line if k == 0 else pltpu.roll(line, NZ - 4 * k, 1)
    rows_y[pl.ds(place_y, 1), :] = send_rows[pl.ds(place_y, 1), :]
    for k in range(1, NGY):
        peer = lax.rem(place_y + k, NGY)
        copy = remote(
            send_rows.at[pl.ds(peer, 1), :], rows_y.at[pl.ds(place_y, 1), :], psend_y.at[k], precv_y.at[k], place_x, peer
        )
        copy.start()
        sends.append(copy)
    for k in range(1, NGY):
        source = lax.rem(place_y + NGY - k, NGY)
        there = gather.at[:, pl.ds(source * NGX, NGX), :]
        remote(there, there, send_y.at[k], recv_y.at[k], place_x, place_y).wait_recv()

    for n in range(3):
        mat[pl.ds(NZ * n, NZ), :] = gather[n].T
    sub = iota((8, NZ), 0)

    def rows(n):
        return mat[pl.ds(8 * n, 8), :]

    moves = (0, 1, NZ - 1, NGX, NZ - NGX)
    total = jnp.zeros((8, NZ), f32)
    for n in range(5 * GROUPS):
        total = total + rows(n)
    total = total + rows(LEAK_AT // 8)
    for h in range(GROUPS):
        block = rows(h)
        slots[pl.ds(8 * h, 8), :] = jnp.where(sub == h, total, -block)
    for d in range(1, 5):
        for h in range(GROUPS):
            v = -rows(d * GROUPS + h)
            slots[pl.ds((d * GROUPS + h) * 8, 8), :] = pltpu.roll(v, (NZ - moves[d]) % NZ, 1)
    rhs = rows(RHS_AT // 8)
    for d in range(1, 5):
        away = (0, 2, 1, 4, 3)[d]
        rhs = rhs + pltpu.roll(rows(OUT_AT // 8 + away - 1), moves[d], 1)

    def dot(a, b):
        return jnp.sum(jnp.sum(a * b, axis=0, keepdims=True), axis=1, keepdims=True)

    def tree(values):
        while len(values) > 1:
            values = [a + b for a, b in zip(values[::2], values[1::2])] + values[len(values) // 2 * 2 :]
        return values[0]

    def image(v):
        spread = [jnp.broadcast_to(v[h : h + 1, :], (8, NZ)) for h in range(GROUPS)]
        sides = [tree([slots[pl.ds((d * GROUPS + h) * 8, 8), :] * spread[h] for h in range(GROUPS)]) for d in range(5)]
        return tree([pltpu.roll(sides[d], moves[d], 1) for d in range(1, 5)]) + sides[0]

    w = image(rhs)
    norm = dot(rhs, rhs)
    alpha = norm / dot(w, rhs)

    def one_step(_, carry):
        x, r, q, aq, norm, alpha = carry
        x = x + alpha * q
        r = r - alpha * aq
        new = dot(r, r)
        w = image(r)
        curve = dot(w, r)
        beta = new / norm
        alpha = new / (curve - beta * (new / alpha))
        return x, r, r + beta * q, w + beta * aq, new, alpha

    start = (jnp.zeros((8, NZ), f32), rhs, rhs, w, norm, alpha)
    x, _, q, _, _, alpha = loop(0, CITERS - 1, one_step, start, 1)
    coarse = x + alpha * q
    mine = iota((8, NZ), 1) == me
    values = []
    for d in range(5):
        v = coarse if d == 0 else pltpu.roll(coarse, moves[d], 1)
        values.append(jnp.sum(jnp.where(mine, v, 0.0), axis=1, keepdims=True))

    def look_up(ids, d):
        v = jnp.broadcast_to(values[d][0:1, :], ids.shape)
        for g in range(1, GROUPS):
            v = jnp.where(ids == g, values[d][g : g + 1, :], v)
        return v

    for copy in halo:
        copy.wait_recv()
    for copy in loads:
        copy.wait()
    pc[0, pl.ds(8, CY), :] = far[0] + look_up(nb4[0], 1)
    pc[CX + 1, pl.ds(8, CY), :] = far[1] + look_up(nb4[1], 2)
    far[2] = far[2] + look_up(nb4[2], 3)
    far[3] = far[3] + look_up(nb4[3], 4)

    def fill(x, _):
        pc[x + 1, pl.ds(8, CY), :] = look_up(agg[x], 0)
        pc[x + 1, pl.ds(7, 1), :] = far[2, pl.ds(x, 1), :]
        pc[x + 1, pl.ds(CY + 8, 1), :] = far[3, pl.ds(x, 1), :]
        return 0

    loop(0, CX, fill, 0, 8)

    def finish(x, _):
        for c in range(4):
            at = pl.ds(8 * c, 8)
            mid = pl.ds(8 * c + 8, 8)
            here = pc[x + 1, mid, :]
            z = cz[x, at, :]
            near = cx[x + 1, at, :] * pc[x + 2, mid, :] + cx[x, at, :] * pc[x, mid, :]
            near = near + (
                cy[x, pl.ds(8 * c + 1, 8), :] * pc[x + 1, pl.ds(8 * c + 9, 8), :]
                + cy[x, at, :] * pc[x + 1, pl.ds(8 * c + 7, 8), :]
            )
            near = near + (z * lane_next(here) + lane_prev(z * here))
            update_o[x, at, :] = tall[x, at, :] + (1.0 - relax) * here + dinv[x, at, :] * near
        return 0

    loop(0, CX, finish, 0, 8)
    for k in range(1, NGY):
        source = lax.rem(place_y + NGY - k, NGY)
        there = rows_y.at[pl.ds(source, 1), :]
        remote(there, there, psend_y.at[k], precv_y.at[k], place_x, place_y).wait_recv()
    well_o[...] = jnp.sum(rows_y[...], axis=0, keepdims=True)
    for copy in sends + halo:
        copy.wait_send()


def coarse_part(sums, parts, faces, t, dinv, cx, cy, cz, agg, nb4):
    v = pltpu.VMEM
    sds = jax.ShapeDtypeStruct
    dma = pltpu.SemaphoreType.DMA
    return pl.pallas_call(
        coarse_kernel,
        out_shape=[sds(BLK, f32), sds((1, NZ), f32)],
        in_specs=[VMEM, VMEM, ANY] + [ANY] * 6 + [VMEM],
        out_specs=[VMEM, VMEM],
        scratch_shapes=[
            v((3, NDEV, NZ), f32), v((ROWS, NZ), f32), v((5 * 64, NZ), f32), v((NGY, NZ), f32), v((NGX, NZ), f32), v((NGY, NZ), f32),
            v(BLK, f32), v(BLK, f32), v((CX + 1, CY, NZ), f32), v((CX, CY + 8, NZ), f32), v(BLK, f32), v(BLK, i32),
            v((4, 32, NZ), f32), v((CX + 2, CY + 16, NZ), f32),
            dma((8,)), dma((NGX,)), dma((NGX,)), dma((NGY,)), dma((NGY,)),
            dma((NGX,)), dma((NGX,)), dma((NGY,)), dma((NGY,)), dma((4,)), dma((4,)),
        ],
        compiler_params=pltpu.CompilerParams(
            collective_id=1, has_side_effects=True, vmem_limit_bytes=BIG
        ),
        name="coarse",
    )(sums, parts, faces, t, dinv, cx, cy, cz, agg, nb4)


def last_kernel(update_h, well, target, update_o, well_o, held, sem_in, sem_out):
    part = CX // 4
    moves = []
    for n in range(4):
        at = pl.ds(part * n, part)
        copy = pltpu.make_async_copy(update_h.at[at], held.at[at], sem_in.at[n])
        copy.start()
        moves.append((copy, pltpu.make_async_copy(held.at[at], update_o.at[at], sem_out.at[n])))
    for j in range(4):
        well_o[j] = well[0, j] - target[j]
    for arrive, leave in moves:
        arrive.wait()
        leave.start()
    for _, leave in moves:
        leave.wait()


def last_part(update, well, target):
    sds = jax.ShapeDtypeStruct
    return pl.pallas_call(
        last_kernel,
        out_shape=[sds(BLK, f32), sds((4,), f32)],
        in_specs=[ANY, SMEM, SMEM],
        out_specs=[ANY, SMEM],
        scratch_shapes=[pltpu.VMEM(BLK, f32), pltpu.SemaphoreType.DMA((4,)), pltpu.SemaphoreType.DMA((4,))],
        compiler_params=pltpu.CompilerParams(vmem_limit_bytes=BIG),
        name="last",
    )(update, well, target)


def per_device(
    pressure, water_sat, gas_sat, old_content, pore_volume, trans_x, trans_y, trans_z, active, aggregate,
    well_cells, well_index, bottom_hole, well_target,
):
    net, cx, cy, cz, mob, sums, nb, wells = exchange(
        pressure, water_sat, gas_sat, active, trans_x, trans_y, trans_z, aggregate, well_cells, well_index, bottom_hole
    )
    residual, t, dinv, sums, faces, parts = local(
        pressure, water_sat, gas_sat, old_content, pore_volume, active, aggregate, mob, net, cx, cy, cz, nb, wells, sums
    )
    update, well = coarse_part(sums, parts, faces, t, dinv, cx, cy, cz, aggregate, nb)
    update, well_residual = last_part(update, well, well_target)
    return residual, update, well_residual


def solution(mesh):
    cells = P("gx", "gy", None)
    three = P(None, "gx", "gy", None)
    well, one = P(("gx", "gy"), None), P(("gx", "gy"))
    return jax.shard_map(
        per_device,
        mesh=mesh,
        in_specs=(cells, cells, cells, three) + (cells,) * 6 + (well, well, one, one),
        out_specs=(three, cells, one),
        check_vma=False,
    )
```

```python
import jax
import jax.numpy as jnp
from jax import lax
from jax.experimental import pallas as pl
from jax.experimental.pallas import tpu as pltpu
from jax.sharding import PartitionSpec as P

CX, CY, NZ = 32, 32, 128
PERF = 16
GROUPS = 8
CITERS = 24
NGX, NGY = 8, 16
NDEV = NGX * NGY
ROWS = 384
RHS_AT, OUT_AT, LEAK_AT = 320, 328, 360

precise = lax.Precision.HIGHEST
compress = (0.001, 0.001, 0.005)
viscosity = (0.5, 1.5, 0.2)
density = (1.0, 0.8, 0.2)
gravity_step = 0.05
relax = 0.6
dead_leak = 0.001

BIG = 60 * 1024 * 1024
f32, i32 = jnp.float32, jnp.int32
MESH = pl.DeviceIdType.MESH
ANY = pl.BlockSpec(memory_space=pl.ANY)
VMEM = pl.BlockSpec(memory_space=pltpu.VMEM)
SMEM = pl.BlockSpec(memory_space=pltpu.SMEM)


def iota(shape, dim):
    return lax.broadcasted_iota(i32, shape, dim)


def greet(barrier):
    place_x, place_y = lax.axis_index("gx"), lax.axis_index("gy")
    for k in range(1, NGX):
        pl.semaphore_signal(barrier, inc=1, device_id=(lax.rem(place_x + k, NGX), place_y), device_id_type=MESH)
    for k in range(1, NGY):
        pl.semaphore_signal(barrier, inc=1, device_id=(place_x, lax.rem(place_y + k, NGY)), device_id_type=MESH)


def loop(first, last, body, carry, steps):
    def several(i, carry):
        for n in range(steps):
            carry = body(first + i * steps + n, carry)
        return carry

    return lax.fori_loop(0, (last - first) // steps, several, carry)


def remote(src, dst, send, recv, x, y):
    return pltpu.make_async_remote_copy(
        src_ref=src, dst_ref=dst, send_sem=send, recv_sem=recv, device_id=(x, y), device_id_type=MESH
    )


def mobility_of(p, ws, gs):
    so = 1.0 - ws - gs
    out = []
    for k, s in enumerate((ws, so, gs)):
        out.append((1.0 + compress[k] * (p - 1.0)) * s * s * (1.0 / viscosity[k]))
    return out


def lane_next(v):
    return pltpu.roll(v, NZ - 1, 1)


def lane_prev(v):
    return pltpu.roll(v, 1, 1)


def line(v):
    return jnp.sum(v, axis=0, keepdims=True)


PAIRS = [(a, b) for a in range(GROUPS) for b in range(a + 1, GROUPS)]
BODY = (pl.ds(0, CX), pl.ds(0, CY), slice(None))


def exchange_kernel(
    p_h, ws_h, gs_h, act_h, tx_h, ty_h, tz_h, agg_h, cells_h, windex_h, hole_h,
    net_o, cx_o, cy_o, cz_o, mob_o, sums_o, nb_o, wells,
    p, ws, gs, act, tx, ty, tz, agg, xlo_f, xlo_i, xhi_f, xhi_i, ylo_f, ylo_i, yhi_f, yhi_i,
    lam, live, mob, net, fy, cx, cy, cz, rim, acc, e4, own4, nb4, cells, windex, hole,
    load_sem, out_sem, face_send, face_recv, send_x, recv_x, send_y, recv_y,
):
    place_x, place_y = lax.axis_index("gx"), lax.axis_index("gy")
    me = place_y * NGX + place_x
    barrier = pltpu.get_barrier_semaphore()
    greet(barrier)
    loads = []
    for src, dst in (
        (cells_h, cells), (windex_h, windex), (hole_h, hole),
        (p_h, p.at[BODY]), (ws_h, ws), (gs_h, gs), (act_h, act), (tx_h, tx), (ty_h, ty), (tz_h, tz), (agg_h, agg.at[BODY])
    ):
        copy = pltpu.make_async_copy(src, dst, load_sem.at[len(loads)])
        copy.start()
        loads.append(copy)
    for copy in loads[:3]:
        copy.wait()
    lane = iota((1, NZ), 1)
    pad = lambda v: jnp.concatenate([v, jnp.zeros((4, NZ - PERF), f32)], axis=1)
    both = pad(cells[...].astype(f32)) + pltpu.roll(pad(windex[...]), PERF, 1)
    row, hole_row = jnp.zeros((1, NZ), f32), jnp.zeros((1, NZ), f32)
    for j in range(4):
        piece = both[j : j + 1]
        if j:
            piece = pltpu.roll(piece, 32 * j, 1)
        row = row + piece
        hole_row = jnp.where(lane // 32 == j, hole[j], hole_row)
    wells[0, pl.ds(me, 1), :] = row
    wells[1, pl.ds(me, 1), :] = hole_row
    pl.semaphore_wait(barrier, NGX - 1 + NGY - 1)

    own = wells.at[:, pl.ds(me, 1), :]
    sends = []
    for k in range(1, NGX):
        sends.append(remote(own, own, send_x.at[k], recv_x.at[k], lax.rem(place_x + k, NGX), place_y))
    up_x, down_x = lax.rem(place_x + 1, NGX), lax.rem(place_x + NGX - 1, NGX)
    up_y, down_y = lax.rem(place_y + 1, NGY), lax.rem(place_y + NGY - 1, NGY)
    faces = []

    def face(src, dst, x, y):
        n = len(faces)
        faces.append(remote(src, dst, face_send.at[n], face_recv.at[n], x, y))

    for n, ref in enumerate((p_h, ws_h, gs_h, tx_h)):
        face(ref.at[CX - 1], xlo_f.at[n], up_x, place_y)
    for n, ref in enumerate((act_h, agg_h)):
        face(ref.at[CX - 1], xlo_i.at[n], up_x, place_y)
    for n, ref in enumerate((p_h, ws_h, gs_h)):
        face(ref.at[0], xhi_f.at[n], down_x, place_y)
    for n, ref in enumerate((act_h, agg_h)):
        face(ref.at[0], xhi_i.at[n], down_x, place_y)
    for n, ref in enumerate((p_h, ws_h, gs_h, ty_h)):
        face(ref.at[:, CY - 1, :], ylo_f.at[n], place_x, up_y)
    for n, ref in enumerate((act_h, agg_h)):
        face(ref.at[:, CY - 1, :], ylo_i.at[n], place_x, up_y)
    for n, ref in enumerate((p_h, ws_h, gs_h)):
        face(ref.at[:, 0, :], yhi_f.at[n], place_x, down_y)
    for n, ref in enumerate((act_h, agg_h)):
        face(ref.at[:, 0, :], yhi_i.at[n], place_x, down_y)
    for copy in sends + faces:
        copy.start()

    for copy in loads[3:7]:
        copy.wait()

    def mobilities(x, _):
        parts = mobility_of(p[x, pl.ds(0, CY), :], ws[x], gs[x])
        for k in range(3):
            lam[k, x, pl.ds(0, CY), :] = parts[k]
        m = act[x].astype(f32)
        live[x, pl.ds(0, CY), :] = m
        mob[x] = m * (parts[0] + parts[1] + parts[2])
        none = jnp.zeros((1, NZ), f32)
        for k in range(3):
            lam[k, x, pl.ds(CY, 1), :] = none
            fy[k, x, pl.ds(0, 1), :] = none
        p[x, pl.ds(CY, 1), :] = none
        live[x, pl.ds(CY, 1), :] = none
        agg[x, pl.ds(CY, 1), :] = jnp.zeros((1, NZ), i32)
        cy[x, pl.ds(0, 1), :] = none
        one = pl.ds(x, 1)
        for side, y in ((0, 0), (1, CY - 1)):
            for k in range(3):
                rim[side, k, one, :] = parts[k][y : y + 1]
            rim[side, 3, one, :] = p[x, pl.ds(y, 1), :]
            rim[side, 4, one, :] = m[y : y + 1]
        return 0

    for k in range(3):
        lam[k, CX] = jnp.zeros((CY + 8, NZ), f32)
    p[CX] = jnp.zeros((CY + 8, NZ), f32)
    live[CX] = jnp.zeros((CY + 8, NZ), f32)
    agg[CX] = jnp.zeros((CY + 8, NZ), i32)
    loop(0, CX, mobilities, 0, 8)
    outs = []

    def give(src, dst):
        copy = pltpu.make_async_copy(src, dst, out_sem.at[len(outs)])
        copy.start()
        outs.append(copy)

    give(mob, mob_o)
    for copy in loads[7:]:
        copy.wait()
    layer_8 = iota((8, NZ), 1)
    row_8 = iota((8, NZ), 0)

    def fluxes(x, carry):
        below = [list(v) for v in carry]
        for c in range(4):
            at = pl.ds(8 * c, 8)
            up = pl.ds(8 * c + 1, 8)
            pp, m = p[x, at, :], live[x, at, :]
            la = [lam[k, x, at, :] for k in range(3)]
            lt = la[0] + la[1] + la[2]
            sums = []
            ln = [lam[k, x + 1, at, :] for k in range(3)]
            f = tx[x, at, :] * m * live[x + 1, at, :]
            d = pp - p[x + 1, at, :]
            for k in range(3):
                flux = f * (0.5 * (la[k] + ln[k])) * d
                sums.append(flux - below[k][c])
                below[k][c] = flux
            e = f * (0.5 * (lt + (ln[0] + ln[1] + ln[2])))
            cx[x + 1, at, :] = e
            ln = [lam[k, x, up, :] for k in range(3)]
            f = ty[x, at, :] * m * live[x, up, :]
            d = pp - p[x, up, :]
            for k in range(3):
                flux = f * (0.5 * (la[k] + ln[k])) * d
                fy[k, x, up, :] = flux
                sums[k] = sums[k] + (flux - fy[k, x, at, :])
            e = f * (0.5 * (lt + (ln[0] + ln[1] + ln[2])))
            cy[x, up, :] = e
            ln = [lane_next(v) for v in la]
            f = jnp.where(layer_8 == NZ - 1, 0.0, tz[x, at, :] * m * lane_next(m))
            d = pp - lane_next(pp)
            for k in range(3):
                flux = f * (0.5 * (la[k] + ln[k])) * (d + density[k] * gravity_step)
                net[k, x, at, :] = sums[k] + (flux - lane_prev(flux))
            cz[x, at, :] = f * (0.5 * (lt + (ln[0] + ln[1] + ln[2])))
        return tuple(tuple(v) for v in below[:3])

    zero = jnp.zeros((8, NZ), f32)
    first = ((zero,) * 4,) * 3
    half = loop(0, CX // 2, fluxes, first, 4)
    for k in range(1, NGX):
        source = place_y * NGX + lax.rem(place_x + NGX - k, NGX)
        there = wells.at[:, pl.ds(source, 1), :]
        remote(there, there, send_x.at[k], recv_x.at[k], lax.rem(place_x + k, NGX), place_y).wait_recv()
    block = wells.at[:, pl.ds(place_y * NGX, NGX), :]
    for k in range(1, NGY):
        copy = remote(block, block, send_y.at[k], recv_y.at[k], place_x, lax.rem(place_y + k, NGY))
        copy.start()
        sends.append(copy)
    loop(CX // 2, CX, fluxes, half, 4)
    give(cz, cz_o)
    for copy in faces:
        copy.wait_recv()

    def face_flux(f, low, high):
        e = f * (0.5 * ((low[0] + low[1] + low[2]) + (high[0] + high[1] + high[2])))
        return [f * (0.5 * (low[k] + high[k])) * (low[3] - high[3]) for k in range(3)], e

    live_at = lambda ids, flag: ids.astype(f32) * jnp.where(flag, 0.0, 1.0)
    body = pl.ds(0, CY)
    low = mobility_of(xlo_f[0], xlo_f[1], xlo_f[2]) + [xlo_f[0]]
    high = [lam[k, 0, body, :] for k in range(3)] + [p[0, body, :]]
    flux, e = face_flux(xlo_f[3] * live_at(xlo_i[0], place_x == 0) * live[0, body, :], low, high)
    for k in range(3):
        net[k, 0] = net[k, 0] - flux[k]
    cx[0] = e
    e4[0] = e
    low = [lam[k, CX - 1, body, :] for k in range(3)] + [p[CX - 1, body, :]]
    high = mobility_of(xhi_f[0], xhi_f[1], xhi_f[2]) + [xhi_f[0]]
    flux, e = face_flux(tx[CX - 1] * live[CX - 1, body, :] * live_at(xhi_i[0], place_x == NGX - 1), low, high)
    for k in range(3):
        net[k, CX - 1] = net[k, CX - 1] + flux[k]
    cx[CX] = e
    e4[1] = e
    low = mobility_of(ylo_f[0], ylo_f[1], ylo_f[2]) + [ylo_f[0]]
    high = [rim[0, k] for k in range(4)]
    flux_low, e = face_flux(ylo_f[3] * live_at(ylo_i[0], place_y == 0) * rim[0, 4], low, high)
    e4[2] = e
    low = [rim[1, k] for k in range(4)]
    high = mobility_of(yhi_f[0], yhi_f[1], yhi_f[2]) + [yhi_f[0]]
    for x in range(CX):
        rim[0, 0, pl.ds(x, 1), :] = ty[x, pl.ds(CY - 1, 1), :]
    flux_high, e = face_flux(rim[0, 0] * rim[1, 4] * live_at(yhi_i[0], place_y == NGY - 1), low, high)
    e4[3] = e
    for x in range(CX):
        one = slice(x, x + 1)
        first_row, last_row = pl.ds(0, 1), pl.ds(CY - 1, 1)
        for k in range(3):
            net[k, x, first_row, :] = net[k, x, first_row, :] - flux_low[k][one]
            net[k, x, last_row, :] = net[k, x, last_row, :] + flux_high[k][one]
        cy[x, first_row, :] = e4[2, pl.ds(x, 1), :]
        cy[x, pl.ds(CY, 1), :] = e[one]
        own4[2, pl.ds(x, 1), :] = agg[x, first_row, :]
        own4[3, pl.ds(x, 1), :] = agg[x, last_row, :]
    for src, dst in ((net, net_o), (cx, cx_o), (cy, cy_o)):
        give(src, dst)

    def crossings(x, sums):
        sums = list(sums)
        for c in range(4):
            at = pl.ds(8 * c, 8)
            up = pl.ds(8 * c + 1, 8)
            a = agg[x, at, :]
            for b, e, ok in (
                (agg[x + 1, at, :], cx[x + 1, at, :], x < CX - 1),
                (agg[x, up, :], cy[x, up, :], (row_8 < 7) if c == 3 else None),
            ):
                code = jnp.minimum(a, b) * GROUPS + jnp.maximum(a, b)
                if ok is not None:
                    code = jnp.where(ok, code, -1)
                for n, (g, h) in enumerate(PAIRS):
                    sums[n] = sums[n] + jnp.where(code == g * GROUPS + h, e, 0.0)
            cross = jnp.where(a != lane_next(a), cz[x, at, :], 0.0)
            for n, (g, h) in enumerate(PAIRS):
                if h == g + 1:
                    sums[n] = sums[n] + jnp.where(a == g, cross, 0.0)
        return tuple(sums)

    acc[...] = jnp.zeros_like(acc)
    sums = loop(0, CX, crossings, (zero,) * len(PAIRS), 2)
    for n, (g, h) in enumerate(PAIRS):
        v = line(sums[n])[0]
        acc[h * GROUPS + g, :] = v
        acc[g * GROUPS + h, :] = v

    own4[0] = agg[0, pl.ds(0, CY), :]
    own4[1] = agg[CX - 1, pl.ds(0, CY), :]
    nb4[0] = xlo_i[1]
    nb4[1] = xhi_i[1]
    nb4[2] = ylo_i[1]
    nb4[3] = yhi_i[1]
    give(nb4, nb_o)

    def side(d, _):
        e, a, b = e4[d], own4[d], nb4[d]
        for h in range(GROUPS):
            w = jnp.where(b == h, e, 0.0)
            rows = [line(jnp.where(a == g, w, 0.0)) for g in range(GROUPS)]
            start = pl.multiple_of(((d + 1) * GROUPS + h) * GROUPS, 8)
            acc[pl.ds(start, GROUPS), :] = jnp.concatenate(rows, axis=0)
        return 0

    lax.fori_loop(0, 4, side, 0)
    for n in range(3):
        sums_o[n] = jnp.sum(acc[pl.ds(NZ * n, NZ), :].T, axis=0, keepdims=True)
    for k in range(1, NGY):
        source = lax.rem(place_y + NGY - k, NGY)
        there = wells.at[:, pl.ds(source * NGX, NGX), :]
        remote(there, there, send_y.at[k], recv_y.at[k], place_x, lax.rem(place_y + k, NGY)).wait_recv()
    for copy in sends + faces:
        copy.wait_send()
    for copy in outs:
        copy.wait()


BLK = (CX, CY, NZ)


def exchange(p, ws, gs, act, tx, ty, tz, agg, cells, windex, hole):
    sds = jax.ShapeDtypeStruct
    dma = pltpu.SemaphoreType.DMA
    v = pltpu.VMEM
    face = lambda n, t: v((n, 32, NZ), t)
    return pl.pallas_call(
        exchange_kernel,
        out_shape=[
            sds((3,) + BLK, f32), sds((CX + 1, CY, NZ), f32), sds((CX, CY + 8, NZ), f32), sds(BLK, f32), sds(BLK, f32),
            sds((3, 1, NZ), f32), sds((4, 32, NZ), i32), sds((2, NDEV, NZ), f32),
        ],
        in_specs=[ANY] * 11,
        out_specs=[ANY] * 5 + [VMEM, ANY, VMEM],
        scratch_shapes=[
            v((CX + 1, CY + 8, NZ), f32), v(BLK, f32), v(BLK, f32), v(BLK, i32),
            v(BLK, f32), v(BLK, f32), v(BLK, f32), v((CX + 1, CY + 8, NZ), i32),
            face(4, f32), face(2, i32), face(3, f32), face(2, i32), face(4, f32), face(2, i32), face(3, f32), face(2, i32),
            v((3, CX + 1, CY + 8, NZ), f32), v((CX + 1, CY + 8, NZ), f32), v(BLK, f32), v((3,) + BLK, f32),
            v((3, CX, CY + 8, NZ), f32), v((CX + 1, CY, NZ), f32), v((CX, CY + 8, NZ), f32), v(BLK, f32),
            v((2, 5, 32, NZ), f32), v((ROWS, NZ), f32), face(4, f32), face(4, i32), face(4, i32),
            v((4, PERF), i32), v((4, PERF), f32), pltpu.SMEM((4,), f32),
            dma((11,)), dma((8,)), dma((22,)), dma((22,)), dma((NGX,)), dma((NGX,)), dma((NGY,)), dma((NGY,)),
        ],
        compiler_params=pltpu.CompilerParams(collective_id=0, has_side_effects=True, vmem_limit_bytes=BIG),
        name="exchange",
    )(p, ws, gs, act, tx, ty, tz, agg, cells, windex, hole)


def local_kernel(
    p_h, ws_h, gs_h, old_h, pv_h, act_h, agg_h, mob_h, net_h, cx_h, cy_h, cz_h, nb_h, wells_h, sums_h,
    res_o, t_o, dinv_o, sums_o, faces_o, parts_o,
    p, ws, gs, act, agg, old, pv, net, cx, cy, cz, nb4,
    mob, w0, w1, trows, loc, cols, loc_s, s, rem, leak, dinv, res, t, acc, s4, wells, sums, parts_v,
    sem, out_sem, one_sem,
):
    place_x, place_y = lax.axis_index("gx"), lax.axis_index("gy")
    copies = []

    def fetch(src, dst):
        copy = pltpu.make_async_copy(src, dst, sem.at[len(copies)])
        copy.start()
        copies.append(copy)

    fetch(wells_h, wells)
    fetch(mob_h, mob)
    fetch(p_h, p)
    early = len(copies)
    for src, dst in (
        (ws_h, ws), (gs_h, gs), (act_h, act), (pv_h, pv), (old_h, old), (net_h, net), (cx_h, cx), (cy_h, cy), (cz_h, cz),
        (agg_h, agg), (nb_h, nb4), (sums_h, sums),
    ):
        fetch(src, dst)

    copies[0].wait()
    lane = iota((NDEV, NZ), 1)
    table = wells[0]
    cell = table.astype(i32)
    cell_x, cell_y, layer = cell >> 16, (cell >> 7) & 511, cell & 127
    slot = lane & 31
    here = (slot < PERF) & (cell >= 0) & ((cell_x >> 5) == place_x) & ((cell_y >> 5) == place_y)
    local = ((((cell_x & 31) << 5) + (cell_y & 31)) << 7) + layer
    local = jnp.where(here, local, -1)
    flag = jnp.where(here, 1.0, 0.0).astype(jnp.bfloat16)
    at_in, at_out = iota((NZ, NZ), 0), iota((NZ, NZ), 1)
    pick = ((at_in // 32 == at_out // 32) & (at_out % 32 == 16)) | (at_out == 17)
    counts = jnp.dot(flag, jnp.where(pick, 1.0, 0.0).astype(jnp.bfloat16), preferred_element_type=f32).astype(i32)
    first_layer = pltpu.roll(layer, 18, 1)
    cols[...] = jnp.where(here, local >> 7, -1)
    loc[...] = jnp.where(slot < PERF, local, jnp.where(slot == 18, first_layer, counts))
    to_scalar = pltpu.make_async_copy(loc, loc_s, one_sem)
    to_scalar.start()

    w0[...] = jnp.zeros_like(w0)
    w1[...] = jnp.zeros_like(w1)
    trows[...] = jnp.zeros_like(trows)
    for copy in copies[1:early]:
        copy.wait()
    to_scalar.wait()

    row_lane = iota((1, NZ), 1)

    def one_row(r, _):
        @pl.when(loc_s[r, 17] > 0)
        def _():
            for j in range(4):

                @pl.when(loc_s[r, 32 * j + 16] > 0)
                def _():
                    top = loc_s[r, 32 * j + 18]
                    shift = lax.rem(top - (32 * j + PERF) + 2 * NZ, NZ)
                    index_z = pltpu.roll(wells[0, pl.ds(r, 1), :], shift, 1)
                    hole_z = pltpu.roll(wells[1, pl.ds(r, 1), :], shift, 1)
                    column_z = pltpu.roll(cols[pl.ds(r, 1), :], lax.rem(top - 32 * j + NZ, NZ), 1)
                    column_z = jnp.where((row_lane >= top) & (row_lane < top + PERF), column_z, -1)
                    drive_z = index_z * hole_z
                    mob_z = jnp.zeros((1, NZ), f32)
                    press_z = jnp.zeros((1, NZ), f32)
                    stores = []
                    for k in range(PERF):
                        q = jnp.maximum(loc_s[r, 32 * j + k], 0) >> 7
                        qx, qy = q >> 5, pl.ds(q & 31, 1)
                        hit = column_z == q
                        stores.append((
                            qx, qy, w0[qx, qy, :] + jnp.where(hit, index_z, 0.0), w1[qx, qy, :] + jnp.where(hit, drive_z, 0.0)
                        ))
                        mob_z = jnp.where(hit, mob[qx, qy, :], mob_z)
                        press_z = jnp.where(hit, p[qx, qy, :], press_z)
                    for qx, qy, sum0, sum1 in stores:
                        w0[qx, qy, :] = sum0
                        w1[qx, qy, :] = sum1
                    well = ((r & (NGX - 1)) * NGY + (r >> 3)) * 4 + j
                    trows[pl.ds(well, 1), :] = index_z * mob_z * (hole_z - press_z)

        return 0

    loop(0, NDEV, one_row, 0, 4)
    total = lax.dot_general(
        jnp.ones((8, NZ), f32), trows[...], (((1,), (1,)), ((), ())), precision=precise, preferred_element_type=f32
    )
    sub = iota((8, NZ), 0)
    parts = jnp.zeros((8, NZ), f32)
    for k in range(NGX):
        piece = total[:, NZ * (k // 2) : NZ * (k // 2) + NZ]
        if k % 2:
            piece = pltpu.roll(piece, 64, 1)
        parts = jnp.where(sub == k, piece, parts)
    parts_v[...] = parts

    for copy in copies[early:]:
        copy.wait()

    def residuals(x, _):
        for c in range(4):
            at = pl.ds(8 * c, 8)
            z = cz[x, at, :]
            diag = (cx[x + 1, at, :] + cx[x, at, :]) + (cy[x, pl.ds(8 * c + 1, 8), :] + cy[x, at, :]) + (z + lane_prev(z))
            pp, m = p[x, at, :], act[x, at, :].astype(f32)
            sw, sg = ws[x, at, :], gs[x, at, :]
            so = 1.0 - sw - sg
            vol = pv[x, at, :]
            wa, wb = w0[x, at, :], w1[x, at, :]
            pull = m * (wb - pp * wa)
            rhs = None
            for k, sat in enumerate((sw, so, sg)):
                held = (1.0 + compress[k] * (pp - 1.0)) * sat
                r = m * (vol * (held - old[k, x, at, :]) + net[k, x, at, :]) - pull * (held * sat * (1.0 / viscosity[k]))
                res[k, x, at, :] = r
                rhs = r if rhs is None else rhs + r
            rhs = -rhs
            store = vol * (compress[0] * sw + compress[1] * so + compress[2] * sg)
            lk = m * store + wa * mob[x, at, :] + dead_leak * (1.0 - m)
            leak[x, at, :] = lk
            diag = diag + lk
            di = relax / diag
            dinv[x, at, :] = di
            sm = rhs * di
            s[x + 1, pl.ds(8 * c + 1, 8), :] = sm
            rem[x, at, :] = rhs - diag * sm
        one = pl.ds(x, 1)
        s4[2, one, :] = s[x + 1, pl.ds(1, 1), :]
        s4[3, one, :] = s[x + 1, pl.ds(CY, 1), :]
        s[x + 1, pl.ds(0, 1), :] = jnp.zeros((1, NZ), f32)
        s[x + 1, pl.ds(CY + 1, 1), :] = jnp.zeros((1, NZ), f32)
        return 0

    loop(0, CX, residuals, 0, 4)
    s4[0] = s[1, pl.ds(1, CY), :]
    s4[1] = s[CX, pl.ds(1, CY), :]
    s[0] = jnp.zeros_like(s[0])
    s[CX + 1] = jnp.zeros_like(s[0])
    outs = []

    def give(src, dst):
        copy = pltpu.make_async_copy(src, dst, out_sem.at[len(outs)])
        copy.start()
        outs.append(copy)

    give(res, res_o)
    give(dinv, dinv_o)
    give(s4, faces_o)
    give(parts_v, parts_o)

    zero = jnp.zeros((8, NZ), f32)

    def remainders(x, carry):
        lk_sum, re_sum = [list(v) for v in carry]
        for c in range(4):
            at = pl.ds(8 * c, 8)
            up = pl.ds(8 * c + 1, 8)
            here = s[x + 1, up, :]
            z = cz[x, at, :]
            near = cx[x + 1, at, :] * s[x + 2, up, :] + cx[x, at, :] * s[x, up, :]
            near = near + (cy[x, up, :] * s[x + 1, pl.ds(8 * c + 2, 8), :] + cy[x, at, :] * s[x + 1, at, :])
            near = near + (z * lane_next(here) + lane_prev(z * here))
            re = rem[x, at, :] + near
            t[x, at, :] = here + dinv[x, at, :] * re
            lk = leak[x, at, :]
            a = agg[x, at, :]
            for g in range(GROUPS):
                hit = a == g
                re_sum[g] = re_sum[g] + jnp.where(hit, re, 0.0)
                lk_sum[g] = lk_sum[g] + jnp.where(hit, lk, 0.0)
        return tuple(lk_sum), tuple(re_sum)

    lk_sum, re_sum = loop(0, CX, remainders, ((zero,) * GROUPS, (zero,) * GROUPS), 4)
    give(t, t_o)
    rows = [line(v) for v in re_sum]
    acc[...] = jnp.zeros_like(acc)
    for n in range(2):
        coef = (cx[0], cx[CX])[n]
        es = coef * s4[n]
        rows += [line(jnp.where(nb4[n] == g, es, 0.0)) for g in range(GROUPS)]
    e4 = trows
    for x in range(CX):
        e4[pl.ds(x, 1), :] = cy[x, pl.ds(0, 1), :]
        e4[pl.ds(CX + x, 1), :] = cy[x, pl.ds(CY, 1), :]
    for n in range(2):
        es = e4[pl.ds(CX * n, CX), :] * s4[2 + n]
        rows += [line(jnp.where(nb4[2 + n] == g, es, 0.0)) for g in range(GROUPS)]
    rows += [line(v) for v in lk_sum]
    first = RHS_AT - 2 * NZ
    for n in range(6):
        acc[pl.ds(first + 8 * n, 8), :] = jnp.concatenate(rows[8 * n : 8 * n + 8], axis=0)
    sums[2] = sums[2] + jnp.sum(acc[...].T, axis=0, keepdims=True)
    give(sums, sums_o)
    for copy in outs:
        copy.wait()


def local(p, ws, gs, old, pv, act, agg, mob, net, cx, cy, cz, nb, wells, sums):
    v = pltpu.VMEM
    sds = jax.ShapeDtypeStruct
    dma = pltpu.SemaphoreType.DMA
    return pl.pallas_call(
        local_kernel,
        out_shape=[
            sds((3,) + BLK, f32), sds(BLK, f32), sds(BLK, f32), sds((3, 1, NZ), f32), sds((4, 32, NZ), f32), sds((8, NZ), f32)
        ],
        in_specs=[ANY] * 15,
        out_specs=[ANY] * 6,
        scratch_shapes=[
            v(BLK, f32), v(BLK, f32), v(BLK, f32), v(BLK, i32), v(BLK, i32), v((3,) + BLK, f32), v(BLK, f32),
            v((3,) + BLK, f32), v((CX + 1, CY, NZ), f32), v((CX, CY + 8, NZ), f32), v(BLK, f32), v((4, 32, NZ), i32),
            v(BLK, f32), v(BLK, f32), v(BLK, f32), v((4 * NDEV, NZ), f32), v((NDEV, NZ), i32), v((NDEV, NZ), i32), pltpu.SMEM((NDEV, NZ), i32),
            v((CX + 2, CY + 8, NZ), f32), v(BLK, f32), v(BLK, f32), v(BLK, f32), v((3,) + BLK, f32), v(BLK, f32),
            v((NZ, NZ), f32), v((4, 32, NZ), f32), v((2, NDEV, NZ), f32), v((3, 1, NZ), f32), v((8, NZ), f32),
            dma((16,)), dma((8,)), dma,
        ],
        compiler_params=pltpu.CompilerParams(vmem_limit_bytes=BIG),
        name="local",
    )(p, ws, gs, old, pv, act, agg, mob, net, cx, cy, cz, nb, wells, sums)


def coarse_kernel(
    sums_h, parts_h, faces, t_h, dinv_h, cx_h, cy_h, cz_h, agg_h, nb_h, target,
    update_o, well_o,
    gather, mat, slots, send_rows, rows_x, rows_y, tall, dinv, cx, cy, cz, agg, far, pc, sums, parts, nb4,
    sem, send_x, recv_x, send_y, recv_y, psend_x, precv_x, psend_y, precv_y, fsend, frecv,
):
    place_x, place_y = lax.axis_index("gx"), lax.axis_index("gy")
    me = place_y * NGX + place_x
    barrier = pltpu.get_barrier_semaphore()
    greet(barrier)
    loads = []
    body = (slice(None), pl.ds(0, CY), slice(None))
    for src, dst in ((sums_h, sums), (parts_h, parts), (nb_h, nb4), (t_h, tall), (dinv_h, dinv), (cx_h, cx), (cy_h, cy), (cz_h, cz), (agg_h, agg)):
        copy = pltpu.make_async_copy(src, dst, sem.at[len(loads)])
        copy.start()
        loads.append(copy)
    for copy in loads[:2]:
        copy.wait()
    for n in range(3):
        gather[n, pl.ds(me, 1), :] = sums[n]
    rows_x[pl.ds(place_x, 1), :] = parts[pl.ds(place_x, 1), :]
    pl.semaphore_wait(barrier, NGX - 1 + NGY - 1)

    sends = []
    own = gather.at[:, pl.ds(me, 1), :]
    for k in range(1, NGX):
        peer = lax.rem(place_x + k, NGX)
        sends.append(remote(own, own, send_x.at[k], recv_x.at[k], peer, place_y))
    for k in range(1, NGX):
        peer = lax.rem(place_x + k, NGX)
        sends.append(
            remote(parts.at[pl.ds(peer, 1), :], rows_x.at[pl.ds(place_x, 1), :], psend_x.at[k], precv_x.at[k], peer, place_y)
        )
    halo = [
        remote(faces.at[1], far.at[0], fsend.at[0], frecv.at[0], lax.rem(place_x + 1, NGX), place_y),
        remote(faces.at[0], far.at[1], fsend.at[1], frecv.at[1], lax.rem(place_x + NGX - 1, NGX), place_y),
        remote(faces.at[3], far.at[2], fsend.at[2], frecv.at[2], place_x, lax.rem(place_y + 1, NGY)),
        remote(faces.at[2], far.at[3], fsend.at[3], frecv.at[3], place_x, lax.rem(place_y + NGY - 1, NGY)),
    ]
    for copy in sends + halo:
        copy.start()
    for k in range(1, NGX):
        source = place_y * NGX + lax.rem(place_x + NGX - k, NGX)
        there = gather.at[:, pl.ds(source, 1), :]
        remote(there, there, send_x.at[k], recv_x.at[k], place_x, place_y).wait_recv()
    block = gather.at[:, pl.ds(place_y * NGX, NGX), :]
    for k in range(1, NGY):
        copy = remote(block, block, send_y.at[k], recv_y.at[k], place_x, lax.rem(place_y + k, NGY))
        copy.start()
        sends.append(copy)
    for k in range(1, NGX):
        source = lax.rem(place_x + NGX - k, NGX)
        there = rows_x.at[pl.ds(source, 1), :]
        remote(there, there, psend_x.at[k], precv_x.at[k], place_x, place_y).wait_recv()
    line = jnp.sum(rows_x[...], axis=0, keepdims=True)
    for k in range(NGY):
        send_rows[k : k + 1, :] = line if k == 0 else pltpu.roll(line, NZ - 4 * k, 1)
    rows_y[pl.ds(place_y, 1), :] = send_rows[pl.ds(place_y, 1), :]
    for k in range(1, NGY):
        peer = lax.rem(place_y + k, NGY)
        copy = remote(
            send_rows.at[pl.ds(peer, 1), :], rows_y.at[pl.ds(place_y, 1), :], psend_y.at[k], precv_y.at[k], place_x, peer
        )
        copy.start()
        sends.append(copy)
    for k in range(1, NGY):
        source = lax.rem(place_y + NGY - k, NGY)
        there = gather.at[:, pl.ds(source * NGX, NGX), :]
        remote(there, there, send_y.at[k], recv_y.at[k], place_x, place_y).wait_recv()

    for n in range(3):
        mat[pl.ds(NZ * n, NZ), :] = gather[n].T
    sub = iota((8, NZ), 0)

    def rows(n):
        return mat[pl.ds(8 * n, 8), :]

    moves = (0, 1, NZ - 1, NGX, NZ - NGX)
    total = jnp.zeros((8, NZ), f32)
    for n in range(5 * GROUPS):
        total = total + rows(n)
    total = total + rows(LEAK_AT // 8)
    for h in range(GROUPS):
        block = rows(h)
        slots[pl.ds(8 * h, 8), :] = jnp.where(sub == h, total, -block)
    for d in range(1, 5):
        for h in range(GROUPS):
            v = -rows(d * GROUPS + h)
            slots[pl.ds((d * GROUPS + h) * 8, 8), :] = pltpu.roll(v, (NZ - moves[d]) % NZ, 1)
    rhs = rows(RHS_AT // 8)
    for d in range(1, 5):
        away = (0, 2, 1, 4, 3)[d]
        rhs = rhs + pltpu.roll(rows(OUT_AT // 8 + away - 1), moves[d], 1)

    def dot(a, b):
        return jnp.sum(jnp.sum(a * b, axis=0, keepdims=True), axis=1, keepdims=True)

    def tree(values):
        while len(values) > 1:
            values = [a + b for a, b in zip(values[::2], values[1::2])] + values[len(values) // 2 * 2 :]
        return values[0]

    def image(v):
        spread = [jnp.broadcast_to(v[h : h + 1, :], (8, NZ)) for h in range(GROUPS)]
        sides = [tree([slots[pl.ds((d * GROUPS + h) * 8, 8), :] * spread[h] for h in range(GROUPS)]) for d in range(5)]
        return tree([pltpu.roll(sides[d], moves[d], 1) for d in range(1, 5)]) + sides[0]

    w = image(rhs)
    norm = dot(rhs, rhs)
    alpha = norm / dot(w, rhs)

    def one_step(_, carry):
        x, r, q, aq, norm, alpha = carry
        x = x + alpha * q
        r = r - alpha * aq
        new = dot(r, r)
        w = image(r)
        curve = dot(w, r)
        beta = new / norm
        alpha = new / (curve - beta * (new / alpha))
        return x, r, r + beta * q, w + beta * aq, new, alpha

    start = (jnp.zeros((8, NZ), f32), rhs, rhs, w, norm, alpha)
    x, _, q, _, _, alpha = loop(0, CITERS - 1, one_step, start, 1)
    coarse = x + alpha * q
    mine = iota((8, NZ), 1) == me
    values = []
    for d in range(5):
        v = coarse if d == 0 else pltpu.roll(coarse, moves[d], 1)
        values.append(jnp.sum(jnp.where(mine, v, 0.0), axis=1, keepdims=True))

    def look_up(ids, d):
        v = jnp.broadcast_to(values[d][0:1, :], ids.shape)
        for g in range(1, GROUPS):
            v = jnp.where(ids == g, values[d][g : g + 1, :], v)
        return v

    for copy in halo:
        copy.wait_recv()
    for copy in loads[2:]:
        copy.wait()
    pc[0, pl.ds(8, CY), :] = far[0] + look_up(nb4[0], 1)
    pc[CX + 1, pl.ds(8, CY), :] = far[1] + look_up(nb4[1], 2)
    far[2] = far[2] + look_up(nb4[2], 3)
    far[3] = far[3] + look_up(nb4[3], 4)

    def fill(x, _):
        pc[x + 1, pl.ds(8, CY), :] = look_up(agg[x], 0)
        pc[x + 1, pl.ds(7, 1), :] = far[2, pl.ds(x, 1), :]
        pc[x + 1, pl.ds(CY + 8, 1), :] = far[3, pl.ds(x, 1), :]
        return 0

    loop(0, CX, fill, 0, 8)

    def finish(x, _):
        for c in range(4):
            at = pl.ds(8 * c, 8)
            mid = pl.ds(8 * c + 8, 8)
            here = pc[x + 1, mid, :]
            z = cz[x, at, :]
            near = cx[x + 1, at, :] * pc[x + 2, mid, :] + cx[x, at, :] * pc[x, mid, :]
            near = near + (
                cy[x, pl.ds(8 * c + 1, 8), :] * pc[x + 1, pl.ds(8 * c + 9, 8), :]
                + cy[x, at, :] * pc[x + 1, pl.ds(8 * c + 7, 8), :]
            )
            near = near + (z * lane_next(here) + lane_prev(z * here))
            update_o[x, at, :] = tall[x, at, :] + (1.0 - relax) * here + dinv[x, at, :] * near
        return 0

    loop(0, CX, finish, 0, 8)
    for k in range(1, NGY):
        source = lax.rem(place_y + NGY - k, NGY)
        there = rows_y.at[pl.ds(source, 1), :]
        remote(there, there, psend_y.at[k], precv_y.at[k], place_x, place_y).wait_recv()
    rates = jnp.sum(rows_y[...], axis=0, keepdims=True)
    for j in range(4):
        well_o[j] = rates[0, j] - target[j]
    for copy in sends + halo:
        copy.wait_send()


def coarse_part(sums, parts, faces, t, dinv, cx, cy, cz, agg, nb4, target):
    v = pltpu.VMEM
    sds = jax.ShapeDtypeStruct
    dma = pltpu.SemaphoreType.DMA
    return pl.pallas_call(
        coarse_kernel,
        out_shape=[sds(BLK, f32), sds((4,), f32)],
        in_specs=[ANY] * 10 + [SMEM],
        out_specs=[VMEM, SMEM],
        scratch_shapes=[
            v((3, NDEV, NZ), f32), v((ROWS, NZ), f32), v((5 * 64, NZ), f32), v((NGY, NZ), f32), v((NGX, NZ), f32), v((NGY, NZ), f32),
            v(BLK, f32), v(BLK, f32), v((CX + 1, CY, NZ), f32), v((CX, CY + 8, NZ), f32), v(BLK, f32), v(BLK, i32),
            v((4, 32, NZ), f32), v((CX + 2, CY + 16, NZ), f32),
            v((3, 1, NZ), f32), v((8, NZ), f32), v((4, 32, NZ), i32),
            dma((9,)), dma((NGX,)), dma((NGX,)), dma((NGY,)), dma((NGY,)),
            dma((NGX,)), dma((NGX,)), dma((NGY,)), dma((NGY,)), dma((4,)), dma((4,)),
        ],
        compiler_params=pltpu.CompilerParams(
            collective_id=1, has_side_effects=True, vmem_limit_bytes=BIG
        ),
        name="coarse",
    )(sums, parts, faces, t, dinv, cx, cy, cz, agg, nb4, target)


def last_kernel(update_h, well_h, update_o, well_o, held, sem_in, sem_out, well_sem):
    part = CX // 4
    moves = []
    well = pltpu.make_async_copy(well_h, well_o, well_sem)
    well.start()
    for n in range(4):
        at = pl.ds(part * n, part)
        copy = pltpu.make_async_copy(update_h.at[at], held.at[at], sem_in.at[n])
        copy.start()
        moves.append((copy, pltpu.make_async_copy(held.at[at], update_o.at[at], sem_out.at[n])))
    for arrive, leave in moves:
        arrive.wait()
        leave.start()
    for _, leave in moves:
        leave.wait()
    well.wait()


def last_part(update, well):
    sds = jax.ShapeDtypeStruct
    return pl.pallas_call(
        last_kernel,
        out_shape=[sds(BLK, f32), sds((4,), f32)],
        in_specs=[ANY, ANY],
        out_specs=[ANY, ANY],
        scratch_shapes=[pltpu.VMEM(BLK, f32), pltpu.SemaphoreType.DMA((4,)), pltpu.SemaphoreType.DMA((4,)), pltpu.SemaphoreType.DMA],
        compiler_params=pltpu.CompilerParams(vmem_limit_bytes=BIG),
        name="last",
    )(update, well)


def per_device(
    pressure, water_sat, gas_sat, old_content, pore_volume, trans_x, trans_y, trans_z, active, aggregate,
    well_cells, well_index, bottom_hole, well_target,
):
    net, cx, cy, cz, mob, sums, nb, wells = exchange(
        pressure, water_sat, gas_sat, active, trans_x, trans_y, trans_z, aggregate, well_cells, well_index, bottom_hole
    )
    residual, t, dinv, sums, faces, parts = local(
        pressure, water_sat, gas_sat, old_content, pore_volume, active, aggregate, mob, net, cx, cy, cz, nb, wells, sums
    )
    update, well = coarse_part(sums, parts, faces, t, dinv, cx, cy, cz, aggregate, nb, well_target)
    update, well_residual = last_part(update, well)
    return residual, update, well_residual


def solution(mesh):
    cells = P("gx", "gy", None)
    three = P(None, "gx", "gy", None)
    well, one = P(("gx", "gy"), None), P(("gx", "gy"))
    return jax.shard_map(
        per_device,
        mesh=mesh,
        in_specs=(cells, cells, cells, three) + (cells,) * 6 + (well, well, one, one),
        out_specs=(three, cells, one),
        check_vma=False,
    )
```

```python
import jax
import jax.numpy as jnp
from jax import lax
from jax.experimental import pallas as pl
from jax.experimental.pallas import tpu as pltpu
from jax.sharding import PartitionSpec as P

CX, CY, NZ = 32, 32, 128
PERF = 16
GROUPS = 8
CITERS = 24
NGX, NGY = 8, 16
NDEV = NGX * NGY
ROWS = 384
RHS_AT, OUT_AT, LEAK_AT = 320, 328, 360

precise = lax.Precision.HIGHEST
compress = (0.001, 0.001, 0.005)
viscosity = (0.5, 1.5, 0.2)
density = (1.0, 0.8, 0.2)
gravity_step = 0.05
relax = 0.6
dead_leak = 0.001

BIG = 60 * 1024 * 1024
f32, i32 = jnp.float32, jnp.int32
MESH = pl.DeviceIdType.MESH
ANY = pl.BlockSpec(memory_space=pl.ANY)
VMEM = pl.BlockSpec(memory_space=pltpu.VMEM)
SMEM = pl.BlockSpec(memory_space=pltpu.SMEM)


def iota(shape, dim):
    return lax.broadcasted_iota(i32, shape, dim)


def greet(barrier):
    place_x, place_y = lax.axis_index("gx"), lax.axis_index("gy")
    for k in range(1, NGX):
        pl.semaphore_signal(barrier, inc=1, device_id=(lax.rem(place_x + k, NGX), place_y), device_id_type=MESH)
    for k in range(1, NGY):
        pl.semaphore_signal(barrier, inc=1, device_id=(place_x, lax.rem(place_y + k, NGY)), device_id_type=MESH)


def loop(first, last, body, carry, steps):
    def several(i, carry):
        for n in range(steps):
            carry = body(first + i * steps + n, carry)
        return carry

    return lax.fori_loop(0, (last - first) // steps, several, carry)


def remote(src, dst, send, recv, x, y):
    return pltpu.make_async_remote_copy(
        src_ref=src, dst_ref=dst, send_sem=send, recv_sem=recv, device_id=(x, y), device_id_type=MESH
    )


def mobility_of(p, ws, gs):
    so = 1.0 - ws - gs
    out = []
    for k, s in enumerate((ws, so, gs)):
        out.append((1.0 + compress[k] * (p - 1.0)) * s * s * (1.0 / viscosity[k]))
    return out


def lane_next(v):
    return pltpu.roll(v, NZ - 1, 1)


def lane_prev(v):
    return pltpu.roll(v, 1, 1)


def line(v):
    return jnp.sum(v, axis=0, keepdims=True)


PAIRS = [(a, b) for a in range(GROUPS) for b in range(a + 1, GROUPS)]
BODY = (pl.ds(0, CX), pl.ds(0, CY), slice(None))


def exchange_kernel(
    p_h, ws_h, gs_h, act_h, tx_h, ty_h, tz_h, agg_h, cells_h, windex_h, hole_h,
    net_o, cx_o, cy_o, cz_o, mob_o, sums_o, nb_o, wells,
    p, ws, gs, act, tx, ty, tz, agg, xlo_f, xlo_i, xhi_f, xhi_i, ylo_f, ylo_i, yhi_f, yhi_i,
    lam, live, mob, net, fy, cx, cy, cz, rim, acc, e4, own4, nb4, cells, windex, hole,
    load_sem, out_sem, face_send, face_recv, send_x, recv_x, send_y, recv_y,
):
    place_x, place_y = lax.axis_index("gx"), lax.axis_index("gy")
    me = place_y * NGX + place_x
    barrier = pltpu.get_barrier_semaphore()
    greet(barrier)
    loads = []
    for src, dst in (
        (cells_h, cells), (windex_h, windex), (hole_h, hole),
        (p_h, p.at[BODY]), (ws_h, ws), (gs_h, gs), (act_h, act), (tx_h, tx), (ty_h, ty), (tz_h, tz), (agg_h, agg.at[BODY])
    ):
        copy = pltpu.make_async_copy(src, dst, load_sem.at[len(loads)])
        copy.start()
        loads.append(copy)
    for copy in loads[:3]:
        copy.wait()
    lane = iota((1, NZ), 1)
    pad = lambda v: jnp.concatenate([v, jnp.zeros((4, NZ - PERF), f32)], axis=1)
    both = pad(cells[...].astype(f32)) + pltpu.roll(pad(windex[...]), PERF, 1)
    row, hole_row = jnp.zeros((1, NZ), f32), jnp.zeros((1, NZ), f32)
    for j in range(4):
        piece = both[j : j + 1]
        if j:
            piece = pltpu.roll(piece, 32 * j, 1)
        row = row + piece
        hole_row = jnp.where(lane // 32 == j, hole[j], hole_row)
    wells[0, pl.ds(me, 1), :] = row
    wells[1, pl.ds(me, 1), :] = hole_row
    pl.semaphore_wait(barrier, NGX - 1 + NGY - 1)

    own = wells.at[:, pl.ds(me, 1), :]
    sends = []
    for k in range(1, NGX):
        sends.append(remote(own, own, send_x.at[k], recv_x.at[k], lax.rem(place_x + k, NGX), place_y))
    up_x, down_x = lax.rem(place_x + 1, NGX), lax.rem(place_x + NGX - 1, NGX)
    up_y, down_y = lax.rem(place_y + 1, NGY), lax.rem(place_y + NGY - 1, NGY)
    faces = []

    def face(src, dst, x, y):
        n = len(faces)
        faces.append(remote(src, dst, face_send.at[n], face_recv.at[n], x, y))

    for n, ref in enumerate((p_h, ws_h, gs_h, tx_h)):
        face(ref.at[CX - 1], xlo_f.at[n], up_x, place_y)
    for n, ref in enumerate((act_h, agg_h)):
        face(ref.at[CX - 1], xlo_i.at[n], up_x, place_y)
    for n, ref in enumerate((p_h, ws_h, gs_h)):
        face(ref.at[0], xhi_f.at[n], down_x, place_y)
    for n, ref in enumerate((act_h, agg_h)):
        face(ref.at[0], xhi_i.at[n], down_x, place_y)
    for n, ref in enumerate((p_h, ws_h, gs_h, ty_h)):
        face(ref.at[:, CY - 1, :], ylo_f.at[n], place_x, up_y)
    for n, ref in enumerate((act_h, agg_h)):
        face(ref.at[:, CY - 1, :], ylo_i.at[n], place_x, up_y)
    for n, ref in enumerate((p_h, ws_h, gs_h)):
        face(ref.at[:, 0, :], yhi_f.at[n], place_x, down_y)
    for n, ref in enumerate((act_h, agg_h)):
        face(ref.at[:, 0, :], yhi_i.at[n], place_x, down_y)
    for copy in sends + faces:
        copy.start()

    for copy in loads[3:7]:
        copy.wait()

    def mobilities(x, _):
        parts = mobility_of(p[x, pl.ds(0, CY), :], ws[x], gs[x])
        for k in range(3):
            lam[k, x, pl.ds(0, CY), :] = parts[k]
        m = act[x].astype(f32)
        live[x, pl.ds(0, CY), :] = m
        mob[x] = m * (parts[0] + parts[1] + parts[2])
        none = jnp.zeros((1, NZ), f32)
        for k in range(3):
            lam[k, x, pl.ds(CY, 1), :] = none
            fy[k, x, pl.ds(0, 1), :] = none
        p[x, pl.ds(CY, 1), :] = none
        live[x, pl.ds(CY, 1), :] = none
        agg[x, pl.ds(CY, 1), :] = jnp.zeros((1, NZ), i32)
        cy[x, pl.ds(0, 1), :] = none
        one = pl.ds(x, 1)
        for side, y in ((0, 0), (1, CY - 1)):
            for k in range(3):
                rim[side, k, one, :] = parts[k][y : y + 1]
            rim[side, 3, one, :] = p[x, pl.ds(y, 1), :]
            rim[side, 4, one, :] = m[y : y + 1]
        return 0

    for k in range(3):
        lam[k, CX] = jnp.zeros((CY + 8, NZ), f32)
    p[CX] = jnp.zeros((CY + 8, NZ), f32)
    live[CX] = jnp.zeros((CY + 8, NZ), f32)
    agg[CX] = jnp.zeros((CY + 8, NZ), i32)
    loop(0, CX, mobilities, 0, 8)
    outs = []

    def give(src, dst):
        copy = pltpu.make_async_copy(src, dst, out_sem.at[len(outs)])
        copy.start()
        outs.append(copy)

    give(mob, mob_o)
    for copy in loads[7:]:
        copy.wait()
    layer_8 = iota((8, NZ), 1)
    row_8 = iota((8, NZ), 0)

    def fluxes(x, carry):
        below = [list(v) for v in carry]
        for c in range(4):
            at = pl.ds(8 * c, 8)
            up = pl.ds(8 * c + 1, 8)
            pp, m = p[x, at, :], live[x, at, :]
            la = [lam[k, x, at, :] for k in range(3)]
            lt = la[0] + la[1] + la[2]
            sums = []
            ln = [lam[k, x + 1, at, :] for k in range(3)]
            f = tx[x, at, :] * m * live[x + 1, at, :]
            d = pp - p[x + 1, at, :]
            for k in range(3):
                flux = f * (0.5 * (la[k] + ln[k])) * d
                sums.append(flux - below[k][c])
                below[k][c] = flux
            e = f * (0.5 * (lt + (ln[0] + ln[1] + ln[2])))
            cx[x + 1, at, :] = e
            ln = [lam[k, x, up, :] for k in range(3)]
            f = ty[x, at, :] * m * live[x, up, :]
            d = pp - p[x, up, :]
            for k in range(3):
                flux = f * (0.5 * (la[k] + ln[k])) * d
                fy[k, x, up, :] = flux
                sums[k] = sums[k] + (flux - fy[k, x, at, :])
            e = f * (0.5 * (lt + (ln[0] + ln[1] + ln[2])))
            cy[x, up, :] = e
            ln = [lane_next(v) for v in la]
            f = jnp.where(layer_8 == NZ - 1, 0.0, tz[x, at, :] * m * lane_next(m))
            d = pp - lane_next(pp)
            for k in range(3):
                flux = f * (0.5 * (la[k] + ln[k])) * (d + density[k] * gravity_step)
                net[k, x, at, :] = sums[k] + (flux - lane_prev(flux))
            cz[x, at, :] = f * (0.5 * (lt + (ln[0] + ln[1] + ln[2])))
        return tuple(tuple(v) for v in below[:3])

    zero = jnp.zeros((8, NZ), f32)
    first = ((zero,) * 4,) * 3
    half = loop(0, CX // 2, fluxes, first, 4)
    for k in range(1, NGX):
        source = place_y * NGX + lax.rem(place_x + NGX - k, NGX)
        there = wells.at[:, pl.ds(source, 1), :]
        remote(there, there, send_x.at[k], recv_x.at[k], lax.rem(place_x + k, NGX), place_y).wait_recv()
    block = wells.at[:, pl.ds(place_y * NGX, NGX), :]
    for k in range(1, NGY):
        copy = remote(block, block, send_y.at[k], recv_y.at[k], place_x, lax.rem(place_y + k, NGY))
        copy.start()
        sends.append(copy)
    loop(CX // 2, CX, fluxes, half, 4)
    give(cz, cz_o)
    for copy in faces:
        copy.wait_recv()

    def face_flux(f, low, high):
        e = f * (0.5 * ((low[0] + low[1] + low[2]) + (high[0] + high[1] + high[2])))
        return [f * (0.5 * (low[k] + high[k])) * (low[3] - high[3]) for k in range(3)], e

    live_at = lambda ids, flag: ids.astype(f32) * jnp.where(flag, 0.0, 1.0)
    body = pl.ds(0, CY)
    low = mobility_of(xlo_f[0], xlo_f[1], xlo_f[2]) + [xlo_f[0]]
    high = [lam[k, 0, body, :] for k in range(3)] + [p[0, body, :]]
    flux, e = face_flux(xlo_f[3] * live_at(xlo_i[0], place_x == 0) * live[0, body, :], low, high)
    for k in range(3):
        net[k, 0] = net[k, 0] - flux[k]
    cx[0] = e
    e4[0] = e
    low = [lam[k, CX - 1, body, :] for k in range(3)] + [p[CX - 1, body, :]]
    high = mobility_of(xhi_f[0], xhi_f[1], xhi_f[2]) + [xhi_f[0]]
    flux, e = face_flux(tx[CX - 1] * live[CX - 1, body, :] * live_at(xhi_i[0], place_x == NGX - 1), low, high)
    for k in range(3):
        net[k, CX - 1] = net[k, CX - 1] + flux[k]
    cx[CX] = e
    e4[1] = e
    low = mobility_of(ylo_f[0], ylo_f[1], ylo_f[2]) + [ylo_f[0]]
    high = [rim[0, k] for k in range(4)]
    flux_low, e = face_flux(ylo_f[3] * live_at(ylo_i[0], place_y == 0) * rim[0, 4], low, high)
    e4[2] = e
    low = [rim[1, k] for k in range(4)]
    high = mobility_of(yhi_f[0], yhi_f[1], yhi_f[2]) + [yhi_f[0]]
    for x in range(CX):
        rim[0, 0, pl.ds(x, 1), :] = ty[x, pl.ds(CY - 1, 1), :]
    flux_high, e = face_flux(rim[0, 0] * rim[1, 4] * live_at(yhi_i[0], place_y == NGY - 1), low, high)
    e4[3] = e
    for x in range(CX):
        one = slice(x, x + 1)
        first_row, last_row = pl.ds(0, 1), pl.ds(CY - 1, 1)
        for k in range(3):
            net[k, x, first_row, :] = net[k, x, first_row, :] - flux_low[k][one]
            net[k, x, last_row, :] = net[k, x, last_row, :] + flux_high[k][one]
        cy[x, first_row, :] = e4[2, pl.ds(x, 1), :]
        cy[x, pl.ds(CY, 1), :] = e[one]
        own4[2, pl.ds(x, 1), :] = agg[x, first_row, :]
        own4[3, pl.ds(x, 1), :] = agg[x, last_row, :]
    for src, dst in ((net, net_o), (cx, cx_o), (cy, cy_o)):
        give(src, dst)

    def crossings(x, sums):
        sums = list(sums)
        for c in range(4):
            at = pl.ds(8 * c, 8)
            up = pl.ds(8 * c + 1, 8)
            a = agg[x, at, :]
            for b, e, ok in (
                (agg[x + 1, at, :], cx[x + 1, at, :], x < CX - 1),
                (agg[x, up, :], cy[x, up, :], (row_8 < 7) if c == 3 else None),
            ):
                code = jnp.minimum(a, b) * GROUPS + jnp.maximum(a, b)
                if ok is not None:
                    code = jnp.where(ok, code, -1)
                for n, (g, h) in enumerate(PAIRS):
                    sums[n] = sums[n] + jnp.where(code == g * GROUPS + h, e, 0.0)
            cross = jnp.where(a != lane_next(a), cz[x, at, :], 0.0)
            for n, (g, h) in enumerate(PAIRS):
                if h == g + 1:
                    sums[n] = sums[n] + jnp.where(a == g, cross, 0.0)
        return tuple(sums)

    acc[...] = jnp.zeros_like(acc)
    sums = loop(0, CX, crossings, (zero,) * len(PAIRS), 2)
    for n, (g, h) in enumerate(PAIRS):
        v = line(sums[n])[0]
        acc[h * GROUPS + g, :] = v
        acc[g * GROUPS + h, :] = v

    own4[0] = agg[0, pl.ds(0, CY), :]
    own4[1] = agg[CX - 1, pl.ds(0, CY), :]
    nb4[0] = xlo_i[1]
    nb4[1] = xhi_i[1]
    nb4[2] = ylo_i[1]
    nb4[3] = yhi_i[1]
    give(nb4, nb_o)

    def side(d, _):
        e, a, b = e4[d], own4[d], nb4[d]
        for h in range(GROUPS):
            w = jnp.where(b == h, e, 0.0)
            rows = [line(jnp.where(a == g, w, 0.0)) for g in range(GROUPS)]
            start = pl.multiple_of(((d + 1) * GROUPS + h) * GROUPS, 8)
            acc[pl.ds(start, GROUPS), :] = jnp.concatenate(rows, axis=0)
        return 0

    lax.fori_loop(0, 4, side, 0)
    for n in range(3):
        sums_o[n] = jnp.sum(acc[pl.ds(NZ * n, NZ), :].T, axis=0, keepdims=True)
    for k in range(1, NGY):
        source = lax.rem(place_y + NGY - k, NGY)
        there = wells.at[:, pl.ds(source * NGX, NGX), :]
        remote(there, there, send_y.at[k], recv_y.at[k], place_x, lax.rem(place_y + k, NGY)).wait_recv()
    for copy in sends + faces:
        copy.wait_send()
    for copy in outs:
        copy.wait()


BLK = (CX, CY, NZ)


def exchange(p, ws, gs, act, tx, ty, tz, agg, cells, windex, hole):
    sds = jax.ShapeDtypeStruct
    dma = pltpu.SemaphoreType.DMA
    v = pltpu.VMEM
    face = lambda n, t: v((n, 32, NZ), t)
    return pl.pallas_call(
        exchange_kernel,
        out_shape=[
            sds((3,) + BLK, f32), sds((CX + 1, CY, NZ), f32), sds((CX, CY + 8, NZ), f32), sds(BLK, f32), sds(BLK, f32),
            sds((3, 1, NZ), f32), sds((4, 32, NZ), i32), sds((2, NDEV, NZ), f32),
        ],
        in_specs=[ANY] * 11,
        out_specs=[ANY] * 5 + [VMEM, ANY, VMEM],
        scratch_shapes=[
            v((CX + 1, CY + 8, NZ), f32), v(BLK, f32), v(BLK, f32), v(BLK, i32),
            v(BLK, f32), v(BLK, f32), v(BLK, f32), v((CX + 1, CY + 8, NZ), i32),
            face(4, f32), face(2, i32), face(3, f32), face(2, i32), face(4, f32), face(2, i32), face(3, f32), face(2, i32),
            v((3, CX + 1, CY + 8, NZ), f32), v((CX + 1, CY + 8, NZ), f32), v(BLK, f32), v((3,) + BLK, f32),
            v((3, CX, CY + 8, NZ), f32), v((CX + 1, CY, NZ), f32), v((CX, CY + 8, NZ), f32), v(BLK, f32),
            v((2, 5, 32, NZ), f32), v((ROWS, NZ), f32), face(4, f32), face(4, i32), face(4, i32),
            v((4, PERF), i32), v((4, PERF), f32), pltpu.SMEM((4,), f32),
            dma((11,)), dma((8,)), dma((22,)), dma((22,)), dma((NGX,)), dma((NGX,)), dma((NGY,)), dma((NGY,)),
        ],
        compiler_params=pltpu.CompilerParams(collective_id=0, has_side_effects=True, vmem_limit_bytes=BIG),
        name="exchange",
    )(p, ws, gs, act, tx, ty, tz, agg, cells, windex, hole)


def local_kernel(
    p_h, ws_h, gs_h, old_h, pv_h, act_h, agg_h, mob_h, net_h, cx_h, cy_h, cz_h, nb_h, wells_h, sums_h,
    res_o, t_o, dinv_o, sums_o, faces_o, parts_o,
    p, ws, gs, act, agg, old, pv, net, cx, cy, cz, nb4,
    mob, w0, w1, trows, loc, cols, loc_s, s, rem, leak, dinv, res, t, acc, s4, wells, sums, parts_v,
    sem, out_sem, one_sem,
):
    place_x, place_y = lax.axis_index("gx"), lax.axis_index("gy")
    copies = []

    def fetch(src, dst):
        copy = pltpu.make_async_copy(src, dst, sem.at[len(copies)])
        copy.start()
        copies.append(copy)

    fetch(wells_h, wells)
    fetch(mob_h, mob)
    fetch(p_h, p)
    early = len(copies)
    for src, dst in (
        (ws_h, ws), (gs_h, gs), (act_h, act), (pv_h, pv), (old_h, old), (net_h, net), (cx_h, cx), (cy_h, cy), (cz_h, cz),
        (agg_h, agg), (nb_h, nb4), (sums_h, sums),
    ):
        fetch(src, dst)

    copies[0].wait()
    lane = iota((NDEV, NZ), 1)
    table = wells[0]
    cell = table.astype(i32)
    cell_x, cell_y, layer = cell >> 16, (cell >> 7) & 511, cell & 127
    slot = lane & 31
    here = (slot < PERF) & (cell >= 0) & ((cell_x >> 5) == place_x) & ((cell_y >> 5) == place_y)
    local = ((((cell_x & 31) << 5) + (cell_y & 31)) << 7) + layer
    local = jnp.where(here, local, -1)
    flag = jnp.where(here, 1.0, 0.0).astype(jnp.bfloat16)
    at_in, at_out = iota((NZ, NZ), 0), iota((NZ, NZ), 1)
    pick = ((at_in // 32 == at_out // 32) & (at_out % 32 == 16)) | (at_out == 17)
    counts = jnp.dot(flag, jnp.where(pick, 1.0, 0.0).astype(jnp.bfloat16), preferred_element_type=f32).astype(i32)
    first_layer = pltpu.roll(layer, 18, 1)
    cols[...] = jnp.where(here, local >> 7, -1)
    loc[...] = jnp.where(slot < PERF, local, jnp.where(slot == 18, first_layer, counts))
    to_scalar = pltpu.make_async_copy(loc, loc_s, one_sem)
    to_scalar.start()

    w0[...] = jnp.zeros_like(w0)
    w1[...] = jnp.zeros_like(w1)
    trows[...] = jnp.zeros_like(trows)
    for copy in copies[1:early]:
        copy.wait()
    to_scalar.wait()

    row_lane = iota((1, NZ), 1)

    def one_row(r, _):
        @pl.when(loc_s[r, 17] > 0)
        def _():
            for j in range(4):

                @pl.when(loc_s[r, 32 * j + 16] > 0)
                def _():
                    top = loc_s[r, 32 * j + 18]
                    shift = lax.rem(top - (32 * j + PERF) + 2 * NZ, NZ)
                    index_z = pltpu.roll(wells[0, pl.ds(r, 1), :], shift, 1)
                    hole_z = pltpu.roll(wells[1, pl.ds(r, 1), :], shift, 1)
                    column_z = pltpu.roll(cols[pl.ds(r, 1), :], lax.rem(top - 32 * j + NZ, NZ), 1)
                    column_z = jnp.where((row_lane >= top) & (row_lane < top + PERF), column_z, -1)
                    drive_z = index_z * hole_z
                    mob_z = jnp.zeros((1, NZ), f32)
                    press_z = jnp.zeros((1, NZ), f32)
                    stores = []
                    for k in range(PERF):
                        q = jnp.maximum(loc_s[r, 32 * j + k], 0) >> 7
                        qx, qy = q >> 5, pl.ds(q & 31, 1)
                        hit = column_z == q
                        stores.append((
                            qx, qy, w0[qx, qy, :] + jnp.where(hit, index_z, 0.0), w1[qx, qy, :] + jnp.where(hit, drive_z, 0.0)
                        ))
                        mob_z = jnp.where(hit, mob[qx, qy, :], mob_z)
                        press_z = jnp.where(hit, p[qx, qy, :], press_z)
                    for qx, qy, sum0, sum1 in stores:
                        w0[qx, qy, :] = sum0
                        w1[qx, qy, :] = sum1
                    well = ((r & (NGX - 1)) * NGY + (r >> 3)) * 4 + j
                    trows[pl.ds(well, 1), :] = index_z * mob_z * (hole_z - press_z)

        return 0

    loop(0, NDEV, one_row, 0, 4)
    total = lax.dot_general(
        jnp.ones((8, NZ), f32), trows[...], (((1,), (1,)), ((), ())), precision=precise, preferred_element_type=f32
    )
    sub = iota((8, NZ), 0)
    parts = jnp.zeros((8, NZ), f32)
    for k in range(NGX):
        piece = total[:, NZ * (k // 2) : NZ * (k // 2) + NZ]
        if k % 2:
            piece = pltpu.roll(piece, 64, 1)
        parts = jnp.where(sub == k, piece, parts)
    parts_v[...] = parts

    for copy in copies[early:]:
        copy.wait()

    def residuals(x, _):
        for c in range(4):
            at = pl.ds(8 * c, 8)
            z = cz[x, at, :]
            diag = (cx[x + 1, at, :] + cx[x, at, :]) + (cy[x, pl.ds(8 * c + 1, 8), :] + cy[x, at, :]) + (z + lane_prev(z))
            pp, m = p[x, at, :], act[x, at, :].astype(f32)
            sw, sg = ws[x, at, :], gs[x, at, :]
            so = 1.0 - sw - sg
            vol = pv[x, at, :]
            wa, wb = w0[x, at, :], w1[x, at, :]
            pull = m * (wb - pp * wa)
            rhs = None
            for k, sat in enumerate((sw, so, sg)):
                held = (1.0 + compress[k] * (pp - 1.0)) * sat
                r = m * (vol * (held - old[k, x, at, :]) + net[k, x, at, :]) - pull * (held * sat * (1.0 / viscosity[k]))
                res[k, x, at, :] = r
                rhs = r if rhs is None else rhs + r
            rhs = -rhs
            store = vol * (compress[0] * sw + compress[1] * so + compress[2] * sg)
            lk = m * store + wa * mob[x, at, :] + dead_leak * (1.0 - m)
            leak[x, at, :] = lk
            diag = diag + lk
            di = relax / diag
            dinv[x, at, :] = di
            sm = rhs * di
            s[x + 1, pl.ds(8 * c + 1, 8), :] = sm
            rem[x, at, :] = rhs - diag * sm
        one = pl.ds(x, 1)
        s4[2, one, :] = s[x + 1, pl.ds(1, 1), :]
        s4[3, one, :] = s[x + 1, pl.ds(CY, 1), :]
        s[x + 1, pl.ds(0, 1), :] = jnp.zeros((1, NZ), f32)
        s[x + 1, pl.ds(CY + 1, 1), :] = jnp.zeros((1, NZ), f32)
        return 0

    loop(0, CX, residuals, 0, 4)
    s4[0] = s[1, pl.ds(1, CY), :]
    s4[1] = s[CX, pl.ds(1, CY), :]
    s[0] = jnp.zeros_like(s[0])
    s[CX + 1] = jnp.zeros_like(s[0])
    outs = []

    def give(src, dst):
        copy = pltpu.make_async_copy(src, dst, out_sem.at[len(outs)])
        copy.start()
        outs.append(copy)

    give(res, res_o)
    give(dinv, dinv_o)
    give(s4, faces_o)
    give(parts_v, parts_o)

    zero = jnp.zeros((8, NZ), f32)

    def remainders(x, carry):
        lk_sum, re_sum = [list(v) for v in carry]
        for c in range(4):
            at = pl.ds(8 * c, 8)
            up = pl.ds(8 * c + 1, 8)
            here = s[x + 1, up, :]
            z = cz[x, at, :]
            near = cx[x + 1, at, :] * s[x + 2, up, :] + cx[x, at, :] * s[x, up, :]
            near = near + (cy[x, up, :] * s[x + 1, pl.ds(8 * c + 2, 8), :] + cy[x, at, :] * s[x + 1, at, :])
            near = near + (z * lane_next(here) + lane_prev(z * here))
            re = rem[x, at, :] + near
            t[x, at, :] = here + dinv[x, at, :] * re
            lk = leak[x, at, :]
            a = agg[x, at, :]
            for g in range(GROUPS):
                hit = a == g
                re_sum[g] = re_sum[g] + jnp.where(hit, re, 0.0)
                lk_sum[g] = lk_sum[g] + jnp.where(hit, lk, 0.0)
        return tuple(lk_sum), tuple(re_sum)

    lk_sum, re_sum = loop(0, CX, remainders, ((zero,) * GROUPS, (zero,) * GROUPS), 4)
    give(t, t_o)
    rows = [line(v) for v in re_sum]
    acc[...] = jnp.zeros_like(acc)
    for n in range(2):
        coef = (cx[0], cx[CX])[n]
        es = coef * s4[n]
        rows += [line(jnp.where(nb4[n] == g, es, 0.0)) for g in range(GROUPS)]
    e4 = trows
    for x in range(CX):
        e4[pl.ds(x, 1), :] = cy[x, pl.ds(0, 1), :]
        e4[pl.ds(CX + x, 1), :] = cy[x, pl.ds(CY, 1), :]
    for n in range(2):
        es = e4[pl.ds(CX * n, CX), :] * s4[2 + n]
        rows += [line(jnp.where(nb4[2 + n] == g, es, 0.0)) for g in range(GROUPS)]
    rows += [line(v) for v in lk_sum]
    first = RHS_AT - 2 * NZ
    for n in range(6):
        acc[pl.ds(first + 8 * n, 8), :] = jnp.concatenate(rows[8 * n : 8 * n + 8], axis=0)
    sums[2] = sums[2] + jnp.sum(acc[...].T, axis=0, keepdims=True)
    give(sums, sums_o)
    for copy in outs:
        copy.wait()


def local(p, ws, gs, old, pv, act, agg, mob, net, cx, cy, cz, nb, wells, sums):
    v = pltpu.VMEM
    sds = jax.ShapeDtypeStruct
    dma = pltpu.SemaphoreType.DMA
    return pl.pallas_call(
        local_kernel,
        out_shape=[
            sds((3,) + BLK, f32), sds(BLK, f32), sds(BLK, f32), sds((3, 1, NZ), f32), sds((4, 32, NZ), f32), sds((8, NZ), f32)
        ],
        in_specs=[ANY] * 15,
        out_specs=[ANY] * 6,
        scratch_shapes=[
            v(BLK, f32), v(BLK, f32), v(BLK, f32), v(BLK, i32), v(BLK, i32), v((3,) + BLK, f32), v(BLK, f32),
            v((3,) + BLK, f32), v((CX + 1, CY, NZ), f32), v((CX, CY + 8, NZ), f32), v(BLK, f32), v((4, 32, NZ), i32),
            v(BLK, f32), v(BLK, f32), v(BLK, f32), v((4 * NDEV, NZ), f32), v((NDEV, NZ), i32), v((NDEV, NZ), i32), pltpu.SMEM((NDEV, NZ), i32),
            v((CX + 2, CY + 8, NZ), f32), v(BLK, f32), v(BLK, f32), v(BLK, f32), v((3,) + BLK, f32), v(BLK, f32),
            v((NZ, NZ), f32), v((4, 32, NZ), f32), v((2, NDEV, NZ), f32), v((3, 1, NZ), f32), v((8, NZ), f32),
            dma((16,)), dma((8,)), dma,
        ],
        compiler_params=pltpu.CompilerParams(vmem_limit_bytes=BIG),
        name="local",
    )(p, ws, gs, old, pv, act, agg, mob, net, cx, cy, cz, nb, wells, sums)


def coarse_kernel(
    sums_h, parts_h, faces, t_h, dinv_h, cx_h, cy_h, cz_h, agg_h, nb_h, target,
    update_o, well_o,
    gather, mat, slots, send_rows, rows_x, rows_y, tall, dinv, cx, cy, cz, agg, far, pc, sums, parts, nb4, update,
    sem, leave_sem, send_x, recv_x, send_y, recv_y, psend_x, precv_x, psend_y, precv_y, fsend, frecv,
):
    place_x, place_y = lax.axis_index("gx"), lax.axis_index("gy")
    me = place_y * NGX + place_x
    barrier = pltpu.get_barrier_semaphore()
    greet(barrier)
    loads = []
    body = (slice(None), pl.ds(0, CY), slice(None))
    for src, dst in ((sums_h, sums), (parts_h, parts), (nb_h, nb4), (t_h, tall), (dinv_h, dinv), (cx_h, cx), (cy_h, cy), (cz_h, cz), (agg_h, agg)):
        copy = pltpu.make_async_copy(src, dst, sem.at[len(loads)])
        copy.start()
        loads.append(copy)
    for copy in loads[:2]:
        copy.wait()
    for n in range(3):
        gather[n, pl.ds(me, 1), :] = sums[n]
    rows_x[pl.ds(place_x, 1), :] = parts[pl.ds(place_x, 1), :]
    pl.semaphore_wait(barrier, NGX - 1 + NGY - 1)

    sends = []
    own = gather.at[:, pl.ds(me, 1), :]
    for k in range(1, NGX):
        peer = lax.rem(place_x + k, NGX)
        sends.append(remote(own, own, send_x.at[k], recv_x.at[k], peer, place_y))
    for k in range(1, NGX):
        peer = lax.rem(place_x + k, NGX)
        sends.append(
            remote(parts.at[pl.ds(peer, 1), :], rows_x.at[pl.ds(place_x, 1), :], psend_x.at[k], precv_x.at[k], peer, place_y)
        )
    halo = [
        remote(faces.at[1], far.at[0], fsend.at[0], frecv.at[0], lax.rem(place_x + 1, NGX), place_y),
        remote(faces.at[0], far.at[1], fsend.at[1], frecv.at[1], lax.rem(place_x + NGX - 1, NGX), place_y),
        remote(faces.at[3], far.at[2], fsend.at[2], frecv.at[2], place_x, lax.rem(place_y + 1, NGY)),
        remote(faces.at[2], far.at[3], fsend.at[3], frecv.at[3], place_x, lax.rem(place_y + NGY - 1, NGY)),
    ]
    for copy in sends + halo:
        copy.start()
    for k in range(1, NGX):
        source = place_y * NGX + lax.rem(place_x + NGX - k, NGX)
        there = gather.at[:, pl.ds(source, 1), :]
        remote(there, there, send_x.at[k], recv_x.at[k], place_x, place_y).wait_recv()
    block = gather.at[:, pl.ds(place_y * NGX, NGX), :]
    for k in range(1, NGY):
        copy = remote(block, block, send_y.at[k], recv_y.at[k], place_x, lax.rem(place_y + k, NGY))
        copy.start()
        sends.append(copy)
    for k in range(1, NGX):
        source = lax.rem(place_x + NGX - k, NGX)
        there = rows_x.at[pl.ds(source, 1), :]
        remote(there, there, psend_x.at[k], precv_x.at[k], place_x, place_y).wait_recv()
    line = jnp.sum(rows_x[...], axis=0, keepdims=True)
    for k in range(NGY):
        send_rows[k : k + 1, :] = line if k == 0 else pltpu.roll(line, NZ - 4 * k, 1)
    rows_y[pl.ds(place_y, 1), :] = send_rows[pl.ds(place_y, 1), :]
    for k in range(1, NGY):
        peer = lax.rem(place_y + k, NGY)
        copy = remote(
            send_rows.at[pl.ds(peer, 1), :], rows_y.at[pl.ds(place_y, 1), :], psend_y.at[k], precv_y.at[k], place_x, peer
        )
        copy.start()
        sends.append(copy)
    for k in range(1, NGY):
        source = lax.rem(place_y + NGY - k, NGY)
        there = gather.at[:, pl.ds(source * NGX, NGX), :]
        remote(there, there, send_y.at[k], recv_y.at[k], place_x, place_y).wait_recv()

    for n in range(3):
        mat[pl.ds(NZ * n, NZ), :] = gather[n].T
    sub = iota((8, NZ), 0)

    def rows(n):
        return mat[pl.ds(8 * n, 8), :]

    moves = (0, 1, NZ - 1, NGX, NZ - NGX)
    total = jnp.zeros((8, NZ), f32)
    for n in range(5 * GROUPS):
        total = total + rows(n)
    total = total + rows(LEAK_AT // 8)
    for h in range(GROUPS):
        block = rows(h)
        slots[pl.ds(8 * h, 8), :] = jnp.where(sub == h, total, -block)
    for d in range(1, 5):
        for h in range(GROUPS):
            v = -rows(d * GROUPS + h)
            slots[pl.ds((d * GROUPS + h) * 8, 8), :] = pltpu.roll(v, (NZ - moves[d]) % NZ, 1)
    rhs = rows(RHS_AT // 8)
    for d in range(1, 5):
        away = (0, 2, 1, 4, 3)[d]
        rhs = rhs + pltpu.roll(rows(OUT_AT // 8 + away - 1), moves[d], 1)

    def dot(a, b):
        return jnp.sum(jnp.sum(a * b, axis=0, keepdims=True), axis=1, keepdims=True)

    def tree(values):
        while len(values) > 1:
            values = [a + b for a, b in zip(values[::2], values[1::2])] + values[len(values) // 2 * 2 :]
        return values[0]

    def image(v):
        spread = [jnp.broadcast_to(v[h : h + 1, :], (8, NZ)) for h in range(GROUPS)]
        sides = [tree([slots[pl.ds((d * GROUPS + h) * 8, 8), :] * spread[h] for h in range(GROUPS)]) for d in range(5)]
        return tree([pltpu.roll(sides[d], moves[d], 1) for d in range(1, 5)]) + sides[0]

    w = image(rhs)
    norm = dot(rhs, rhs)
    alpha = norm / dot(w, rhs)

    def one_step(_, carry):
        x, r, q, aq, norm, alpha = carry
        x = x + alpha * q
        r = r - alpha * aq
        new = dot(r, r)
        w = image(r)
        curve = dot(w, r)
        beta = new / norm
        alpha = new / (curve - beta * (new / alpha))
        return x, r, r + beta * q, w + beta * aq, new, alpha

    start = (jnp.zeros((8, NZ), f32), rhs, rhs, w, norm, alpha)
    x, _, q, _, _, alpha = loop(0, CITERS - 1, one_step, start, 1)
    coarse = x + alpha * q
    mine = iota((8, NZ), 1) == me
    values = []
    for d in range(5):
        v = coarse if d == 0 else pltpu.roll(coarse, moves[d], 1)
        values.append(jnp.sum(jnp.where(mine, v, 0.0), axis=1, keepdims=True))

    def look_up(ids, d):
        v = jnp.broadcast_to(values[d][0:1, :], ids.shape)
        for g in range(1, GROUPS):
            v = jnp.where(ids == g, values[d][g : g + 1, :], v)
        return v

    for copy in halo:
        copy.wait_recv()
    for copy in loads[2:]:
        copy.wait()
    pc[0, pl.ds(8, CY), :] = far[0] + look_up(nb4[0], 1)
    pc[CX + 1, pl.ds(8, CY), :] = far[1] + look_up(nb4[1], 2)
    far[2] = far[2] + look_up(nb4[2], 3)
    far[3] = far[3] + look_up(nb4[3], 4)

    def fill(x, _):
        pc[x + 1, pl.ds(8, CY), :] = look_up(agg[x], 0)
        pc[x + 1, pl.ds(7, 1), :] = far[2, pl.ds(x, 1), :]
        pc[x + 1, pl.ds(CY + 8, 1), :] = far[3, pl.ds(x, 1), :]
        return 0

    loop(0, CX, fill, 0, 8)

    def finish(x, _):
        for c in range(4):
            at = pl.ds(8 * c, 8)
            mid = pl.ds(8 * c + 8, 8)
            here = pc[x + 1, mid, :]
            z = cz[x, at, :]
            near = cx[x + 1, at, :] * pc[x + 2, mid, :] + cx[x, at, :] * pc[x, mid, :]
            near = near + (
                cy[x, pl.ds(8 * c + 1, 8), :] * pc[x + 1, pl.ds(8 * c + 9, 8), :]
                + cy[x, at, :] * pc[x + 1, pl.ds(8 * c + 7, 8), :]
            )
            near = near + (z * lane_next(here) + lane_prev(z * here))
            update[x, at, :] = tall[x, at, :] + (1.0 - relax) * here + dinv[x, at, :] * near
        return 0

    leaves = []
    for n in range(4):
        loop(8 * n, 8 * n + 8, finish, 0, 8)
        at = pl.ds(8 * n, 8)
        copy = pltpu.make_async_copy(update.at[at], update_o.at[at], leave_sem.at[n])
        copy.start()
        leaves.append(copy)
    for k in range(1, NGY):
        source = lax.rem(place_y + NGY - k, NGY)
        there = rows_y.at[pl.ds(source, 1), :]
        remote(there, there, psend_y.at[k], precv_y.at[k], place_x, place_y).wait_recv()
    rates = jnp.sum(rows_y[...], axis=0, keepdims=True)
    for j in range(4):
        well_o[j] = rates[0, j] - target[j]
    for copy in sends + halo:
        copy.wait_send()
    for copy in leaves:
        copy.wait()


def coarse_part(sums, parts, faces, t, dinv, cx, cy, cz, agg, nb4, target):
    v = pltpu.VMEM
    sds = jax.ShapeDtypeStruct
    dma = pltpu.SemaphoreType.DMA
    return pl.pallas_call(
        coarse_kernel,
        out_shape=[sds(BLK, f32), sds((4,), f32)],
        in_specs=[ANY] * 10 + [SMEM],
        out_specs=[ANY, SMEM],
        scratch_shapes=[
            v((3, NDEV, NZ), f32), v((ROWS, NZ), f32), v((5 * 64, NZ), f32), v((NGY, NZ), f32), v((NGX, NZ), f32), v((NGY, NZ), f32),
            v(BLK, f32), v(BLK, f32), v((CX + 1, CY, NZ), f32), v((CX, CY + 8, NZ), f32), v(BLK, f32), v(BLK, i32),
            v((4, 32, NZ), f32), v((CX + 2, CY + 16, NZ), f32),
            v((3, 1, NZ), f32), v((8, NZ), f32), v((4, 32, NZ), i32), v(BLK, f32),
            dma((9,)), dma((4,)), dma((NGX,)), dma((NGX,)), dma((NGY,)), dma((NGY,)),
            dma((NGX,)), dma((NGX,)), dma((NGY,)), dma((NGY,)), dma((4,)), dma((4,)),
        ],
        compiler_params=pltpu.CompilerParams(
            collective_id=1, has_side_effects=True, vmem_limit_bytes=BIG
        ),
        name="coarse",
    )(sums, parts, faces, t, dinv, cx, cy, cz, agg, nb4, target)


def last_kernel(update_h, well_h, update_o, well_o, held, sem_in, sem_out, well_sem):
    part = CX // 4
    moves = []
    well = pltpu.make_async_copy(well_h, well_o, well_sem)
    well.start()
    for n in range(4):
        at = pl.ds(part * n, part)
        copy = pltpu.make_async_copy(update_h.at[at], held.at[at], sem_in.at[n])
        copy.start()
        moves.append((copy, pltpu.make_async_copy(held.at[at], update_o.at[at], sem_out.at[n])))
    for arrive, leave in moves:
        arrive.wait()
        leave.start()
    for _, leave in moves:
        leave.wait()
    well.wait()


def last_part(update, well):
    sds = jax.ShapeDtypeStruct
    return pl.pallas_call(
        last_kernel,
        out_shape=[sds(BLK, f32), sds((4,), f32)],
        in_specs=[ANY, ANY],
        out_specs=[ANY, ANY],
        scratch_shapes=[pltpu.VMEM(BLK, f32), pltpu.SemaphoreType.DMA((4,)), pltpu.SemaphoreType.DMA((4,)), pltpu.SemaphoreType.DMA],
        compiler_params=pltpu.CompilerParams(vmem_limit_bytes=BIG),
        name="last",
    )(update, well)


def per_device(
    pressure, water_sat, gas_sat, old_content, pore_volume, trans_x, trans_y, trans_z, active, aggregate,
    well_cells, well_index, bottom_hole, well_target,
):
    net, cx, cy, cz, mob, sums, nb, wells = exchange(
        pressure, water_sat, gas_sat, active, trans_x, trans_y, trans_z, aggregate, well_cells, well_index, bottom_hole
    )
    residual, t, dinv, sums, faces, parts = local(
        pressure, water_sat, gas_sat, old_content, pore_volume, active, aggregate, mob, net, cx, cy, cz, nb, wells, sums
    )
    update, well = coarse_part(sums, parts, faces, t, dinv, cx, cy, cz, aggregate, nb, well_target)
    update, well_residual = last_part(update, well)
    return residual, update, well_residual


def solution(mesh):
    cells = P("gx", "gy", None)
    three = P(None, "gx", "gy", None)
    well, one = P(("gx", "gy"), None), P(("gx", "gy"))
    return jax.shard_map(
        per_device,
        mesh=mesh,
        in_specs=(cells, cells, cells, three) + (cells,) * 6 + (well, well, one, one),
        out_specs=(three, cells, one),
        check_vma=False,
    )
```
